32 devices in a mesh: dp: 8 (over z, x), expert: 4 (over y, core).
Axes of the slice: x: 2, y: 2, z: 4, core: 2. Of those that a mesh axis runs over, the one named last changes fastest.
Arguments:
- tokens: bfloat16 [31520, 512], P(('dp', 'expert')), may hold values from -6 to 6
- cotangent: bfloat16 [31520, 512], P(('dp', 'expert')), may hold values from -6 to 6
- routes: int32 [31520, 2], P(('dp', 'expert')), may hold values from 0 to 15, all different within a row; in each aligned block of 985 rows (0 to 984, 985 to 1969, ...) at most 246 rows name the same one
- combine: float32 [31520, 2], P(('dp', 'expert')), may hold values from 0.25 to 0.75
- attn_master: float32 [512, 2048], P('dp')
- attn_first: float32 [512, 2048], P('dp')
- attn_second: float32 [512, 2048], P('dp')
- vector_master: float32 [5, 512], P(None, 'dp')
- vector_first: float32 [5, 512], P(None, 'dp')
- vector_second: float32 [5, 512], P(None, 'dp')
- expert_master: float32 [512, 2, 16, 2048], P('dp', None, 'expert'), may hold values from -0.25 to 0.25
- expert_first: float32 [512, 2, 16, 2048], P('dp', None, 'expert')
- expert_second: float32 [512, 2, 16, 2048], P('dp', None, 'expert')
Outputs:
- mixed: bfloat16 [31520, 512], P(('dp', 'expert'))
- grad_tokens: bfloat16 [31520, 512], P(('dp', 'expert'))
- attn_master_new: float32 [512, 2048], P('dp')
- attn_first_new: float32 [512, 2048], P('dp')
- attn_second_new: float32 [512, 2048], P('dp')
- vector_master_new: float32 [5, 512], P(None, 'dp')
- vector_first_new: float32 [5, 512], P(None, 'dp')
- vector_second_new: float32 [5, 512], P(None, 'dp')
- expert_master_new: float32 [512, 2, 16, 2048], P('dp', None, 'expert')
- expert_first_new: float32 [512, 2, 16, 2048], P('dp', None, 'expert')
- expert_second_new: float32 [512, 2, 16, 2048], P('dp', None, 'expert')
The draws below stay inside these ranges and needn't reach their ends.
Inputs may be any that keep to these rules, and one draw needn't show every extreme that they name: `routes`: within the 985 rows of one device (aligned blocks) no expert is named in more than 246 slots, some expert in exactly 246; a row names 2 different experts.
All inputs are finite; a program needn't handle non-finite values.
Results may differ from the reference program's by a relative error of at most 0.015.
The reference program's roundings to bfloat16 on the way count: a program that leaves them out, or rounds other values in their place, can miss the bound.
Values may be sent and summed in bfloat16 or wider, within the bound.
A program may use at most 256 MiB of HBM per device.

```python
import math
import jax
import jax.numpy as jnp
import numpy as np
from jax import lax

D = 512
HEADS = 8
HEAD_DIM = 64
FF = 2048
SEQ = 197
TOP = 2
STEP = 10
EXPERTS = 16
TOK_DEV = 985
TOKENS = 31520
CAP = 246


def attn_size():
    column = jnp.arange(4 * D)
    return (jnp.where(column < 3 * D, 1.5, 0.5) * math.sqrt(TOKENS))[None, :]


def vector_size():
    return jnp.array([3.9, 3.9, 0.85, 0.85, 1.4], jnp.float32)[:, None] * math.sqrt(TOKENS)


def expert_size():
    return 0.3 * math.sqrt(TOKENS * TOP / EXPERTS)


def first_moment(key, extent, size_scale):
    return 0.111 * size_scale * jax.random.truncated_normal(key, -3.0, 3.0, extent, jnp.float32)


def second_moment(key, extent, size_scale):
    factor = jnp.exp(jax.random.uniform(key, extent, jnp.float32, 0.0, math.log(4.0)))
    return 0.001 * size_scale * size_scale * factor


def draw_attn_master(key, part):
    key = jax.random.fold_in(key, 11)
    base_draw = jax.random.truncated_normal(key, -4.0, 4.0, (D, 4 * D), jnp.float32)
    column = jnp.arange(4 * D)
    column_scale = jnp.where(column < 3 * D, 1.5, 4.0) / math.sqrt(D)
    return base_draw * column_scale[None, :]


def draw_attn_first(key, part):
    key = jax.random.fold_in(key, 12)
    return first_moment(key, (D, 4 * D), attn_size())


def draw_attn_second(key, part):
    key = jax.random.fold_in(key, 13)
    return second_moment(key, (D, 4 * D), attn_size())


def draw_vector_master(key, part):
    key = jax.random.fold_in(key, 14)
    gain_rows = jax.random.uniform(jax.random.fold_in(key, 1), (5, D), jnp.float32, 0.6, 1.4)
    shifts = 0.1 * jax.random.truncated_normal(jax.random.fold_in(key, 2), -4.0, 4.0, (5, D), jnp.float32)
    row_index = jnp.arange(5)[:, None]
    return jnp.where((row_index == 0) | (row_index == 2), gain_rows, shifts)


def draw_vector_first(key, part):
    key = jax.random.fold_in(key, 15)
    return first_moment(key, (5, D), vector_size())


def draw_vector_second(key, part):
    key = jax.random.fold_in(key, 16)
    return second_moment(key, (5, D), vector_size())


def draw_expert_first(key, part):
    key = jax.random.fold_in(key, 17)
    return first_moment(key, (D, 2, EXPERTS, FF), expert_size())


def draw_expert_second(key, part):
    key = jax.random.fold_in(key, 18)
    return second_moment(key, (D, 2, EXPERTS, FF), expert_size())


def block_levels(stream_key, shape, cuts, low, largest):
    factor_of, own = 1.0, jax.random.fold_in(stream_key, 6)
    for dim, shards_of in cuts:
        steps = jnp.exp(jax.random.uniform(jax.random.fold_in(own, dim), (shards_of,), jnp.float32, low / len(cuts), largest / len(cuts)))
        factor_of = factor_of * jnp.repeat(steps, shape[dim] // shards_of).reshape([-1 if axis == dim else 1 for axis in range(len(shape))])
    return factor_of


def shared_out(rng, own, number, rows, count, top, bound, slope):
    sequence = jax.random.permutation(rng, count)
    crowded, ordinary = load_shares(count, rows * top, bound, slope, True), load_shares(count, rows * top, bound, slope, False)
    places = jnp.arange(count)

    def named(lengths, rotation):
        used = int((lengths > 0).sum())
        fixed = max(1, used // 4)
        passed = fixed + (places - fixed + rotation * (used - fixed)) % max(1, count - fixed)
        return jnp.zeros((count,), jnp.int32).at[sequence[jnp.where(places < fixed, places, passed)]].set(jnp.asarray(lengths, jnp.int32))

    lengths = jnp.where(number % 4 == 0, named(crowded, number // 4), named(ordinary, number - number // 4 - 1))
    mixed = jax.random.permutation(jax.random.fold_in(own, 3), count)
    donor, sink = mixed[0:count // 2 * 2:2], mixed[1:count // 2 * 2:2]
    room = jnp.minimum(lengths[donor] - 1, bound - lengths[sink]) // 2
    room = jnp.where((donor == sequence[0]) | (sink == sequence[0]) | (lengths[sink] == 0), 0, jnp.maximum(room, 0))
    passed = jax.random.randint(jax.random.fold_in(own, 4), (count // 2,), 0, 1 << 20) % (room + 1)
    lengths = lengths.at[donor].add(-passed).at[sink].add(passed)
    members = jnp.searchsorted(jnp.cumsum(lengths), jnp.arange(rows * top), side="right").astype(jnp.int32)
    table = members.reshape(top, rows).T
    table = table[jax.random.permutation(jax.random.fold_in(own, 1), rows)]
    rotation = jax.random.randint(jax.random.fold_in(own, 2), (rows, 1), 0, top)
    return jnp.take_along_axis(table, (jnp.arange(top)[None, :] + rotation) % top, axis=1)


def load_shares(number_of, total, reach, lean, full):
    loads = [(1 << 20) // math.isqrt(rank ** lean) + 1 for rank in range(1, number_of + 1)]
    largest = reach if full else min(reach, max(-(-total // number_of), total * loads[0] // sum(loads)))
    least = 1 if total - largest >= number_of - 1 else 0
    counts, spare = [largest] + [least] * (number_of - 1), total - largest - least * (number_of - 1)
    while spare > 0:
        candidates = [i for i in range(1, number_of) if counts[i] < largest] or [i for i in range(1, number_of) if counts[i] < reach]
        pool, budget = sum([loads[i] for i in candidates]), spare
        for i in candidates:
            extra = min(reach - counts[i], max(1, budget * loads[i] // pool), spare)
            counts[i] = counts[i] + extra
            spare = spare - extra
    return np.array(counts)


def centred(stream_key, shape, deviation, limit, pieces=(), kind=jnp.bfloat16):
    factor_of = block_levels(stream_key, shape, pieces, -0.22, 0.18) if pieces else 1.0
    drawn = jax.random.normal(stream_key, shape, jnp.float32) * deviation * factor_of
    return jnp.minimum(jnp.maximum(drawn, -limit), limit).astype(kind)


def setup_inputs(seed: int = 0) -> dict:
    key_list = jax.random.split(jax.random.key(seed), 14)
    tokens = centred(key_list[0], (TOKENS, D), 1.0, 6.0, ((0, 32),))
    cotangent = centred(key_list[1], (TOKENS, D), 1.0, 6.0, ((0, 32),))
    routes_keys = jax.random.split(jax.random.fold_in(key_list[2], 1), TOKENS // TOK_DEV)
    routes_turns = jax.random.permutation(jax.random.fold_in(key_list[2], 3), TOKENS // TOK_DEV)
    routes = jax.vmap(lambda own, number: shared_out(jax.random.fold_in(key_list[2], 2), own, number, TOK_DEV, EXPERTS, TOP, CAP, 1))(routes_keys, routes_turns).reshape((TOKENS, TOP))
    combine = jnp.clip(0.25 + 0.5 * jax.random.uniform(key_list[3], (TOKENS, TOP), jnp.float32) ** block_levels(key_list[3], (TOKENS, TOP), ((0, 32),), -0.2, 0.2), 0.25, 0.75)
    attn_master = draw_attn_master(jax.random.fold_in(key_list[13], 71), 0)
    attn_first = draw_attn_first(jax.random.fold_in(key_list[13], 71), 0)
    attn_second = draw_attn_second(jax.random.fold_in(key_list[13], 71), 0)
    vector_master = draw_vector_master(jax.random.fold_in(key_list[13], 71), 0)
    vector_first = draw_vector_first(jax.random.fold_in(key_list[13], 71), 0)
    vector_second = draw_vector_second(jax.random.fold_in(key_list[13], 71), 0)
    expert_master = centred(key_list[10], (D, 2, EXPERTS, FF), D ** -0.5, 0.25, ((0, 8), (2, 4)), jnp.float32)
    expert_first = draw_expert_first(jax.random.fold_in(key_list[13], 71), 0)
    expert_second = draw_expert_second(jax.random.fold_in(key_list[13], 71), 0)
    return {"tokens": tokens, "cotangent": cotangent, "routes": routes, "combine": combine, "attn_master": attn_master, "attn_first": attn_first, "attn_second": attn_second, "vector_master": vector_master, "vector_first": vector_first, "vector_second": vector_second, "expert_master": expert_master, "expert_first": expert_first, "expert_second": expert_second}


LN_EPS = 1e-06
BETA_ONE = 0.9
BETA_TWO = 0.999
ADAM_EPS = 1e-08
HIGH = lax.Precision.HIGHEST

@jax.custom_vjp
def low(v):
    return lax.optimization_barrier(v.astype(jnp.bfloat16)).astype(jnp.float32)

@jax.custom_vjp
def low_back(v):
    return v

def low_keep(v):
    return (low(v), None)

def low_pass(kept, grad):
    return (grad,)

def back_keep(v):
    return (v, None)

def back_low(kept, grad):
    return (low(grad),)
low.defvjp(low_keep, low_pass)
low_back.defvjp(back_keep, back_low)

def layer_norm(values, gain_row, shift_row):
    average = lax.optimization_barrier(jnp.mean(values, axis=-1, keepdims=True))
    centered = values - average
    spread = lax.optimization_barrier(jnp.mean(centered * centered, axis=-1, keepdims=True))
    return centered * lax.rsqrt(spread + LN_EPS) * gain_row + shift_row

def slot_places(routes_blk):
    devices_in = routes_blk.shape[0] // TOK_DEV
    flat_routes = routes_blk.reshape(devices_in, TOK_DEV * TOP)
    onehot = (flat_routes[:, :, None] == jnp.arange(EXPERTS, dtype=jnp.int32)[None, None, :]).astype(jnp.int32)
    before = jnp.cumsum(onehot, axis=1) - onehot
    places = lax.optimization_barrier(jnp.sum(before * onehot, axis=2)) + (jnp.arange(devices_in, dtype=jnp.int32) * CAP)[:, None]
    return places.reshape(devices_in * TOK_DEV, TOP).astype(jnp.int32)

def forward(inputs, attn_weight, vectors, expert_weight, routes_blk, places, combine_blk):
    rows_here = inputs.shape[0]
    images = rows_here // SEQ
    slot_total = rows_here // TOK_DEV * CAP
    normed = low(layer_norm(inputs, vectors[0], vectors[1]))
    packed = low_back(low(jnp.dot(normed, attn_weight[:, :3 * D], precision=HIGH, preferred_element_type=jnp.float32)))
    packed = packed.reshape(images, SEQ, 3, HEADS, HEAD_DIM)
    queries = packed[:, :, 0]
    keys_all = packed[:, :, 1]
    values_all = packed[:, :, 2]
    scores = low_back(jnp.einsum('bqhc,bkhc->bhqk', queries, keys_all, precision=HIGH) * HEAD_DIM ** (-0.5))
    weights_soft = low(jax.nn.softmax(scores, axis=-1))
    attended = jnp.einsum('bhqk,bkhc->bqhc', weights_soft, values_all, precision=HIGH).reshape(rows_here, D)
    attended = low_back(low(attended))
    middle = inputs + low_back(jnp.dot(attended, attn_weight[:, 3 * D:], precision=HIGH, preferred_element_type=jnp.float32)) + vectors[4]
    mixed_in = low(layer_norm(middle, vectors[2], vectors[3]))
    buffer = jnp.zeros((EXPERTS, slot_total, D), jnp.float32)
    for which_slot in range(TOP):
        buffer = buffer.at[routes_blk[:, which_slot], places[:, which_slot]].add(low_back(mixed_in))
    preact = low_back(jnp.einsum('ecd,def->ecf', buffer, expert_weight[:, 0], precision=HIGH))
    hidden = low(jax.nn.gelu(preact, approximate=False))
    expert_out = low_back(low(jnp.einsum('ecf,def->ecd', hidden, expert_weight[:, 1], precision=HIGH)))
    result = middle
    for which_slot in range(TOP):
        picked = expert_out[routes_blk[:, which_slot], places[:, which_slot]]
        result = result + combine_blk[:, which_slot:which_slot + 1] * picked
    return result

def adam_update(master, first, second, gradient, step_rate, decay_rate):
    first = BETA_ONE * first + (1.0 - BETA_ONE) * gradient
    second = BETA_TWO * second + (1.0 - BETA_TWO) * gradient * gradient
    first_hat = first / (1.0 - BETA_ONE ** STEP)
    second_hat = second / (1.0 - BETA_TWO ** STEP)
    master = master - step_rate * (first_hat / (jnp.sqrt(second_hat) + ADAM_EPS) + decay_rate * master)
    return (master, first, second)

def reference(tokens, cotangent, routes, combine, attn_master, attn_first, attn_second, vector_master, vector_first, vector_second, expert_master, expert_first, expert_second):
    attn_weight = low(attn_master)
    vectors = low(vector_master)
    expert_weight = low(expert_master)
    block_rows = 4 * TOK_DEV
    block_count = TOKENS // block_rows

    def one_block(totals, block_index):
        start_row = block_index * block_rows

        def take_rows(array):
            return lax.dynamic_slice_in_dim(array, start_row, block_rows, 0)
        routes_blk = take_rows(routes)
        places = slot_places(routes_blk)
        combine_blk = take_rows(combine)

        def apply_block(inputs, attn_arg, vector_arg, expert_arg):
            return forward(inputs, attn_arg, vector_arg, expert_arg, routes_blk, places, combine_blk)
        result, pullback = jax.vjp(apply_block, take_rows(tokens).astype(jnp.float32), attn_weight, vectors, expert_weight)
        gradients = pullback(take_rows(cotangent).astype(jnp.float32))
        totals = jax.tree.map(jnp.add, totals, tuple(gradients[1:]))
        return (totals, (result.astype(jnp.bfloat16), gradients[0].astype(jnp.bfloat16)))
    zeros_start = (jnp.zeros_like(attn_weight), jnp.zeros_like(vectors), jnp.zeros_like(expert_weight))
    totals, outputs = lax.scan(one_block, zeros_start, jnp.arange(block_count, dtype=jnp.int32))
    mixed = outputs[0].reshape(TOKENS, D)
    grad_tokens = outputs[1].reshape(TOKENS, D)
    attn_new = adam_update(attn_master, attn_first, attn_second, totals[0], 0.03, 0.1)
    vector_new = adam_update(vector_master, vector_first, vector_second, totals[1], 0.2, 0.0)
    expert_new = adam_update(expert_master, expert_first, expert_second, totals[2], 0.02, 0.1)
    return (mixed, grad_tokens, attn_new[0], attn_new[1], attn_new[2], vector_new[0], vector_new[1], vector_new[2], expert_new[0], expert_new[1], expert_new[2])
```

```python
import functools

import jax
import jax.numpy as jnp
from jax import lax
from jax.experimental import pallas as pl
from jax.experimental.pallas import tpu as pltpu
from jax.sharding import PartitionSpec as P

D = 512
HEADS = 8
HEAD_DIM = 64
SEQ = 197
TOP = 2
STEP = 10
PAD = 256
SENT = 208
CORES = 2
COLUMNS = 2

LN_EPS = 1e-06
BETA_ONE = 0.9
BETA_TWO = 0.999
ADAM_EPS = 1e-08
MESH = pl.DeviceIdType.MESH
F32 = jnp.float32
BF16 = jnp.bfloat16
VMEM_LIMIT = 60 * 1024 * 1024


def dot(left, right):
    return jnp.dot(left, right, preferred_element_type=F32)


def contract_rows(left, right):
    return lax.dot_general(
        left, right, (((0,), (0,)), ((), ())), preferred_element_type=F32
    )


def contract_last(left, right):
    return lax.dot_general(
        left, right, (((1,), (1,)), ((), ())), preferred_element_type=F32
    )


def normalize(values):
    centered = values - jnp.mean(values, axis=-1, keepdims=True)
    inverse = lax.rsqrt(jnp.mean(centered * centered, axis=-1, keepdims=True) + LN_EPS)
    return (centered * inverse, inverse)


def norm_back(grad_normed, normed, inverse):
    first_mean = jnp.mean(grad_normed, axis=-1, keepdims=True)
    second_mean = jnp.mean(grad_normed * normed, axis=-1, keepdims=True)
    return inverse * (grad_normed - first_mean - normed * second_mean)


def remote(source, target, send_sem, recv_sem, device):
    return pltpu.make_async_remote_copy(
        src_ref=source,
        dst_ref=target,
        send_sem=send_sem,
        recv_sem=recv_sem,
        device_id=device,
        device_id_type=MESH,
    )


def greet(devices):
    barrier = pltpu.get_barrier_semaphore()
    for device in devices:
        pl.semaphore_signal(barrier, inc=1, device_id=device, device_id_type=MESH)
    pl.semaphore_wait(barrier, len(devices))


def softmax_rows(query, key_rows, half, lane):
    own = jnp.where(lane // HEAD_DIM == half, query, jnp.zeros_like(query))
    scores = contract_last(own, key_rows) * HEAD_DIM ** (-0.5)
    column = lax.broadcasted_iota(jnp.int32, scores.shape, 1)
    scores = jnp.where(column < SEQ, scores, -1e30)
    powers = jnp.exp(scores - jnp.max(scores, axis=-1, keepdims=True))
    return powers * (1.0 / jnp.sum(powers, axis=-1, keepdims=True))


def front_kernel(
    shards, lines, tok, cot, route, comb, attn, vec, expw,
    u_all, g_all, place_out, comb_out, wfull, attnw, vec_out, middle, qkv, att,
    route_all, comb_all, vslots, chosen,
    attn_send, attn_recv, vec_send, vec_recv, pass_sem, table_send, table_recv,
    g_sem, u_send, u_recv, own_sem, up_send, up_recv, down_send, down_recv, x_send, x_recv,
):
    dp, me = lax.axis_index("dp"), lax.axis_index("expert")
    z, x = dp // COLUMNS, dp % COLUMNS
    y, core = me // CORES, me % CORES
    images = tok.shape[0]
    local = expw.shape[0]
    rows = attn.shape[0]
    half = rows // CORES
    mate = (dp, y * CORES + 1 - core)
    over = (dp, (1 - y) * CORES + core)
    corner = (dp, (1 - y) * CORES + 1 - core)
    above = (jnp.minimum(z + 1, lines - 1) * COLUMNS + x, me)
    below = (jnp.maximum(z - 1, 0) * COLUMNS + x, me)
    beside = (z * COLUMNS + 1 - x, me)
    peers = [(lax.rem(dp + k, shards), me) for k in range(1, shards)]
    sources = [lax.rem(dp + shards - k, shards) for k in range(1, shards)]
    greet(peers + [mate, over, corner])
    mine = pl.ds(pl.multiple_of(core * half, half), half)

    for k, peer in enumerate(peers):
        remote(attn.at[mine], attnw.at[dp, mine], attn_send.at[k], attn_recv.at[dp], peer).start()
        remote(vec, vslots.at[dp], vec_send.at[k], vec_recv.at[dp], peer).start()
    tables = []
    for k, partner in enumerate((mate, over, corner)):
        tables.append(remote(route, route_all.at[me], table_send.at[k, 0], table_recv.at[me, 0], partner))
        tables.append(remote(comb, comb_all.at[me], table_send.at[k, 1], table_recv.at[me, 1], partner))
    for copy in tables:
        copy.start()
    g_own = cot.at[:, pl.ds(0, SENT)]
    g_mate = remote(g_own, g_all.at[me, :, pl.ds(0, SENT)], g_sem.at[0], g_sem.at[1], mate)
    g_over = remote(g_own, g_all.at[me, :, pl.ds(0, SENT)], g_sem.at[2], g_sem.at[3], over)
    g_mate.start()
    g_over.start()

    def up(e, hop, source):
        shard = (z - hop) * COLUMNS + x
        return remote(source, wfull.at[e, :, shard], up_send.at[e, hop], up_recv.at[e, hop], above)

    def down(e, hop, source):
        shard = (z + hop) * COLUMNS + x
        return remote(source, wfull.at[e, :, shard], down_send.at[e, hop], down_recv.at[e, hop], below)

    def across(e, place, source):
        shard = place * COLUMNS + x
        return remote(source, wfull.at[e, :, shard], x_send.at[e, place], x_recv.at[e, place], beside)

    def start_own(e):
        @pl.when(z < lines - 1)
        def _():
            up(e, 0, expw.at[e]).start()

        @pl.when(z > 0)
        def _():
            down(e, 0, expw.at[e]).start()

        across(e, z, expw.at[e]).start()

    def hand_on(step):
        e, hop = step // (lines - 1), step % (lines - 1)

        @pl.when(jnp.logical_and(hop == 0, e + 2 < local))
        def _():
            start_own(e + 2)

        from_below = jnp.maximum(z - 1 - hop, 0)
        from_above = jnp.minimum(z + 1 + hop, lines - 1)

        @pl.when(z - 1 - hop >= 0)
        def _():
            held = wfull.at[e, :, from_below * COLUMNS + x]
            remote(held, held, up_send.at[e, hop], up_recv.at[e, hop], above).wait_recv()

            @pl.when(z < lines - 1)
            def _():
                remote(held, held, up_send.at[e, hop + 1], up_recv.at[e, hop + 1], above).start()

            remote(held, held, x_send.at[e, from_below], x_recv.at[e, from_below], beside).start()

        @pl.when(z + 1 + hop <= lines - 1)
        def _():
            held = wfull.at[e, :, from_above * COLUMNS + x]
            remote(held, held, down_send.at[e, hop], down_recv.at[e, hop], below).wait_recv()

            @pl.when(z > 0)
            def _():
                remote(held, held, down_send.at[e, hop + 1], down_recv.at[e, hop + 1], below).start()

            remote(held, held, x_send.at[e, from_above], x_recv.at[e, from_above], beside).start()

    start_own(0)
    start_own(1)
    own_copy = pltpu.make_async_copy(expw, wfull.at[:, :, dp], own_sem)
    own_copy.start()

    attnw[dp, mine] = attn[mine]
    vslots[dp] = vec[...]
    route_all[me] = route[...]
    comb_all[me] = comb[...]
    g_all[me] = cot[...]
    empty = jnp.zeros((images, PAD - SENT, D), BF16)
    for k in range(1, 4):
        other = lax.rem(me + k, 4)
        u_all[other, :, SENT:, :] = empty
        g_all[other, :, SENT:, :] = empty

    for k, (peer, source) in enumerate(zip(peers, sources)):
        remote(attn.at[mine], attnw.at[source, mine], attn_send.at[k], attn_recv.at[source], peer).wait()
        remote(vec, vslots.at[source], vec_send.at[k], vec_recv.at[source], peer).wait()
    halves = attnw.at[:, mine]
    to_mate = remote(halves, halves, pass_sem.at[0], pass_sem.at[1], mate)
    to_mate.start()

    lane = lax.broadcasted_iota(jnp.int32, (128, D), 1)
    entry = lax.broadcasted_iota(jnp.int32, (128, D), 0)
    width = D // shards
    vectors = jnp.zeros((8, D), F32)
    for d in range(shards):
        spread = jnp.where(jnp.logical_and(entry < width, lane == entry + d * width), 1.0, 0.0)
        vectors = vectors + dot(vslots[d].astype(BF16), spread.astype(BF16))
    vec_out[...] = vectors
    gain_one, shift_one = vectors[0:1], vectors[1:2]
    gain_two, shift_two, shift_out = vectors[2:3], vectors[3:4], vectors[4:5]

    others = remote(attnw.at[:, pl.ds(pl.multiple_of((1 - core) * half, half), half)],
                    attnw.at[:, pl.ds(pl.multiple_of((1 - core) * half, half), half)],
                    pass_sem.at[0], pass_sem.at[1], mate)
    others.wait_recv()
    pair_lane = lax.broadcasted_iota(jnp.int32, (PAD, 2 * HEAD_DIM), 1)

    def one_image(i, carry):
        inputs = tok[i].astype(F32)
        normed, _ = normalize(inputs)
        lowered = (normed * gain_one + shift_one).astype(BF16)
        for part in range(3):
            columns = pl.ds(part * D, D)
            qkv[i, :, columns] = dot(lowered, attnw[:, :, columns].reshape(D, D)).astype(BF16)
        for pair in range(HEADS // 2):
            offset = pair * 2 * HEAD_DIM
            query = qkv[i, :, offset : offset + 128]
            key_rows = qkv[i, :, D + offset : D + offset + 128]
            value = qkv[i, :, 2 * D + offset : 2 * D + offset + 128]
            results = []
            for which in range(2):
                probs = softmax_rows(query, key_rows, which, pair_lane)
                results.append(dot(probs.astype(BF16), value))
            joined = jnp.where(pair_lane < HEAD_DIM, results[0], results[1])
            att[i, :, offset : offset + 128] = joined.astype(BF16)
        mid = inputs + dot(att[i], attnw[:, :, 3 * D :].reshape(D, D)) + shift_out
        middle[i] = mid
        normed_two, _ = normalize(mid)
        u_all[me, i] = (normed_two * gain_two + shift_two).astype(BF16)
        part = u_all.at[me, i, pl.ds(0, SENT)]
        remote(part, part, u_send.at[i, 0], u_recv.at[i, 0], over).start()
        remote(part, part, u_send.at[i, 1], u_recv.at[i, 1], mate).start()

        @pl.when(i % 2 == 1)
        def _():
            hand_on(i // 2)

        return carry

    lax.fori_loop(0, images, one_image, 0)

    g_over_part = g_all.at[(1 - y) * CORES + core, :, pl.ds(0, SENT)]
    remote(g_over_part, g_over_part, g_sem.at[2], g_sem.at[3], over).wait()
    g_pass = remote(g_over_part, g_over_part, g_sem.at[4], g_sem.at[5], mate)
    g_pass.start()

    def pass_u(i, carry):
        part = u_all.at[(1 - y) * CORES + core, i, pl.ds(0, SENT)]
        remote(part, part, u_send.at[i, 0], u_recv.at[i, 0], over).wait_recv()
        remote(part, part, u_send.at[i, 2], u_recv.at[i, 2], mate).start()
        return carry

    lax.fori_loop(0, images, pass_u, 0)

    for k, partner in enumerate((mate, over, corner)):
        source = partner[1]
        remote(route, route_all.at[source], table_send.at[k, 0], table_recv.at[source, 0], partner).wait()
        remote(comb, comb_all.at[source], table_send.at[k, 1], table_recv.at[source, 1], partner).wait()
    for s in range(4):
        for el in range(local):
            named = me * local + el
            row = s * local + el
            hits = [route_all[s, t : t + 1, :] == named for t in range(TOP)]
            chosen[row : row + 1, :] = sum(jnp.where(h, 1.0, 0.0) for h in hits)
            comb_out[row : row + 1, :] = sum(
                jnp.where(h, comb_all[s, t : t + 1, :], 0.0) for t, h in enumerate(hits)
            )
    earlier = lax.broadcasted_iota(jnp.int32, (PAD, PAD), 0) < lax.broadcasted_iota(
        jnp.int32, (PAD, PAD), 1
    )
    earlier = jnp.where(earlier, 1.0, 0.0).astype(BF16)
    total = jnp.zeros((4 * local, 1), F32)
    for i in range(images):
        block = chosen[:, i * PAD : (i + 1) * PAD]
        position = total + dot(block.astype(BF16), earlier)
        place_out[:, i * PAD : (i + 1) * PAD] = jnp.where(block > 0.0, position, -1.0).astype(
            jnp.int32
        )
        total = total + jnp.sum(block, axis=1, keepdims=True)

    def hand_on_rest(step, carry):
        hand_on(step)
        return carry

    lax.fori_loop(images // 2, local * (lines - 1), hand_on_rest, 0)

    def wait_images(i, carry):
        part = u_all.at[me, i, pl.ds(0, SENT)]
        remote(part, part, u_send.at[i, 0], u_recv.at[i, 0], over).wait_send()
        remote(part, part, u_send.at[i, 1], u_recv.at[i, 1], mate).wait()
        remote(part, part, u_send.at[i, 2], u_recv.at[i, 2], mate).wait()
        return carry

    lax.fori_loop(0, images, wait_images, 0)
    to_mate.wait_send()
    g_mate.wait()
    g_pass.wait()
    own_copy.wait()

    def wait_weights(e, carry):
        one = wfull.at[e, :, dp]
        for hop in range(lines - 1):
            @pl.when(jnp.logical_and(z - hop >= 0, z < lines - 1))
            def _():
                remote(one, one, up_send.at[e, hop], up_recv.at[e, hop], above).wait_send()

            @pl.when(jnp.logical_and(z + hop <= lines - 1, z > 0))
            def _():
                remote(one, one, down_send.at[e, hop], down_recv.at[e, hop], below).wait_send()

        for place in range(lines):
            remote(one, one, x_send.at[e, place], x_recv.at[e, place], beside).wait()
        return carry

    lax.fori_loop(0, local, wait_weights, 0)


def front(shards, group, tok, cot, route, comb, attn, vec, expw):
    lines = shards // COLUMNS
    images, local = tok.shape[0], expw.shape[0]
    width = images * PAD
    dma = pltpu.SemaphoreType.DMA
    vm = pl.BlockSpec(memory_space=pltpu.VMEM)
    hbm = pl.BlockSpec(memory_space=pl.ANY)
    shape = jax.ShapeDtypeStruct
    return pl.pallas_call(
        functools.partial(front_kernel, shards, lines),
        out_shape=(
            shape((group, images, PAD, D), BF16),
            shape((group, images, PAD, D), BF16),
            shape((group * local, width), jnp.int32),
            shape((group * local, width), F32),
            shape((local, 2, shards) + expw.shape[2:], BF16),
            shape((shards,) + attn.shape, BF16),
            shape((8, D), F32),
            shape((images, PAD, D), F32),
            shape((images, PAD, 3 * D), BF16),
            shape((images, PAD, D), BF16),
        ),
        in_specs=[vm] * 6 + [hbm],
        out_specs=[vm] * 4 + [hbm] + [vm] * 5,
        scratch_shapes=[
            pltpu.VMEM((group, 8, width), jnp.int32),
            pltpu.VMEM((group, 8, width), F32),
            pltpu.VMEM((shards, 8, 128), F32),
            pltpu.VMEM((group * local, width), F32),
            dma((shards,)), dma((shards,)), dma((shards,)), dma((shards,)),
            dma((2,)), dma((3, 2)), dma((group, 2)),
            dma((6,)), dma((images, 3)), dma((images, 3)), dma(()),
            dma((local, lines)), dma((local, lines)), dma((local, lines)), dma((local, lines)),
            dma((local, lines)), dma((local, lines)),
        ],
        compiler_params=pltpu.CompilerParams(
            collective_id=0, has_side_effects=True, vmem_limit_bytes=VMEM_LIMIT
        ),
    )(tok, cot, route, comb, attn, vec, expw)


def gelu_parts(preact):
    size = jnp.abs(preact)
    inner = 1.0 / (1.0 + 0.23164189 * size)
    series = inner * (
        0.127414796
        + inner * (-0.142248368 + inner * (0.7107068705 + inner * (-0.7265760135 + inner * 0.5307027145)))
    )
    bell = jnp.exp(-0.5 * preact * preact)
    tail = series * bell
    area = jnp.where(preact >= 0.0, 1.0 - tail, tail)
    return preact * area, area + preact * bell * 0.3989422804014327


def expert_kernel(
    lines, place, comb, u_all, g_all, wfull,
    grads, own_out, got_mate, got_corner, got_over,
    ubuf, gbuf, wbuf, work, x_t, m_t, yacc, dacc, mine, sent, xr, zr, zs, fin,
    load_sem, w_sem, fin_sem, own_sem, x_send, x_recv, up_send, up_recv, down_send, down_recv,
    back_send, back_recv, credit_x, credit_up, credit_down,
):
    dp, me = lax.axis_index("dp"), lax.axis_index("expert")
    z, x = dp // COLUMNS, dp % COLUMNS
    y, core = me // CORES, me % CORES
    group, images = u_all.shape[0], u_all.shape[1]
    local = wfull.shape[0]
    slots = x_t.shape[1] // group
    ff = wfull.shape[-1]
    tile = work.shape[-1]
    tiles = ff // tile
    last = lines - 1
    mate = (dp, y * CORES + 1 - core)
    over = (dp, (1 - y) * CORES + core)
    above = (lax.rem(z + 1, lines) * COLUMNS + x, me)
    below = (lax.rem(z + last, lines) * COLUMNS + x, me)
    beside = (z * COLUMNS + 1 - x, me)
    greet([above, below, beside, mate, over])

    def load(step):
        slot = step % 2
        s = step % group
        return (
            pltpu.make_async_copy(u_all.at[s], ubuf.at[slot], load_sem.at[slot, 0]),
            pltpu.make_async_copy(g_all.at[s], gbuf.at[slot], load_sem.at[slot, 1]),
        )

    def load_weights(e):
        return pltpu.make_async_copy(wfull.at[e], wbuf, w_sem)

    def send_across(e, k):
        slot = e % 2
        return remote(sent.at[slot, k], xr.at[slot, k], x_send.at[slot, k], x_recv.at[slot, k], beside)

    def send_up(k, hop):
        return remote(zs.at[k, 0], zr.at[k, 0, hop], up_send.at[k], up_recv.at[k, hop], above)

    def send_down(k, hop):
        return remote(zs.at[k, 1], zr.at[k, 1, hop], down_send.at[k], down_recv.at[k, hop], below)

    def partial(e, k, owner):
        slot = e % 2
        return mine[slot, k, owner].astype(F32) + xr[slot, k, owner].astype(F32)

    def one_hop(e, k, hop, way, ahead, send, credit, owner):
        @pl.when(jnp.logical_and(ahead <= hop, ahead < last))
        def _():
            if hop > 0:
                @pl.when(ahead <= hop - 1)
                def _():
                    send(k, hop - 1).wait_send()

            @pl.when(jnp.logical_and(ahead == hop, e >= 1))
            def _():
                pl.semaphore_wait(credit.at[k], 1)

            value = partial(e, k, owner)
            if hop > 0:
                @pl.when(ahead >= 1)
                def _():
                    send(k, hop - 1).wait_recv()
                    zs[k, way] = (value + zr[k, way, hop - 1].astype(F32)).astype(BF16)

                @pl.when(ahead < 1)
                def _():
                    zs[k, way] = value.astype(BF16)
            else:
                zs[k, way] = value.astype(BF16)
            send(k, hop).start()

    def hop_step(e, k, hop):
        if hop == 0:
            send_across(e, k).wait_recv()
        one_hop(e, k, hop, 0, z, send_up, credit_up, jnp.minimum(z + last - hop, last))
        one_hop(e, k, hop, 1, last - z, send_down, credit_down, jnp.maximum(z - last + hop, 0))

    def finish(e, k):
        copy = pltpu.make_async_copy(fin.at[k], grads.at[e, k], fin_sem.at[k])

        @pl.when(e >= 1)
        def _():
            copy.wait()

        fin[k] = partial(e, k, z)

        @pl.when(z > 0)
        def _():
            send_up(k, last - 1).wait_recv()
            fin[k] += zr[k, 0, last - 1].astype(F32)
            send_down(k, last - 1).wait_send()

        @pl.when(z < last)
        def _():
            send_down(k, last - 1).wait_recv()
            fin[k] += zr[k, 1, last - 1].astype(F32)
            send_up(k, last - 1).wait_send()

        copy.start()

        @pl.when(jnp.logical_and(e + 1 < local, z > 0))
        def _():
            pl.semaphore_signal(credit_up.at[k], inc=1, device_id=below, device_id_type=MESH)

        @pl.when(jnp.logical_and(e + 1 < local, z < last))
        def _():
            pl.semaphore_signal(credit_down.at[k], inc=1, device_id=above, device_id_type=MESH)

        @pl.when(e + 2 < local)
        def _():
            pl.semaphore_signal(credit_x.at[k], inc=1, device_id=beside, device_id_type=MESH)

    def weight_grad(e, k):
        slot = e % 2
        left = x_t if k == 0 else m_t

        @pl.when(e >= 2)
        def _():
            send_across(e, k).wait_send()

        rows = wfull.shape[3]

        def one_tile(j, carry):
            right = work[tiles * (1 - k) + j, : group * slots, :]
            block = dot(left[...], right).astype(BF16)
            columns = pl.ds(pl.multiple_of(j * tile, tile), tile)
            for d in range(lines * COLUMNS):
                part = block[d * rows : (d + 1) * rows]

                @pl.when(x == d % COLUMNS)
                def _():
                    mine[slot, k, d // COLUMNS, :, columns] = part

                @pl.when(x != d % COLUMNS)
                def _():
                    sent[slot, k, d // COLUMNS, :, columns] = part

            return carry

        lax.fori_loop(0, tiles, one_tile, 0)

        @pl.when(e >= 2)
        def _():
            pl.semaphore_wait(credit_x.at[k], 1)

        send_across(e, k).start()

    slot_row = lax.broadcasted_iota(jnp.int32, (slots, images * PAD), 0)

    def one_source(e, s):
        step = e * group + s
        buffer = step % 2
        for copy in load(step):
            copy.wait()

        @pl.when(step + 1 < local * group)
        def _():
            for copy in load(step + 1):
                copy.start()

        row = s * local + e
        hit = slot_row == place[pl.ds(row, 1), :]
        pick = jnp.where(hit, 1.0, 0.0).astype(BF16)
        share = jnp.sum(jnp.where(hit, comb[pl.ds(row, 1), :], 0.0), axis=1, keepdims=True)
        arrived = dot(pick, ubuf[buffer].reshape(images * PAD, D)).astype(BF16)
        grad = (share * dot(pick, gbuf[buffer].reshape(images * PAD, D))).astype(BF16)
        here = pl.ds(pl.multiple_of(s * slots, slots), slots)
        x_t[:, here] = arrived.T
        m_t[:, here] = grad.T

        def one_tile(j, carry):
            columns = pl.ds(pl.multiple_of(j * tile, tile), tile)
            preact = dot(arrived, wbuf[0, :, :, columns].reshape(D, tile))
            hidden, slope = gelu_parts(preact)
            work[j, here, :] = hidden.astype(BF16)
            grad_hidden = dot(grad, wbuf[1, :, :, columns].reshape(D, tile))
            work[tiles + j, here, :] = (grad_hidden * slope).astype(BF16)
            return carry

        lax.fori_loop(0, tiles, one_tile, 0)
        made = jnp.zeros((slots, D), F32)
        back = jnp.zeros((slots, D), F32)
        for j in range(tiles):
            columns = pl.ds(j * tile, tile)
            made += contract_last(work[j, here, :], wbuf[1, :, :, columns].reshape(D, tile))
            back += contract_last(work[tiles + j, here, :], wbuf[0, :, :, columns].reshape(D, tile))
        made = (share * made.astype(BF16).astype(F32)).astype(BF16)
        back = back.astype(BF16)
        for i in range(images):
            part = pick[:, i * PAD : (i + 1) * PAD]
            rows = pl.ds(i * SENT, SENT)
            for total, values in ((yacc, made), (dacc, back)):
                placed = contract_rows(part, values)[:SENT]

                @pl.when(e == 0)
                def _():
                    total[s, rows, :] = placed

                @pl.when(e > 0)
                def _():
                    total[s, rows, :] += placed

    load_weights(0).start()
    for copy in load(0):
        copy.start()

    def one_expert(e, carry):
        load_weights(e).wait()

        def step(s, carry):
            one_source(e, s)
            before = e - 2
            for turn, actions in enumerate((
                (lambda: hop_step(before, 0, 0),),
                (lambda: hop_step(before, 0, 1), lambda: hop_step(before, 1, 0)),
                (lambda: hop_step(before, 0, 2), lambda: hop_step(before, 1, 1)),
                (lambda: finish(before, 0), lambda: hop_step(before, 1, 2)),
            )):
                @pl.when(jnp.logical_and(before >= 0, s == turn))
                def _():
                    for action in actions:
                        action()

            return carry

        lax.fori_loop(0, group, step, 0)

        @pl.when(e + 1 < local)
        def _():
            load_weights(e + 1).start()

        weight_grad(e, 0)

        @pl.when(e >= 2)
        def _():
            finish(e - 2, 1)

        weight_grad(e, 1)
        return carry

    lax.fori_loop(0, local, one_expert, 0)

    corner_s = (1 - y) * CORES + 1 - core
    mate_s = y * CORES + 1 - core
    over_s = (1 - y) * CORES + core
    sums = (dacc, yacc)
    for n, total in enumerate(sums):
        work[2 * n] = total[corner_s].astype(BF16)
        remote(work.at[2 * n], got_corner.at[n], back_send.at[n, 0], back_recv.at[n, 0], mate).start()
        work[2 * n + 1] = total[mate_s].astype(BF16)
        remote(work.at[2 * n + 1], got_mate.at[n], back_send.at[n, 1], back_recv.at[n, 1], mate).start()
    for n, total in enumerate(sums):
        pltpu.make_async_copy(total.at[me], own_out.at[n], own_sem.at[n]).start()
    for n, total in enumerate(sums):
        remote(work.at[2 * n], got_corner.at[n], back_send.at[n, 0], back_recv.at[n, 0], mate).wait_recv()
        landed = pltpu.make_async_copy(got_corner.at[n], work.at[4 + n], own_sem.at[2])
        landed.start()
        landed.wait()
        work[4 + n] = (total[over_s] + work[4 + n].astype(F32)).astype(BF16)
        remote(work.at[4 + n], got_over.at[n], back_send.at[n, 2], back_recv.at[n, 2], over).start()

    def drain(e, carry):
        hop_step(e, 0, 0)
        hop_step(e, 0, 1)
        hop_step(e, 0, 2)
        hop_step(e, 1, 0)
        finish(e, 0)
        hop_step(e, 1, 1)
        hop_step(e, 1, 2)
        finish(e, 1)
        for k in range(2):
            send_across(e, k).wait_send()
        return carry

    lax.fori_loop(local - 2, local, drain, 0)
    for n, total in enumerate(sums):
        remote(work.at[2 * n], got_corner.at[n], back_send.at[n, 0], back_recv.at[n, 0], mate).wait_send()
        remote(work.at[2 * n + 1], got_mate.at[n], back_send.at[n, 1], back_recv.at[n, 1], mate).wait()
        remote(work.at[4 + n], got_over.at[n], back_send.at[n, 2], back_recv.at[n, 2], over).wait()
        pltpu.make_async_copy(total.at[me], own_out.at[n], own_sem.at[n]).wait()
        pltpu.make_async_copy(fin.at[n], grads.at[0, n], fin_sem.at[n]).wait()


def experts_step(shards, capacity, place, comb, u_all, g_all, wfull):
    lines = shards // COLUMNS
    group, images = u_all.shape[:2]
    local, _, _, rows, ff = wfull.shape
    slots = -(-capacity // 128) * 128
    tile = 512
    tiles = ff // tile
    sent_rows = images * SENT
    dma = pltpu.SemaphoreType.DMA
    regular = pltpu.SemaphoreType.REGULAR
    vm = pl.BlockSpec(memory_space=pltpu.VMEM)
    hbm = pl.BlockSpec(memory_space=pl.ANY)
    shape = jax.ShapeDtypeStruct
    hops = lines - 1
    return pl.pallas_call(
        functools.partial(expert_kernel, lines),
        out_shape=(
            shape((local, 2, rows, ff), F32),
            shape((2, sent_rows, D), F32),
            shape((2, sent_rows, D), BF16),
            shape((2, sent_rows, D), BF16),
            shape((2, sent_rows, D), BF16),
        ),
        in_specs=[vm] * 2 + [hbm] * 3,
        out_specs=[hbm] * 5,
        scratch_shapes=[
            pltpu.VMEM((2, images, PAD, D), BF16),
            pltpu.VMEM((2, images, PAD, D), BF16),
            pltpu.VMEM((2, shards, rows, ff), BF16),
            pltpu.VMEM((2 * tiles, max(sent_rows, group * slots), tile), BF16),
            pltpu.VMEM((D, group * slots), BF16),
            pltpu.VMEM((D, group * slots), BF16),
            pltpu.VMEM((group, sent_rows, D), F32),
            pltpu.VMEM((group, sent_rows, D), F32),
            pltpu.VMEM((2, 2, lines, rows, ff), BF16),
            pltpu.VMEM((2, 2, lines, rows, ff), BF16),
            pltpu.VMEM((2, 2, lines, rows, ff), BF16),
            pltpu.VMEM((2, 2, hops, rows, ff), BF16),
            pltpu.VMEM((2, 2, rows, ff), BF16),
            pltpu.VMEM((2, rows, ff), F32),
            dma((2, 2)), dma(()), dma((2,)), dma((3,)),
            dma((2, 2)), dma((2, 2)), dma((2,)), dma((2, hops)), dma((2,)), dma((2, hops)),
            dma((2, 3)), dma((2, 3)),
            regular((2,)), regular((2,)), regular((2,)),
        ],
        compiler_params=pltpu.CompilerParams(
            collective_id=1, has_side_effects=True, vmem_limit_bytes=VMEM_LIMIT
        ),
    )(place, comb, u_all, g_all, wfull)


def adam_update(master, first, second, gradient, step_rate, decay_rate):
    first = BETA_ONE * first + (1.0 - BETA_ONE) * gradient
    second = BETA_TWO * second + (1.0 - BETA_TWO) * gradient * gradient
    first_hat = first / (1.0 - BETA_ONE**STEP)
    second_hat = second / (1.0 - BETA_TWO**STEP)
    master = master - step_rate * (
        first_hat / (jnp.sqrt(second_hat) + ADAM_EPS) + decay_rate * master
    )
    return (master, first, second)


def back_kernel(
    lines, tok, cot, middle, qkv, att, attnw, vectors, own, got_mate, got_over,
    attn_old, first_old, second_old, vec_old, vec_first_old, vec_second_old,
    mixed, grad_tok, attn_new, first_new, second_new, vec_new, vec_first_new, vec_second_new,
    g_low, g_mid, dqkv, lowered, d_att, v_sum,
    part_own, part_a, sum_a, part_b, sum_b, part_c, sum_c, part_d, sum_d, whole,
    v_stage, v_got, v_lines,
    a_sem, b_sem, c_sem, d_send, d_recv, e_send, e_recv, v_sem, vd_send, vd_recv,
):
    dp, me = lax.axis_index("dp"), lax.axis_index("expert")
    z, x = dp // COLUMNS, dp % COLUMNS
    y, core = me // CORES, me % CORES
    images = tok.shape[0]
    shards, rows = attnw.shape[:2]
    half, quarter = rows // 2, rows // 4
    mate = (dp, y * CORES + 1 - core)
    over = (dp, (1 - y) * CORES + core)
    corner = (dp, (1 - y) * CORES + 1 - core)
    beside = (z * COLUMNS + 1 - x, me)
    along = [(lax.rem(z + k, lines) * COLUMNS + x, me) for k in range(1, lines)]
    greet([mate, over, corner, beside] + along)
    gain_one, shift_one = vectors[0:1], vectors[1:2]
    gain_two = vectors[2:3]
    v_sum[...] = jnp.zeros_like(v_sum)

    def rows_of(start, size):
        return pl.ds(pl.multiple_of(start, quarter), size)

    kept, given = rows_of(core * half, half), rows_of((1 - core) * half, half)
    kept_y, given_y = rows_of(y * quarter, quarter), rows_of((1 - y) * quarter, quarter)
    final_rows = rows_of(core * half + y * quarter, quarter)

    def move_a(p):
        return remote(part_own.at[p, :, given], part_a.at[p], a_sem.at[p, 0], a_sem.at[p, 1], mate)

    def move_b(p):
        return remote(sum_a.at[p, :, given_y], part_b.at[p], b_sem.at[p, 0], b_sem.at[p, 1], over)

    def move_c(p):
        return remote(sum_b.at[p, :, 1 - x], part_c.at[p], c_sem.at[p, 0], c_sem.at[p, 1], beside)

    def move_d(p, k):
        target = lax.rem(z + k, lines)
        return remote(sum_c.at[p, target], part_d.at[p, z], d_send.at[p, k - 1], d_recv.at[p, z], along[k - 1])

    def arrived_d(p, k):
        source = lax.rem(z + lines - k, lines)
        return remote(sum_c.at[p, source], part_d.at[p, source], d_send.at[p, k - 1], d_recv.at[p, source], along[k - 1])

    def move_e(p, k):
        columns = pl.ds(p * D, D)
        mine = whole.at[final_rows, columns]
        return remote(mine, mine, e_send.at[p, k], e_recv.at[p, k], (mate, over, corner)[k])

    def stage_b(p):
        move_a(p).wait()
        sum_a[p] = (part_own[p, :, kept].astype(F32) + part_a[p].astype(F32)).astype(BF16)
        move_b(p).start()

    def stage_c(p):
        move_b(p).wait()
        total = sum_a[p, :, kept_y].astype(F32) + part_b[p].astype(F32)
        sum_b[p] = total.astype(BF16).reshape(lines, COLUMNS, quarter, D)
        move_c(p).start()

    def stage_d(p):
        move_c(p).wait()
        total = sum_b[p, :, x].astype(F32) + part_c[p].astype(F32)
        sum_c[p] = total.astype(BF16)
        sum_d[p] = total
        for k in range(1, lines):
            move_d(p, k).start()

    def stage_e(p):
        total = sum_d[p, z]
        for k in range(1, lines):
            arrived_d(p, k).wait_recv()
            total = total + part_d[p, lax.rem(z + lines - k, lines)].astype(F32)
        whole[final_rows, pl.ds(p * D, D)] = total
        for k in range(3):
            move_e(p, k).start()

    def settle(p):
        for k in range(1, lines):
            move_d(p, k).wait_send()
        for k in range(3):
            move_e(p, k).wait()

    def scatter_part(p, left, right):
        block = contract_rows(left, right).astype(BF16)
        part_own[p] = block.reshape(shards, rows, D)
        move_a(p).start()

    def before_attention(i, carry):
        here = pl.ds(pl.multiple_of(i * SENT, SENT), SENT)
        mid = middle[i]
        returned = own[1, here] + got_mate[1, here].astype(F32) + got_over[1, here].astype(F32)
        mixed[i, :SENT] = (mid[:SENT] + returned).astype(BF16)
        normed, inverse = normalize(mid)
        grad = own[0, here] + got_mate[0, here].astype(F32) + got_over[0, here].astype(F32)
        grad = jnp.concatenate([grad, jnp.zeros((PAD - SENT, D), F32)], axis=0)
        v_sum[2:3] += jnp.sum(grad * normed, axis=0, keepdims=True)
        v_sum[3:4] += jnp.sum(grad, axis=0, keepdims=True)
        total = cot[i].astype(F32) + norm_back(grad * gain_two, normed, inverse)
        v_sum[4:5] += jnp.sum(total, axis=0, keepdims=True)
        g_mid[i] = total
        low = total.astype(BF16)
        g_low[i] = low
        d_att[i] = contract_last(low, attnw[:, :, 3 * D :].reshape(D, D)).astype(BF16)
        return carry

    lax.fori_loop(0, images, before_attention, 0)
    scatter_part(3, att[...].reshape(images * PAD, D), g_low[...].reshape(images * PAD, D))
    pair_lane = lax.broadcasted_iota(jnp.int32, (PAD, 2 * HEAD_DIM), 1)

    def attention(i, carry):
        for pair in range(HEADS // 2):
            offset = pair * 2 * HEAD_DIM
            query = qkv[i, :, offset : offset + 128]
            key_rows = qkv[i, :, D + offset : D + offset + 128]
            value = qkv[i, :, 2 * D + offset : 2 * D + offset + 128]
            grad = d_att[i, :, offset : offset + 128]
            results = []
            for which in range(2):
                probs = softmax_rows(query, key_rows, which, pair_lane)
                grad_own = jnp.where(pair_lane // HEAD_DIM == which, grad, jnp.zeros_like(grad))
                grad_probs = contract_last(grad_own, value)
                inner = jnp.sum(probs * grad_probs, axis=-1, keepdims=True)
                grad_scores = (probs * (grad_probs - inner)).astype(BF16)
                results.append((
                    dot(grad_scores, key_rows) * HEAD_DIM ** (-0.5),
                    contract_rows(grad_scores, query) * HEAD_DIM ** (-0.5),
                    contract_rows(probs.astype(BF16), grad),
                ))
            for part in range(3):
                joined = jnp.where(pair_lane < HEAD_DIM, results[0][part], results[1][part])
                dqkv[i, :, part * D + offset : part * D + offset + 128] = joined.astype(BF16)
        grad = jnp.zeros((PAD, D), F32)
        for part in range(3):
            columns = pl.ds(part * D, D)
            grad += contract_last(dqkv[i, :, columns], attnw[:, :, columns].reshape(D, D))
        normed, inverse = normalize(tok[i].astype(F32))
        lowered[i] = (normed * gain_one + shift_one).astype(BF16)
        v_sum[0:1] += jnp.sum(grad * normed, axis=0, keepdims=True)
        v_sum[1:2] += jnp.sum(grad, axis=0, keepdims=True)
        grad_tok[i] = (g_mid[i] + norm_back(grad * gain_one, normed, inverse)).astype(BF16)
        for turn, stage in enumerate((stage_b, stage_c, stage_d, stage_e)):
            @pl.when(i == turn)
            def _():
                stage(3)

        return carry

    lax.fori_loop(0, images, attention, 0)

    def v_move(n, partner):
        return remote(v_stage.at[n], v_got.at[n], v_sem.at[n, 0], v_sem.at[n, 1], partner)

    v_stage[0] = v_sum[...]
    v_move(0, mate).start()
    for p in range(3):
        scatter_part(p, lowered[...].reshape(images * PAD, D), dqkv[:, :, p * D : (p + 1) * D].reshape(images * PAD, D))
    for n, (stage, partner) in enumerate(((stage_b, over), (stage_c, beside), (stage_d, None))):
        for p in range(3):
            stage(p)
        v_move(n, (mate, over, beside)[n]).wait()
        total = v_stage[n] + v_got[n]
        if partner is not None:
            v_stage[n + 1] = total
            v_move(n + 1, partner).start()
        else:
            v_lines[z] = total
            for k in range(1, lines):
                remote(v_lines.at[z], v_lines.at[z], vd_send.at[k - 1], vd_recv.at[z], along[k - 1]).start()
    for p in range(3):
        stage_e(p)
    for k in range(1, lines):
        source = lax.rem(z + lines - k, lines)
        remote(v_lines.at[source], v_lines.at[source], vd_send.at[k - 1], vd_recv.at[source], along[k - 1]).wait()
    total = v_lines[0]
    for n in range(1, lines):
        total = total + v_lines[n]
    width = D // shards
    for d in range(shards):
        @pl.when(dp == d)
        def _():
            gradient = total[: vec_old.shape[0], d * width : (d + 1) * width]
            new = adam_update(vec_old[...], vec_first_old[...], vec_second_old[...], gradient, 0.2, 0.0)
            vec_new[...], vec_first_new[...], vec_second_new[...] = new

    for p in (3, 0, 1, 2):
        settle(p)
        columns = pl.ds(p * D, D)
        new = adam_update(
            attn_old[:, columns], first_old[:, columns], second_old[:, columns], whole[:, columns], 0.03, 0.1
        )
        attn_new[:, columns], first_new[:, columns], second_new[:, columns] = new


def back(shards, tok, cot, middle, qkv, att, attnw, vectors, own, got_mate, got_over, attn_state, vec_state):
    lines = shards // COLUMNS
    images = tok.shape[0]
    rows = attnw.shape[1]
    half, quarter = rows // 2, rows // 4
    dma = pltpu.SemaphoreType.DMA
    vm = pl.BlockSpec(memory_space=pltpu.VMEM)
    shape = jax.ShapeDtypeStruct
    state = [shape(a.shape, F32) for a in attn_state + vec_state]
    return pl.pallas_call(
        functools.partial(back_kernel, lines),
        out_shape=[shape((images, PAD, D), BF16)] * 2 + state,
        in_specs=[vm] * 16,
        out_specs=[vm] * 8,
        scratch_shapes=[
            pltpu.VMEM((images, PAD, D), BF16),
            pltpu.VMEM((images, PAD, D), F32),
            pltpu.VMEM((images, PAD, 3 * D), BF16),
            pltpu.VMEM((images, PAD, D), BF16),
            pltpu.VMEM((images, PAD, D), BF16),
            pltpu.VMEM((8, D), F32),
            pltpu.VMEM((4, shards, rows, D), BF16),
            pltpu.VMEM((4, shards, half, D), BF16),
            pltpu.VMEM((4, shards, half, D), BF16),
            pltpu.VMEM((4, shards, quarter, D), BF16),
            pltpu.VMEM((4, lines, COLUMNS, quarter, D), BF16),
            pltpu.VMEM((4, lines, quarter, D), BF16),
            pltpu.VMEM((4, lines, quarter, D), BF16),
            pltpu.VMEM((4, lines, quarter, D), BF16),
            pltpu.VMEM((4, lines, quarter, D), F32),
            pltpu.VMEM((rows, 4 * D), F32),
            pltpu.VMEM((3, 8, D), F32),
            pltpu.VMEM((3, 8, D), F32),
            pltpu.VMEM((lines, 8, D), F32),
            dma((4, 2)), dma((4, 2)), dma((4, 2)), dma((4, lines - 1)), dma((4, lines)),
            dma((4, 3)), dma((4, 3)), dma((3, 2)), dma((lines - 1,)), dma((lines,)),
        ],
        compiler_params=pltpu.CompilerParams(
            collective_id=2, has_side_effects=True, vmem_limit_bytes=VMEM_LIMIT
        ),
    )(tok, cot, middle, qkv, att, attnw, vectors, own, got_mate, got_over, *attn_state, *vec_state)


def by_image(rows):
    images = rows.shape[0] // SEQ
    return jnp.pad(rows.reshape((images, SEQ) + rows.shape[1:]), ((0, 0), (0, PAD - SEQ), (0, 0)))


def as_lanes(table, fill):
    images = table.shape[0] // SEQ
    wide = table.T.reshape(TOP, images, SEQ)
    wide = jnp.pad(wide, ((0, 8 - TOP), (0, 0), (0, PAD - SEQ)), constant_values=fill)
    return wide.reshape(8, images * PAD)


def to_tokens(rows, count):
    return rows[:, :SEQ].reshape(count, D)


def chip_body(shards, group):
    def run(
        tokens, cotangent, routes, combine, attn_master, attn_first, attn_second,
        vector_master, vector_first, vector_second, expert_master, expert_first, expert_second,
    ):
        count = tokens.shape[0]
        experts = expert_master.shape[2] * group
        capacity = max(2, 4 * count // experts)
        width = vector_master.shape[1]
        tok, cot = by_image(tokens), by_image(cotangent)
        vec = jnp.pad(
            vector_master, ((0, 8 - vector_master.shape[0]), (0, 128 - width))
        )
        shard = jnp.transpose(expert_master.astype(BF16), (2, 1, 0, 3))
        u_all, g_all, place, comb, wfull, attnw, vectors, middle, qkv, att = front(
            shards, group, tok, cot, as_lanes(routes, -1), as_lanes(combine, 0.0),
            attn_master.astype(BF16), vec, shard,
        )
        grads, own, got_mate, _, got_over = experts_step(
            shards, capacity, place, comb, u_all, g_all, wfull
        )
        mixed, grad_tokens, *state = back(
            shards, tok, cot, middle, qkv, att, attnw, vectors, own, got_mate, got_over,
            [attn_master, attn_first, attn_second], [vector_master, vector_first, vector_second],
        )
        expert_new = adam_update(
            expert_master, expert_first, expert_second, jnp.transpose(grads, (2, 1, 0, 3)), 0.02, 0.1
        )
        return (to_tokens(mixed, count), to_tokens(grad_tokens, count), *state, *expert_new)

    return run


def gelu_slope(preact):
    return (
        0.5 * (1.0 + lax.erf(preact * 0.7071067811865476))
        + preact * jnp.exp(-0.5 * preact * preact) * 0.3989422804014327
    )


def slot_places(routes, experts):
    flat_routes = routes.reshape(-1)
    onehot = (flat_routes[:, None] == jnp.arange(experts, dtype=jnp.int32)[None, :]).astype(
        jnp.int32
    )
    before = jnp.cumsum(onehot, axis=0) - onehot
    return jnp.sum(before * onehot, axis=1)


def general_body(
    tokens,
    cotangent,
    routes,
    combine,
    attn_master,
    attn_first,
    attn_second,
    vector_master,
    vector_first,
    vector_second,
    expert_master,
    expert_first,
    expert_second,
):
    group_size = lax.axis_size("expert")
    local_experts = expert_master.shape[2]
    experts = local_experts * group_size
    token_count = tokens.shape[0]
    capacity = max(2, 4 * token_count // experts)
    images = token_count // SEQ
    score_scale = HEAD_DIM ** (-0.5)
    attn_weight, vector_weight, expert_weight = (
        lax.all_gather(attn_master.astype(jnp.bfloat16), "dp", axis=0, tiled=True),
        lax.all_gather(vector_master.astype(jnp.bfloat16), "dp", axis=1, tiled=True),
        lax.all_gather(expert_master.astype(jnp.bfloat16), "dp", axis=0, tiled=True),
    )
    vectors = vector_weight.astype(jnp.float32)
    w_packed = attn_weight[:, : 3 * D]
    w_project = attn_weight[:, 3 * D :]
    inputs = tokens.astype(jnp.float32)
    normed_one, inverse_one = normalize(inputs)
    lowered_one = (normed_one * vectors[0] + vectors[1]).astype(jnp.bfloat16)
    packed = jnp.dot(lowered_one, w_packed, preferred_element_type=jnp.float32).astype(jnp.bfloat16)
    packed = packed.reshape(images, SEQ, 3, HEADS, HEAD_DIM)
    queries = packed[:, :, 0]
    keys_all = packed[:, :, 1]
    values_all = packed[:, :, 2]
    scores = (
        jnp.einsum("bqhc,bkhc->bhqk", queries, keys_all, preferred_element_type=jnp.float32)
        * score_scale
    )
    softmax_out = jax.nn.softmax(scores, axis=-1)
    softmax_low = softmax_out.astype(jnp.bfloat16)
    attended = jnp.einsum(
        "bhqk,bkhc->bqhc", softmax_low, values_all, preferred_element_type=jnp.float32
    )
    attended = attended.reshape(token_count, D).astype(jnp.bfloat16)
    middle = inputs + jnp.dot(attended, w_project, preferred_element_type=jnp.float32) + vectors[4]
    normed_two, inverse_two = normalize(middle)
    mixed_in = (normed_two * vectors[2] + vectors[3]).astype(jnp.bfloat16)
    slot_index = routes.reshape(-1) * capacity + slot_places(routes, experts)

    def dispatch(slot_rows):
        filled = jnp.zeros((experts * capacity, D), jnp.bfloat16).at[slot_index].set(slot_rows)
        return filled.reshape(group_size, local_experts, capacity, D)

    def collect(returned):
        picked = returned.reshape(experts * capacity, D)[slot_index]
        return picked.reshape(token_count, TOP, D).astype(jnp.float32)

    received = lax.all_to_all(
        dispatch(jnp.repeat(mixed_in, TOP, axis=0)),
        "expert",
        split_axis=0,
        concat_axis=0,
        tiled=True,
    )
    produced = []
    for expert_item in range(local_experts):
        arrived = received[:, expert_item].reshape(group_size * capacity, D)
        preact = jnp.dot(
            arrived, expert_weight[:, 0, expert_item], preferred_element_type=jnp.float32
        )
        hidden = jax.nn.gelu(preact, approximate=False).astype(jnp.bfloat16)
        output_rows = contract_last(hidden, expert_weight[:, 1, expert_item]).astype(jnp.bfloat16)
        produced.append(output_rows.reshape(group_size, capacity, D))
    returned = lax.all_to_all(
        jnp.stack(produced, 1), "expert", split_axis=0, concat_axis=0, tiled=True
    )
    mixed = middle + jnp.sum(combine[:, :, None] * collect(returned), axis=1)
    grad_out = cotangent.astype(jnp.float32)
    slot_grads = (
        (combine[:, :, None] * grad_out[:, None, :])
        .reshape(token_count * TOP, D)
        .astype(jnp.bfloat16)
    )
    grads_in = lax.all_to_all(
        dispatch(slot_grads), "expert", split_axis=0, concat_axis=0, tiled=True
    )
    sent_back = []
    shards = []
    for expert_item in range(local_experts):
        arrived = received[:, expert_item].reshape(group_size * capacity, D)
        arrived_grad = grads_in[:, expert_item].reshape(group_size * capacity, D)
        w_in = expert_weight[:, 0, expert_item]
        w_out = expert_weight[:, 1, expert_item]
        preact = jnp.dot(arrived, w_in, preferred_element_type=jnp.float32)
        hidden = jax.nn.gelu(preact, approximate=False).astype(jnp.bfloat16)
        grad_hidden = jnp.dot(arrived_grad, w_out, preferred_element_type=jnp.float32)
        grad_pre = (grad_hidden * gelu_slope(preact)).astype(jnp.bfloat16)
        sent_back.append(
            contract_last(grad_pre, w_in).astype(jnp.bfloat16).reshape(group_size, capacity, D)
        )
        full_grad = jnp.stack(
            [contract_rows(arrived, grad_pre), contract_rows(arrived_grad, hidden)], 1
        )
        shards.append(lax.psum_scatter(full_grad, "dp", scatter_dimension=0, tiled=True))
    expert_grad = jnp.stack(shards, 2)
    returned_grads = lax.all_to_all(
        jnp.stack(sent_back, 1), "expert", split_axis=0, concat_axis=0, tiled=True
    )
    grad_mixed = jnp.sum(collect(returned_grads), axis=1)
    grad_gain_two = jnp.sum(grad_mixed * normed_two, axis=0)
    grad_shift_two = jnp.sum(grad_mixed, axis=0)
    grad_middle = grad_out + norm_back(grad_mixed * vectors[2], normed_two, inverse_two)
    middle_low = grad_middle.astype(jnp.bfloat16)
    grad_project = contract_rows(attended, middle_low)
    grad_attended = (
        contract_last(middle_low, w_project)
        .astype(jnp.bfloat16)
        .reshape(images, SEQ, HEADS, HEAD_DIM)
    )
    grad_soft = jnp.einsum(
        "bqhc,bkhc->bhqk", grad_attended, values_all, preferred_element_type=jnp.float32
    )
    grad_scores = (
        softmax_out * (grad_soft - jnp.sum(softmax_out * grad_soft, axis=-1, keepdims=True))
    ).astype(jnp.bfloat16)
    grad_queries = (
        jnp.einsum("bhqk,bkhc->bqhc", grad_scores, keys_all, preferred_element_type=jnp.float32)
        * score_scale
    )
    grad_keys = (
        jnp.einsum("bhqk,bqhc->bkhc", grad_scores, queries, preferred_element_type=jnp.float32)
        * score_scale
    )
    grad_values = jnp.einsum(
        "bhqk,bqhc->bkhc", softmax_low, grad_attended, preferred_element_type=jnp.float32
    )
    grad_packed = (
        jnp.stack([grad_queries, grad_keys, grad_values], 2)
        .reshape(token_count, 3 * D)
        .astype(jnp.bfloat16)
    )
    grad_weight_packed = contract_rows(lowered_one, grad_packed)
    grad_lowered = contract_last(grad_packed, w_packed)
    grad_gain_one = jnp.sum(grad_lowered * normed_one, axis=0)
    grad_shift_one = jnp.sum(grad_lowered, axis=0)
    grad_tokens = grad_middle + norm_back(grad_lowered * vectors[0], normed_one, inverse_one)
    attn_grad = jnp.concatenate([grad_weight_packed, grad_project], axis=1)
    vector_grad = jnp.stack(
        [
            grad_gain_one,
            grad_shift_one,
            grad_gain_two,
            grad_shift_two,
            jnp.sum(grad_middle, axis=0),
        ],
        0,
    )
    attn_whole, vector_whole = lax.psum((attn_grad, vector_grad), "expert")
    attn_part, vector_part = (
        lax.psum_scatter(attn_whole, "dp", scatter_dimension=0, tiled=True),
        lax.psum_scatter(vector_whole, "dp", scatter_dimension=1, tiled=True),
    )
    attn_new = adam_update(attn_master, attn_first, attn_second, attn_part, 0.03, 0.1)
    vector_new = adam_update(vector_master, vector_first, vector_second, vector_part, 0.2, 0.0)
    expert_new = adam_update(expert_master, expert_first, expert_second, expert_grad, 0.02, 0.1)
    return (
        mixed.astype(jnp.bfloat16),
        grad_tokens.astype(jnp.bfloat16),
        attn_new[0],
        attn_new[1],
        attn_new[2],
        vector_new[0],
        vector_new[1],
        vector_new[2],
        expert_new[0],
        expert_new[1],
        expert_new[2],
    )


def solution(mesh):
    shards, group = mesh.shape["dp"], mesh.shape["expert"]
    chips = shards == 4 * COLUMNS and group == 2 * CORES
    body = chip_body(shards, group) if chips else general_body
    return jax.shard_map(
        body,
        mesh=mesh,
        in_specs=(
            P(("dp", "expert"), None),
            P(("dp", "expert"), None),
            P(("dp", "expert"), None),
            P(("dp", "expert"), None),
            P("dp", None),
            P("dp", None),
            P("dp", None),
            P(None, "dp"),
            P(None, "dp"),
            P(None, "dp"),
            P("dp", None, "expert", None),
            P("dp", None, "expert", None),
            P("dp", None, "expert", None),
        ),
        out_specs=(
            P(("dp", "expert"), None),
            P(("dp", "expert"), None),
            P("dp", None),
            P("dp", None),
            P("dp", None),
            P(None, "dp"),
            P(None, "dp"),
            P(None, "dp"),
            P("dp", None, "expert", None),
            P("dp", None, "expert", None),
            P("dp", None, "expert", None),
        ),
        check_vma=False,
    )
```

```python
import functools

import jax
import jax.numpy as jnp
from jax import lax
from jax.experimental import pallas as pl
from jax.experimental.pallas import tpu as pltpu
from jax.sharding import PartitionSpec as P

D = 512
HEADS = 8
HEAD_DIM = 64
SEQ = 197
TOP = 2
STEP = 10
PAD = 256
SENT = 208
CORES = 2
COLUMNS = 2

LN_EPS = 1e-06
BETA_ONE = 0.9
BETA_TWO = 0.999
ADAM_EPS = 1e-08
MESH = pl.DeviceIdType.MESH
F32 = jnp.float32
BF16 = jnp.bfloat16
VMEM_LIMIT = 63 * 1024 * 1024


def dot(left, right):
    return jnp.dot(left, right, preferred_element_type=F32)


def contract_rows(left, right):
    return lax.dot_general(
        left, right, (((0,), (0,)), ((), ())), preferred_element_type=F32
    )


def contract_last(left, right):
    return lax.dot_general(
        left, right, (((1,), (1,)), ((), ())), preferred_element_type=F32
    )


def normalize(values):
    centered = values - jnp.mean(values, axis=-1, keepdims=True)
    inverse = lax.rsqrt(jnp.mean(centered * centered, axis=-1, keepdims=True) + LN_EPS)
    return (centered * inverse, inverse)


def norm_back(grad_normed, normed, inverse):
    first_mean = jnp.mean(grad_normed, axis=-1, keepdims=True)
    second_mean = jnp.mean(grad_normed * normed, axis=-1, keepdims=True)
    return inverse * (grad_normed - first_mean - normed * second_mean)


def remote(source, target, send_sem, recv_sem, device):
    return pltpu.make_async_remote_copy(
        src_ref=source,
        dst_ref=target,
        send_sem=send_sem,
        recv_sem=recv_sem,
        device_id=device,
        device_id_type=MESH,
    )


def greet(devices):
    barrier = pltpu.get_barrier_semaphore()
    for device in devices:
        pl.semaphore_signal(barrier, inc=1, device_id=device, device_id_type=MESH)
    pl.semaphore_wait(barrier, len(devices))


def softmax_rows(query, key_rows, half, lane):
    own = jnp.where(lane // HEAD_DIM == half, query, jnp.zeros_like(query))
    scores = contract_last(own, key_rows) * HEAD_DIM ** (-0.5)
    column = lax.broadcasted_iota(jnp.int32, scores.shape, 1)
    scores = jnp.where(column < SEQ, scores, -1e30)
    powers = jnp.exp(scores - jnp.max(scores, axis=-1, keepdims=True))
    return powers * (1.0 / jnp.sum(powers, axis=-1, keepdims=True))


def gelu_parts(preact):
    size = jnp.abs(preact)
    inner = 1.0 / (1.0 + 0.23164189 * size)
    series = inner * (
        0.127414796
        + inner * (-0.142248368 + inner * (0.7107068705 + inner * (-0.7265760135 + inner * 0.5307027145)))
    )
    bell = jnp.exp(-0.5 * preact * preact)
    tail = series * bell
    area = jnp.where(preact >= 0.0, 1.0 - tail, tail)
    return preact * area, area + preact * bell * 0.3989422804014327


def adam_update(master, first, second, gradient, step_rate, decay_rate):
    first = BETA_ONE * first + (1.0 - BETA_ONE) * gradient
    second = BETA_TWO * second + (1.0 - BETA_TWO) * gradient * gradient
    first_hat = first / (1.0 - BETA_ONE**STEP)
    second_hat = second / (1.0 - BETA_TWO**STEP)
    master = master - step_rate * (
        first_hat / (jnp.sqrt(second_hat) + ADAM_EPS) + decay_rate * master
    )
    return (master, first, second)


ROUTE_FIRST = (1,)
SUM_FIRST = (0, 2)
CHAINS = (0, 2, 1, 3)


def block_kernel(
    shards, lines, slots,
    route, comb, attn, vec, vec_old, vec_first_old, vec_second_old,
    tok, cot, expw, attn_old, first_old, second_old,
    vec_new, vec_first_new, vec_second_new,
    u_all, g_all, wfull, middle, qkv, att, own_out, d_mate, d_corner, d_over, y_stage, y_got,
    grads, mixed, grad_tok, attn_new, first_new, second_new,
    attnw, route_all, comb_all, vslots, chosen, place, shares,
    gst, xr, xo, xst, zr, zs, fin,
    part_a, part_b, part_c, part_d, whole, v_sum, v_stage, v_got, v_lines,
    attn_send, attn_recv, vec_send, vec_recv, pass_sem, table_send, table_recv,
    g_sem, u_send, u_recv, own_sem, up_send, up_recv, down_send, down_recv, x_send, x_recv,
    out_sem, in_sem, load_sem, w_sem, fin_sem,
    rx_send, rx_recv, ro_send, ro_recv, ru_send, ru_recv, rd_send, rd_recv, credit_up, credit_down,
    back_send, back_recv, y_send, y_recv,
    a_sem, b_sem, c_sem, d_send, d_recv, e_send, e_recv, v_sem, vd_send, vd_recv,
):
    dp, me = lax.axis_index("dp"), lax.axis_index("expert")
    z, x = dp // COLUMNS, dp % COLUMNS
    y, core = me // CORES, me % CORES
    group, images = u_all.shape[:2]
    local, _, rows, ff = expw.shape
    last = lines - 1
    half, quarter = rows // 2, rows // 4
    tile = 512
    tiles = ff // tile
    mate_s, over_s, corner_s = y * CORES + 1 - core, (1 - y) * CORES + core, (1 - y) * CORES + 1 - core
    mate, over, corner = (dp, mate_s), (dp, over_s), (dp, corner_s)
    above = (lax.rem(z + 1, lines) * COLUMNS + x, me)
    below = (lax.rem(z + last, lines) * COLUMNS + x, me)
    beside = (z * COLUMNS + 1 - x, me)
    along = [(lax.rem(z + k, lines) * COLUMNS + x, me) for k in range(1, lines)]
    peers = [(lax.rem(dp + k, shards), me) for k in range(1, shards)]
    sources = [lax.rem(dp + shards - k, shards) for k in range(1, shards)]
    partners = (mate, over, corner)
    greet(peers + list(partners))
    mine = pl.ds(pl.multiple_of(core * half, half), half)
    theirs = pl.ds(pl.multiple_of((1 - core) * half, half), half)
    sent_images = pl.ds(0, SENT)

    for k, peer in enumerate(peers):
        remote(attn.at[mine], attnw.at[dp, mine], attn_send.at[k], attn_recv.at[dp], peer).start()
        remote(vec, vslots.at[dp], vec_send.at[k], vec_recv.at[dp], peer).start()
    for k, partner in enumerate(partners):
        remote(route, route_all.at[me], table_send.at[k, 0], table_recv.at[me, 0], partner).start()
        remote(comb, comb_all.at[me], table_send.at[k, 1], table_recv.at[me, 1], partner).start()

    def held(e, chain, at):
        column = x if chain == 0 else 1 - x
        return wfull.at[e, :, at * COLUMNS + column]

    def up(e, chain, hop, ref):
        return remote(ref, ref, up_send.at[e * 2 + chain, hop], up_recv.at[e * 2 + chain, hop], above)

    def down(e, chain, hop, ref):
        return remote(ref, ref, down_send.at[e * 2 + chain, hop], down_recv.at[e * 2 + chain, hop], below)

    def across(e, at, ref):
        return remote(ref, ref, x_send.at[e, at], x_recv.at[e, at], beside)

    def start_own(e):
        target = held(e, 0, z)
        remote(expw.at[e], target, x_send.at[e, z], x_recv.at[e, z], beside).start()

        @pl.when(z < last)
        def _():
            remote(expw.at[e], target, up_send.at[e * 2, 0], up_recv.at[e * 2, 0], above).start()

        @pl.when(z > 0)
        def _():
            remote(expw.at[e], target, down_send.at[e * 2, 0], down_recv.at[e * 2, 0], below).start()

    def start_other(e):
        ref = held(e, 1, z)
        across(e, z, ref).wait_recv()

        @pl.when(z < last)
        def _():
            up(e, 1, 0, ref).start()

        @pl.when(z > 0)
        def _():
            down(e, 1, 0, ref).start()

    def hand_on(e, chain, hop):
        cross = e not in ROUTE_FIRST
        from_below = jnp.maximum(z - 1 - hop, 0)
        from_above = jnp.minimum(z + 1 + hop, last)

        @pl.when(z - 1 - hop >= 0)
        def _():
            ref = held(e, chain, from_below)
            up(e, chain, hop, ref).wait_recv()

            @pl.when(z < last)
            def _():
                up(e, chain, hop + 1, ref).start()

            if cross:
                across(e, from_below, ref).start()

        @pl.when(z + 1 + hop <= last)
        def _():
            ref = held(e, chain, from_above)
            down(e, chain, hop, ref).wait_recv()

            @pl.when(z > 0)
            def _():
                down(e, chain, hop + 1, ref).start()

            if cross:
                across(e, from_above, ref).start()

    def weights_here(e):
        if e not in ROUTE_FIRST:
            for at in range(lines):
                across(e, at, held(e, 1, at)).wait_recv()

    def settle_weights(e):
        ref = held(e, 0, z)
        for chain in range(2 if e in ROUTE_FIRST else 1):
            for hop in range(last):
                @pl.when(jnp.logical_and(z - hop >= 0, z < last))
                def _():
                    up(e, chain, hop, ref).wait_send()

                @pl.when(jnp.logical_and(z + hop <= last, z > 0))
                def _():
                    down(e, chain, hop, ref).wait_send()

        if e in ROUTE_FIRST:
            across(e, z, ref).wait_send()
        else:
            for at in range(lines):
                across(e, at, ref).wait_send()

    start_own(0)
    start_own(1)
    g_own = cot.at[:, sent_images]
    g_mine = g_all.at[me]
    remote(g_own, g_mine, g_sem.at[0], g_sem.at[1], mate).start()
    remote(g_own, g_mine, g_sem.at[2], g_sem.at[3], over).start()
    own_copy = pltpu.make_async_copy(expw, wfull.at[:, :, dp], own_sem.at[0])
    own_copy.start()
    g_copy = pltpu.make_async_copy(g_own, g_mine, own_sem.at[1])
    g_copy.start()

    attnw[dp, mine] = attn[mine]
    vslots[dp] = vec[...]
    route_all[me] = route[...]
    comb_all[me] = comb[...]

    for k, partner in enumerate(partners):
        source = partner[1]
        remote(route, route_all.at[source], table_send.at[k, 0], table_recv.at[source, 0], partner).wait()
        remote(comb, comb_all.at[source], table_send.at[k, 1], table_recv.at[source, 1], partner).wait()
    for s in range(group):
        for el in range(local):
            named = me * local + el
            row = s * local + el
            hits = [route_all[s, t : t + 1, :] == named for t in range(TOP)]
            chosen[row : row + 1, :] = sum(jnp.where(h, 1.0, 0.0) for h in hits)
            shares[row : row + 1, :] = sum(
                jnp.where(h, comb_all[s, t : t + 1, :], 0.0) for t, h in enumerate(hits)
            )
    earlier = lax.broadcasted_iota(jnp.int32, (PAD, PAD), 0) < lax.broadcasted_iota(
        jnp.int32, (PAD, PAD), 1
    )
    earlier = jnp.where(earlier, 1.0, 0.0).astype(BF16)
    count = jnp.zeros((group * local, 1), F32)
    for i in range(images):
        block = chosen[:, i * PAD : (i + 1) * PAD]
        position = count + dot(block.astype(BF16), earlier)
        place[:, i * PAD : (i + 1) * PAD] = jnp.where(block > 0.0, position, -1.0).astype(jnp.int32)
        count = count + jnp.sum(block, axis=1, keepdims=True)

    for k, (peer, source) in enumerate(zip(peers, sources)):
        remote(attn.at[mine], attnw.at[source, mine], attn_send.at[k], attn_recv.at[source], peer).wait()
        remote(vec, vslots.at[source], vec_send.at[k], vec_recv.at[source], peer).wait()
    to_mate = remote(attnw.at[:, mine], attnw.at[:, mine], pass_sem.at[0], pass_sem.at[1], mate)
    to_mate.start()
    lane = lax.broadcasted_iota(jnp.int32, (128, D), 1)
    entry = lax.broadcasted_iota(jnp.int32, (128, D), 0)
    width = D // shards
    vectors = jnp.zeros((8, D), F32)
    for d in range(shards):
        spread = jnp.where(jnp.logical_and(entry < width, lane == entry + d * width), 1.0, 0.0)
        vectors = vectors + dot(vslots[d].astype(BF16), spread.astype(BF16))
    gain_one, shift_one = vectors[0:1], vectors[1:2]
    gain_two, shift_two, shift_out = vectors[2:3], vectors[3:4], vectors[4:5]
    remote(attnw.at[:, theirs], attnw.at[:, theirs], pass_sem.at[0], pass_sem.at[1], mate).wait_recv()
    pair_lane = lax.broadcasted_iota(jnp.int32, (PAD, 2 * HEAD_DIM), 1)

    def u_part(s, i):
        return u_all.at[s, i]

    def u_to(k, s, i, partner):
        return remote(u_part(s, i), u_part(s, i), u_send.at[i, k], u_recv.at[i, k], partner)

    def forward(tok_v, qkv_v, att_v, mid_v, u_v):
        fetch = pltpu.make_async_copy(tok, tok_v, in_sem.at[0])
        fetch.start()
        fetch.wait()

        def outs(i):
            return (
                pltpu.make_async_copy(u_v.at[i, sent_images], u_all.at[me, i], out_sem.at[i, 0]),
                pltpu.make_async_copy(qkv_v.at[i], qkv.at[i], out_sem.at[i, 1]),
                pltpu.make_async_copy(att_v.at[i], att.at[i], out_sem.at[i, 2]),
                pltpu.make_async_copy(mid_v.at[i], middle.at[i], out_sem.at[i, 3]),
            )

        def send_image(i):
            outs(i)[0].wait()
            u_to(0, me, i, over).start()
            u_to(1, me, i, mate).start()

        def one_image(i, carry):
            inputs = tok_v[i].astype(F32)
            normed, _ = normalize(inputs)
            lowered = (normed * gain_one + shift_one).astype(BF16)
            for part in range(3):
                columns = pl.ds(part * D, D)
                qkv_v[i, :, columns] = dot(lowered, attnw[:, :, columns].reshape(D, D)).astype(BF16)
            for pair in range(HEADS // 2):
                offset = pair * 2 * HEAD_DIM
                query = qkv_v[i, :, offset : offset + 128]
                key_rows = qkv_v[i, :, D + offset : D + offset + 128]
                value = qkv_v[i, :, 2 * D + offset : 2 * D + offset + 128]
                results = []
                for which in range(2):
                    probs = softmax_rows(query, key_rows, which, pair_lane)
                    results.append(dot(probs.astype(BF16), value))
                joined = jnp.where(pair_lane < HEAD_DIM, results[0], results[1])
                att_v[i, :, offset : offset + 128] = joined.astype(BF16)
            mid = inputs + dot(att_v[i], attnw[:, :, 3 * D :].reshape(D, D)) + shift_out
            mid_v[i] = mid
            normed_two, _ = normalize(mid)
            u_v[i] = (normed_two * gain_two + shift_two).astype(BF16)
            for copy in outs(i):
                copy.start()

            @pl.when(i > 0)
            def _():
                send_image(i - 1)

            for turn, actions in enumerate((
                (lambda: start_other(1), lambda: start_own(2)),
                (lambda: hand_on(0, 0, 1),),
                (lambda: hand_on(1, 0, 0),),
                (lambda: hand_on(0, 0, 2),),
                (lambda: hand_on(1, 1, 0), lambda: start_own(3)),
            )):
                @pl.when(i == turn)
                def _():
                    for action in actions:
                        action()

            return carry

        hand_on(0, 0, 0)
        lax.fori_loop(0, images, one_image, 0)
        send_image(images - 1)
        for i in range(images):
            for copy in outs(i)[1:]:
                copy.wait()

    pl.run_scoped(
        forward,
        pltpu.VMEM((images, PAD, D), BF16),
        pltpu.VMEM((images, PAD, 3 * D), BF16),
        pltpu.VMEM((images, PAD, D), BF16),
        pltpu.VMEM((images, PAD, D), F32),
        pltpu.VMEM((images, PAD, D), BF16),
    )
    g_over = g_all.at[over_s]
    remote(g_over, g_over, g_sem.at[2], g_sem.at[3], over).wait()
    remote(g_over, g_over, g_sem.at[4], g_sem.at[5], mate).start()
    g_mate = g_all.at[mate_s]
    remote(g_mate, g_mate, g_sem.at[0], g_sem.at[1], mate).wait()
    g_corner = g_all.at[corner_s]
    remote(g_corner, g_corner, g_sem.at[4], g_sem.at[5], mate).wait()
    g_copy.wait()
    own_copy.wait()

    def slot_of(e):
        return e % 2 if e < local - 1 else 2

    def cross_sum(e, k):
        return remote(
            gst.at[slot_of(e), k, pl.ds(lines, lines)], xr.at[e // 2, k],
            rx_send.at[e // 2, k], rx_recv.at[e // 2, k], beside,
        )

    def swap(e, k):
        return remote(xst.at[k], xo.at[e // 2, k], ro_send.at[e // 2, k], ro_recv.at[e // 2, k], beside)

    def partial(e, k, owner, which):
        value = gst[slot_of(e), k, which * lines + owner].astype(F32)
        if e not in SUM_FIRST:
            value = value + xr[e // 2, k, owner].astype(F32)
        return value

    def z_send(e, k, way, hop):
        sent, landed = zs.at[k, way], zr.at[k, way, hop]
        if e not in SUM_FIRST:
            sent, landed = sent.at[0], landed.at[0]
        if way == 0:
            return remote(sent, landed, ru_send.at[k], ru_recv.at[k, hop], above)
        return remote(sent, landed, rd_send.at[k], rd_recv.at[k, hop], below)

    def one_hop(e, k, hop, way):
        ahead = z if way == 0 else last - z
        owner = jnp.minimum(z + last - hop, last) if way == 0 else jnp.maximum(z - last + hop, 0)
        credit = (credit_up, credit_down)[way]
        both = range(2 if e in SUM_FIRST else 1)

        @pl.when(jnp.logical_and(ahead <= hop, ahead < last))
        def _():
            if hop > 0:
                @pl.when(ahead <= hop - 1)
                def _():
                    z_send(e, k, way, hop - 1).wait_send()

            if CHAINS.index(e) > 0:
                @pl.when(ahead == hop)
                def _():
                    pl.semaphore_wait(credit.at[k], 1)

            if hop > 0:
                @pl.when(ahead >= 1)
                def _():
                    z_send(e, k, way, hop - 1).wait_recv()
                    for which in both:
                        total = partial(e, k, owner, which) + zr[k, way, hop - 1, which].astype(F32)
                        zs[k, way, which] = total.astype(BF16)

                @pl.when(ahead < 1)
                def _():
                    for which in both:
                        zs[k, way, which] = partial(e, k, owner, which).astype(BF16)
            else:
                for which in both:
                    zs[k, way, which] = partial(e, k, owner, which).astype(BF16)
            z_send(e, k, way, hop).start()

    def hop_step(e, k, hop):
        if hop == 0 and e not in SUM_FIRST:
            cross_sum(e, k).wait_recv()
        one_hop(e, k, hop, 0)
        one_hop(e, k, hop, 1)

    def to_result(e, k):
        return pltpu.make_async_copy(fin.at[k], grads.at[e, k], fin_sem.at[k])

    def finish(e, k):
        turn = CHAINS.index(e)
        if turn > 0:
            to_result(e, k).wait()
        fin[k] = partial(e, k, z, 0)

        @pl.when(z > 0)
        def _():
            z_send(e, k, 0, last - 1).wait_recv()
            fin[k] += zr[k, 0, last - 1, 0].astype(F32)
            z_send(e, k, 1, last - 1).wait_send()

        @pl.when(z < last)
        def _():
            z_send(e, k, 1, last - 1).wait_recv()
            fin[k] += zr[k, 1, last - 1, 0].astype(F32)
            z_send(e, k, 0, last - 1).wait_send()

        if e in SUM_FIRST:
            own = partial(e, k, z, 1)

            @pl.when(z == 0)
            def _():
                xst[k] = (own + zr[k, 1, last - 1, 1].astype(F32)).astype(BF16)

            @pl.when(z == last)
            def _():
                xst[k] = (own + zr[k, 0, last - 1, 1].astype(F32)).astype(BF16)

            @pl.when(jnp.logical_and(z > 0, z < last))
            def _():
                arrived = zr[k, 0, last - 1, 1].astype(F32) + zr[k, 1, last - 1, 1].astype(F32)
                xst[k] = (own + arrived).astype(BF16)

            swap(e, k).start()
        else:
            to_result(e, k).start()
        if turn + 1 < local:
            @pl.when(z > 0)
            def _():
                pl.semaphore_signal(credit_up.at[k], inc=1, device_id=below, device_id_type=MESH)

            @pl.when(z < last)
            def _():
                pl.semaphore_signal(credit_down.at[k], inc=1, device_id=above, device_id_type=MESH)

    def collect(e, k):
        swap(e, k).wait()
        fin[k] += xo[e // 2, k].astype(F32)
        to_result(e, k).start()

    def source_of(e, t):
        r = t if e == local - 1 else group - 1 - t
        across_y = (1 - y) + (r // CORES) * (2 * y - 1)
        return across_y * CORES + (1 - core) + (r % CORES) * (2 * core - 1)

    def experts(ubuf, gbuf, work, x_t, m_t, dacc, made_all, d_stage):
        def load(s):
            return (
                pltpu.make_async_copy(u_all.at[s], ubuf.at[:, sent_images], load_sem.at[0]),
                pltpu.make_async_copy(g_all.at[s], gbuf.at[:, sent_images], load_sem.at[1]),
            )

        def load_weights(e):
            return pltpu.make_async_copy(wfull.at[e], gst.at[2], w_sem)

        def weight_grad(e, k):
            left = x_t if k == 0 else m_t

            def one_tile(j, carry):
                right = work[tiles * (1 - k) + j]
                block = dot(left[...], right).astype(BF16)
                columns = pl.ds(pl.multiple_of(j * tile, tile), tile)
                for d in range(shards):
                    which = lax.rem(x + d % COLUMNS, COLUMNS)
                    index = which * lines + d // COLUMNS
                    gst[slot_of(e), k, index, :, columns] = block[d * rows : (d + 1) * rows]
                return carry

            lax.fori_loop(0, tiles, one_tile, 0)
            if e not in SUM_FIRST:
                cross_sum(e, k).start()

        def pick_of(s, e, i):
            slot_row = lax.broadcasted_iota(jnp.int32, (slots, PAD), 0)
            return slot_row == place[pl.ds(s * local + e, 1), i * PAD : (i + 1) * PAD]

        def one_source(e, t, after_gather):
            s = source_of(e, t)
            for copy in load(s):
                copy.wait()
            arrived = jnp.zeros((slots, D), F32)
            grad = jnp.zeros((slots, D), F32)
            share = jnp.zeros((slots, 1), F32)
            for i in range(images):
                hit = pick_of(s, e, i)
                pick = jnp.where(hit, 1.0, 0.0).astype(BF16)
                weight = shares[pl.ds(s * local + e, 1), i * PAD : (i + 1) * PAD]
                share += jnp.sum(jnp.where(hit, weight, 0.0), axis=1, keepdims=True)
                arrived += dot(pick, ubuf[i])
                grad += dot(pick, gbuf[i])
            arrived = arrived.astype(BF16)
            grad = (share * grad).astype(BF16)
            here = pl.ds(pl.multiple_of(t * slots, slots), slots)
            x_t[:, here] = arrived.T
            m_t[:, here] = grad.T
            after_gather()

            def one_tile(j, carry):
                columns = pl.ds(pl.multiple_of(j * tile, tile), tile)
                preact = dot(arrived, gst[2, 0, :, :, columns].reshape(D, tile))
                hidden, slope = gelu_parts(preact)
                work[j, here, :] = hidden.astype(BF16)
                grad_hidden = dot(grad, gst[2, 1, :, :, columns].reshape(D, tile))
                work[tiles + j, here, :] = (grad_hidden * slope).astype(BF16)
                return carry

            lax.fori_loop(0, tiles, one_tile, 0)
            made = jnp.zeros((slots, D), F32)
            back = jnp.zeros((slots, D), F32)
            for j in range(tiles):
                columns = pl.ds(j * tile, tile)
                made += contract_last(work[j, here, :], gst[2, 1, :, :, columns].reshape(D, tile))
                back += contract_last(work[tiles + j, here, :], gst[2, 0, :, :, columns].reshape(D, tile))
            made_all[s, e * slots : (e + 1) * slots] = (share * made.astype(BF16).astype(F32)).astype(BF16)
            back = back.astype(BF16)
            for i in range(images):
                pick = jnp.where(pick_of(s, e, i), 1.0, 0.0).astype(BF16)
                placed = contract_rows(pick, back)[:SENT]
                if e == 0:
                    dacc[s, i * SENT : (i + 1) * SENT] = placed
                else:
                    dacc[s, i * SENT : (i + 1) * SENT] += placed

        def next_load(e, t):
            @pl.when(t + 1 < group)
            def _():
                if e == 0:
                    @pl.when(t == 0)
                    def _():
                        for i in range(images):
                            u_to(1, mate_s, i, mate).wait()

                    @pl.when(t == 1)
                    def _():
                        for i in range(images):
                            u_to(0, over_s, i, over).wait()
                            u_to(2, over_s, i, mate).start()

                    @pl.when(t == 2)
                    def _():
                        for i in range(images):
                            u_to(2, corner_s, i, mate).wait()

                for copy in load(source_of(e, t + 1)):
                    copy.start()

            if e + 1 < local:
                @pl.when(t + 1 == group)
                def _():
                    for copy in load(source_of(e + 1, 0)):
                        copy.start()

        def to_corner():
            return remote(d_stage.at[0], d_corner, back_send.at[0], back_recv.at[0], mate)

        def to_mate_sum():
            return remote(d_stage.at[1], d_mate, back_send.at[1], back_recv.at[1], mate)

        def to_over():
            return remote(d_stage.at[2], d_over, back_send.at[2], back_recv.at[2], over)

        def sums_corner():
            d_stage[0] = dacc[corner_s].astype(BF16)
            to_corner().start()

        def sums_mate():
            d_stage[1] = dacc[mate_s].astype(BF16)
            to_mate_sum().start()
            to_corner().wait_recv()
            landed = pltpu.make_async_copy(d_corner, d_stage.at[2], load_sem.at[2])
            landed.start()
            landed.wait()
            d_stage[2] = (dacc[over_s] + d_stage[2].astype(F32)).astype(BF16)
            to_over().start()

        plan = {
            (0, 0): (lambda: hand_on(1, 0, 1),),
            (0, 2): (lambda: hand_on(1, 1, 1),),
            (1, 0): (lambda: hand_on(2, 0, 1), lambda: hop_step(0, 1, 1)),
            (1, 1): (lambda: hop_step(0, 0, 2),),
            (1, 2): (lambda: hand_on(2, 0, 2),),
            (1, 3): (lambda: hop_step(0, 1, 2),),
            (2, 0): (lambda: hand_on(3, 0, 1), lambda: collect(0, 0)),
            (2, 1): (lambda: collect(0, 1),),
            (2, 2): (lambda: hand_on(3, 0, 2),),
            (3, 0): (sums_corner, lambda: hop_step(2, 0, 1)),
            (3, 1): (lambda: hop_step(2, 1, 1),),
            (3, 2): (sums_mate, lambda: hop_step(2, 0, 2)),
            (3, 3): (lambda: hop_step(2, 1, 2),),
        }
        after_grad = {
            (0, 0): (lambda: hop_step(0, 0, 0),),
            (0, 1): (lambda: hop_step(0, 1, 0), lambda: hand_on(1, 0, 2), lambda: hand_on(1, 1, 2),
                     lambda: hand_on(2, 0, 0), lambda: hop_step(0, 0, 1)),
            (1, 0): (lambda: finish(0, 0),),
            (1, 1): (lambda: finish(0, 1), lambda: hand_on(3, 0, 0)),
            (2, 0): (lambda: hop_step(2, 0, 0),),
            (2, 1): (lambda: hop_step(2, 1, 0),),
            (3, 0): (lambda: finish(2, 0),),
            (3, 1): (lambda: finish(2, 1),),
        }

        empty = jnp.zeros((images, PAD - SENT, D), BF16)
        ubuf[:, SENT:, :] = empty
        gbuf[:, SENT:, :] = empty
        for copy in load(source_of(0, 0)):
            copy.start()
        for e in range(local):
            weights_here(e)
            load_weights(e).start()
            load_weights(e).wait()

            def step(t, carry, e=e):
                one_source(e, t, lambda: next_load(e, t))
                for turn in range(group):
                    actions = plan.get((e, turn), ())
                    if actions:
                        @pl.when(t == turn)
                        def _():
                            for action in actions:
                                action()

                return carry

            lax.fori_loop(0, group, step, 0)
            for k in range(2):
                weight_grad(e, k)
                for action in after_grad.get((e, k), ()):
                    action()

        pltpu.make_async_copy(dacc.at[me], own_out.at[0], own_sem.at[2]).start()

        def one_sum(s, i):
            total = jnp.zeros((PAD, D), F32)
            for e in range(local):
                pick = jnp.where(pick_of(s, e, i), 1.0, 0.0).astype(BF16)
                total += contract_rows(pick, made_all[s, e * slots : (e + 1) * slots])
            return total[:SENT]

        def stage(k):
            return pltpu.make_async_copy(d_stage.at[k], y_stage.at[k], own_sem.at[3])

        for k, (s, partner) in enumerate(zip((mate_s, over_s, corner_s), partners)):
            (to_corner, to_mate_sum, to_over)[k]().wait_send()
            for i in range(images):
                d_stage[k, i * SENT : (i + 1) * SENT] = one_sum(s, i).astype(BF16)
            stage(k).start()
            stage(k).wait()
            remote(y_stage.at[k], y_got.at[k], y_send.at[k], y_recv.at[k], partner).start()
        for i in range(images):
            dacc[corner_s, i * SENT : (i + 1) * SENT] = one_sum(me, i)
        pltpu.make_async_copy(dacc.at[corner_s], own_out.at[1], own_sem.at[4]).start()
        pltpu.make_async_copy(dacc.at[corner_s], own_out.at[1], own_sem.at[4]).wait()
        pltpu.make_async_copy(dacc.at[me], own_out.at[0], own_sem.at[2]).wait()

    count_rows = images * SENT
    pl.run_scoped(
        experts,
        pltpu.VMEM((images, PAD, D), BF16),
        pltpu.VMEM((images, PAD, D), BF16),
        pltpu.VMEM((2 * tiles, group * slots, tile), BF16),
        pltpu.VMEM((D, group * slots), BF16),
        pltpu.VMEM((D, group * slots), BF16),
        pltpu.VMEM((group, count_rows, D), F32),
        pltpu.VMEM((group, local * slots, D), BF16),
        pltpu.VMEM((3, count_rows, D), BF16),
    )
    remote(d_mate, d_mate, back_send.at[1], back_recv.at[1], mate).wait_recv()
    remote(d_over, d_over, back_send.at[2], back_recv.at[2], over).wait_recv()

    def rows_of(start, size):
        return pl.ds(pl.multiple_of(start, quarter), size)

    kept_y, given_y = rows_of(y * quarter, quarter), rows_of((1 - y) * quarter, quarter)
    final_rows = rows_of(core * half + y * quarter, quarter)

    def backward(g_low, g_mid, d_att, v_fetch):
        v_sum[...] = jnp.zeros_like(v_sum)

        def before_attention(cot_v, mid_v, own_v, mate_v, over_v):
            fetches = [
                pltpu.make_async_copy(source, target, in_sem.at[n])
                for n, (source, target) in enumerate((
                    (cot, cot_v), (middle, mid_v), (own_out.at[0], own_v), (d_mate, mate_v), (d_over, over_v),
                ))
            ]
            for fetch in fetches:
                fetch.start()
            for fetch in fetches:
                fetch.wait()

            def one_image(i, carry):
                here = pl.ds(pl.multiple_of(i * SENT, SENT), SENT)
                normed, inverse = normalize(mid_v[i])
                grad = own_v[here] + mate_v[here].astype(F32) + over_v[here].astype(F32)
                grad = jnp.concatenate([grad, jnp.zeros((PAD - SENT, D), F32)], axis=0)
                v_sum[2:3] += jnp.sum(grad * normed, axis=0, keepdims=True)
                v_sum[3:4] += jnp.sum(grad, axis=0, keepdims=True)
                total = cot_v[i].astype(F32) + norm_back(grad * gain_two, normed, inverse)
                v_sum[4:5] += jnp.sum(total, axis=0, keepdims=True)
                g_mid[i] = total
                low = total.astype(BF16)
                g_low[i] = low
                d_att[i] = contract_last(low, attnw[:, :, 3 * D :].reshape(D, D)).astype(BF16)
                return carry

            lax.fori_loop(0, images, one_image, 0)

        pl.run_scoped(
            before_attention,
            pltpu.VMEM((images, PAD, D), BF16),
            pltpu.VMEM((images, PAD, D), F32),
            pltpu.VMEM((count_rows, D), F32),
            pltpu.VMEM((count_rows, D), BF16),
            pltpu.VMEM((count_rows, D), BF16),
        )

        def through_attention(
            tok_v, qkv_v, att_v, dqkv, lowered, part_own, sum_a, sum_b, sum_c, sum_d, gt_v, old_v, new_v
        ):
            def move_a(p):
                return remote(part_own.at[p, :, theirs], part_a.at[p], a_sem.at[p, 0], a_sem.at[p, 1], mate)

            def move_b(p):
                return remote(sum_a.at[p, :, given_y], part_b.at[p], b_sem.at[p, 0], b_sem.at[p, 1], over)

            def move_c(p):
                return remote(sum_b.at[p, :, 1 - x], part_c.at[p], c_sem.at[p, 0], c_sem.at[p, 1], beside)

            def move_d(p, k):
                target = lax.rem(z + k, lines)
                return remote(
                    sum_c.at[p, target], part_d.at[p, z], d_send.at[p, k - 1], d_recv.at[p, z], along[k - 1]
                )

            def arrived_d(p, k):
                source = lax.rem(z + lines - k, lines)
                return remote(
                    sum_c.at[p, source], part_d.at[p, source], d_send.at[p, k - 1], d_recv.at[p, source],
                    along[k - 1],
                )

            def move_e(p, k):
                own = whole.at[final_rows, pl.ds(p * D, D)]
                return remote(own, own, e_send.at[p, k], e_recv.at[p, k], partners[k])

            def stage_b(p):
                move_a(p).wait()
                sum_a[p] = (part_own[p, :, mine].astype(F32) + part_a[p].astype(F32)).astype(BF16)
                move_b(p).start()

            def stage_c(p):
                move_b(p).wait()
                total = sum_a[p, :, kept_y].astype(F32) + part_b[p].astype(F32)
                sum_b[p] = total.astype(BF16).reshape(lines, COLUMNS, quarter, D)
                move_c(p).start()

            def stage_d(p):
                move_c(p).wait()
                total = sum_b[p, :, x].astype(F32) + part_c[p].astype(F32)
                sum_c[p] = total.astype(BF16)
                sum_d[p] = total
                for k in range(1, lines):
                    move_d(p, k).start()

            def stage_e(p):
                total = sum_d[p, z]
                for k in range(1, lines):
                    arrived_d(p, k).wait_recv()
                    total = total + part_d[p, lax.rem(z + lines - k, lines)].astype(F32)
                whole[final_rows, pl.ds(p * D, D)] = total
                for k in range(3):
                    move_e(p, k).start()

            def settle(p):
                for k in range(1, lines):
                    move_d(p, k).wait_send()
                for k in range(3):
                    move_e(p, k).wait()

            def scatter_part(p, left, right):
                block = contract_rows(left, right).astype(BF16)
                part_own[p] = block.reshape(shards, rows, D)
                move_a(p).start()

            fetches = [
                pltpu.make_async_copy(source, target, in_sem.at[n])
                for n, (source, target) in enumerate((
                    (tok, tok_v), (qkv, qkv_v), (att, att_v),
                    (attn_old, old_v.at[0]), (first_old, old_v.at[1]), (second_old, old_v.at[2]),
                ))
            ]
            for fetch in fetches:
                fetch.start()
            for fetch in fetches:
                fetch.wait()
            scatter_part(3, att_v[...].reshape(images * PAD, D), g_low[...].reshape(images * PAD, D))

            def result(i):
                return pltpu.make_async_copy(gt_v.at[i], grad_tok.at[i], out_sem.at[i, 0])

            def one_image(i, carry):
                for pair in range(HEADS // 2):
                    offset = pair * 2 * HEAD_DIM
                    query = qkv_v[i, :, offset : offset + 128]
                    key_rows = qkv_v[i, :, D + offset : D + offset + 128]
                    value = qkv_v[i, :, 2 * D + offset : 2 * D + offset + 128]
                    grad = d_att[i, :, offset : offset + 128]
                    results = []
                    for which in range(2):
                        probs = softmax_rows(query, key_rows, which, pair_lane)
                        grad_own = jnp.where(pair_lane // HEAD_DIM == which, grad, jnp.zeros_like(grad))
                        grad_probs = contract_last(grad_own, value)
                        inner = jnp.sum(probs * grad_probs, axis=-1, keepdims=True)
                        grad_scores = (probs * (grad_probs - inner)).astype(BF16)
                        results.append((
                            dot(grad_scores, key_rows) * HEAD_DIM ** (-0.5),
                            contract_rows(grad_scores, query) * HEAD_DIM ** (-0.5),
                            contract_rows(probs.astype(BF16), grad),
                        ))
                    for part in range(3):
                        joined = jnp.where(pair_lane < HEAD_DIM, results[0][part], results[1][part])
                        dqkv[i, :, part * D + offset : part * D + offset + 128] = joined.astype(BF16)
                grad = jnp.zeros((PAD, D), F32)
                for part in range(3):
                    columns = pl.ds(part * D, D)
                    grad += contract_last(dqkv[i, :, columns], attnw[:, :, columns].reshape(D, D))
                normed, inverse = normalize(tok_v[i].astype(F32))
                lowered[i] = (normed * gain_one + shift_one).astype(BF16)
                v_sum[0:1] += jnp.sum(grad * normed, axis=0, keepdims=True)
                v_sum[1:2] += jnp.sum(grad, axis=0, keepdims=True)
                gt_v[i] = (g_mid[i] + norm_back(grad * gain_one, normed, inverse)).astype(BF16)
                result(i).start()
                for turn, actions in enumerate((
                    (lambda: stage_b(3), lambda: collect(2, 0), lambda: collect(2, 1), lambda: hop_step(1, 0, 0)),
                    (lambda: stage_c(3), lambda: hop_step(1, 1, 0), lambda: hop_step(1, 0, 1)),
                    (lambda: stage_d(3), lambda: hop_step(1, 1, 1), lambda: hop_step(1, 0, 2)),
                    (lambda: stage_e(3), lambda: hop_step(1, 1, 2), lambda: finish(1, 0)),
                    (lambda: finish(1, 1), lambda: hop_step(3, 0, 0)),
                )):
                    @pl.when(i == turn)
                    def _():
                        for action in actions:
                            action()

                return carry

            lax.fori_loop(0, images, one_image, 0)

            def v_move(n, partner):
                return remote(v_stage.at[n], v_got.at[n], v_sem.at[n, 0], v_sem.at[n, 1], partner)

            v_stage[0] = v_sum[...]
            v_move(0, mate).start()
            for p in range(3):
                scatter_part(
                    p, lowered[...].reshape(images * PAD, D),
                    dqkv[:, :, p * D : (p + 1) * D].reshape(images * PAD, D),
                )
            tail = {
                0: (lambda: hop_step(3, 0, 1),),
                1: (lambda: hop_step(3, 1, 0), lambda: hop_step(3, 0, 2)),
                2: (lambda: hop_step(3, 1, 1), lambda: finish(3, 0)),
            }
            for n, stage in enumerate((stage_b, stage_c, stage_d)):
                for p in range(3):
                    stage(p)
                v_move(n, (mate, over, beside)[n]).wait()
                total = v_stage[n] + v_got[n]
                if n < 2:
                    v_stage[n + 1] = total
                    v_move(n + 1, (over, beside)[n]).start()
                else:
                    v_lines[z] = total
                    for k in range(1, lines):
                        remote(
                            v_lines.at[z], v_lines.at[z], vd_send.at[k - 1], vd_recv.at[z], along[k - 1]
                        ).start()
                for action in tail[n]:
                    action()
            for p in range(3):
                stage_e(p)
            hop_step(3, 1, 2)
            for k in range(1, lines):
                source = lax.rem(z + lines - k, lines)
                remote(
                    v_lines.at[source], v_lines.at[source], vd_send.at[k - 1], vd_recv.at[source], along[k - 1]
                ).wait()
            total = v_lines[0]
            for n in range(1, lines):
                total = total + v_lines[n]
            for d in range(shards):
                @pl.when(dp == d)
                def _():
                    gradient = total[: vec_old.shape[0], d * width : (d + 1) * width]
                    new = adam_update(
                        vec_old[...], vec_first_old[...], vec_second_old[...], gradient, 0.2, 0.0
                    )
                    vec_new[...], vec_first_new[...], vec_second_new[...] = new

            for p in (3, 0, 1, 2):
                settle(p)
            for p in range(4):
                columns = pl.ds(p * D, D)
                new = adam_update(
                    old_v[0, :, columns], old_v[1, :, columns], old_v[2, :, columns], whole[:, columns],
                    0.03, 0.1,
                )
                for n in range(3):
                    new_v[n, :, columns] = new[n]
            results = [
                pltpu.make_async_copy(new_v.at[n], target, in_sem.at[n])
                for n, target in enumerate((attn_new, first_new, second_new))
            ]
            for copy in results:
                copy.start()
            for copy in results:
                copy.wait()
            for i in range(images):
                result(i).wait()

        pl.run_scoped(
            through_attention,
            pltpu.VMEM((images, PAD, D), BF16),
            pltpu.VMEM((images, PAD, 3 * D), BF16),
            pltpu.VMEM((images, PAD, D), BF16),
            pltpu.VMEM((images, PAD, 3 * D), BF16),
            pltpu.VMEM((images, PAD, D), BF16),
            pltpu.VMEM((4, shards, rows, D), BF16),
            pltpu.VMEM((4, shards, half, D), BF16),
            pltpu.VMEM((4, lines, COLUMNS, quarter, D), BF16),
            pltpu.VMEM((4, lines, quarter, D), BF16),
            pltpu.VMEM((4, lines, quarter, D), F32),
            pltpu.VMEM((images, PAD, D), BF16),
            pltpu.VMEM((3, rows, 4 * D), F32),
            pltpu.VMEM((3, rows, 4 * D), F32),
        )

    pl.run_scoped(
        backward,
        pltpu.VMEM((images, PAD, D), BF16),
        pltpu.VMEM((images, PAD, D), F32),
        pltpu.VMEM((images, PAD, D), BF16),
        pltpu.VMEM((8, 128), F32),
    )

    def output(mid_v, own_v, got_v, out_v):
        for k, partner in enumerate(partners):
            remote(y_stage.at[k], y_got.at[k], y_send.at[k], y_recv.at[k], partner).wait()
        fetches = [
            pltpu.make_async_copy(source, target, in_sem.at[n])
            for n, (source, target) in enumerate(((middle, mid_v), (own_out.at[1], own_v), (y_got, got_v)))
        ]
        for fetch in fetches:
            fetch.start()
        for fetch in fetches:
            fetch.wait()
        for i in range(images):
            here = pl.ds(i * SENT, SENT)
            returned = own_v[here]
            for k in range(3):
                returned = returned + got_v[k, here].astype(F32)
            out_v[i, :SENT] = (mid_v[i, :SENT] + returned).astype(BF16)
        copy = pltpu.make_async_copy(out_v, mixed, in_sem.at[3])
        copy.start()
        copy.wait()

    pl.run_scoped(
        output,
        pltpu.VMEM((images, PAD, D), F32),
        pltpu.VMEM((count_rows, D), F32),
        pltpu.VMEM((3, count_rows, D), BF16),
        pltpu.VMEM((images, PAD, D), BF16),
    )
    finish(3, 1)
    to_mate.wait_send()
    for e in range(local):
        settle_weights(e)
        if e not in SUM_FIRST:
            for k in range(2):
                cross_sum(e, k).wait_send()
    for k in range(2):
        to_result(3, k).wait()


def block(shards, capacity, route, comb, attn, vec, tok, cot, expw, attn_state, vec_state, group):
    lines = shards // COLUMNS
    images = tok.shape[0]
    local, _, rows, ff = expw.shape
    slots = -(-capacity // 128) * 128
    half, quarter = rows // 2, rows // 4
    wide = images * PAD
    count_rows = images * SENT
    dma = pltpu.SemaphoreType.DMA
    regular = pltpu.SemaphoreType.REGULAR
    vm = pl.BlockSpec(memory_space=pltpu.VMEM)
    hbm = pl.BlockSpec(memory_space=pl.ANY)
    shape = jax.ShapeDtypeStruct
    states = [shape(a.shape, F32) for a in vec_state]
    attn_states = [shape(a.shape, F32) for a in attn_state]
    last = lines - 1
    outs = pl.pallas_call(
        functools.partial(block_kernel, shards, lines, slots),
        out_shape=states + [
            shape((group, images, SENT, D), BF16),
            shape((group, images, SENT, D), BF16),
            shape((local, 2, shards, rows, ff), BF16),
            shape((images, PAD, D), F32),
            shape((images, PAD, 3 * D), BF16),
            shape((images, PAD, D), BF16),
            shape((2, count_rows, D), F32),
            shape((count_rows, D), BF16),
            shape((count_rows, D), BF16),
            shape((count_rows, D), BF16),
            shape((3, count_rows, D), BF16),
            shape((3, count_rows, D), BF16),
            shape((local, 2, rows, ff), F32),
            shape((images, PAD, D), BF16),
            shape((images, PAD, D), BF16),
        ] + attn_states,
        in_specs=[vm] * 7 + [hbm] * 6,
        out_specs=[vm] * 3 + [hbm] * 18,
        scratch_shapes=[
            pltpu.VMEM((shards,) + attn.shape, BF16),
            pltpu.VMEM((group, 8, wide), jnp.int32),
            pltpu.VMEM((group, 8, wide), F32),
            pltpu.VMEM((shards, 8, 128), F32),
            pltpu.VMEM((group * local, wide), F32),
            pltpu.VMEM((group * local, wide), jnp.int32),
            pltpu.VMEM((group * local, wide), F32),
            pltpu.VMEM((3, 2, shards, rows, ff), BF16),
            pltpu.VMEM((2, 2, lines, rows, ff), BF16),
            pltpu.VMEM((2, 2, rows, ff), BF16),
            pltpu.VMEM((2, rows, ff), BF16),
            pltpu.VMEM((2, 2, last, 2, rows, ff), BF16),
            pltpu.VMEM((2, 2, 2, rows, ff), BF16),
            pltpu.VMEM((2, rows, ff), F32),
            pltpu.VMEM((4, shards, half, D), BF16),
            pltpu.VMEM((4, shards, quarter, D), BF16),
            pltpu.VMEM((4, lines, quarter, D), BF16),
            pltpu.VMEM((4, lines, quarter, D), BF16),
            pltpu.VMEM((rows, 4 * D), F32),
            pltpu.VMEM((8, D), F32),
            pltpu.VMEM((3, 8, D), F32),
            pltpu.VMEM((3, 8, D), F32),
            pltpu.VMEM((lines, 8, D), F32),
            dma((shards,)), dma((shards,)), dma((shards,)), dma((shards,)),
            dma((2,)), dma((3, 2)), dma((group, 2)),
            dma((6,)), dma((images, 3)), dma((images, 3)), dma((5,)),
            dma((2 * local, lines)), dma((2 * local, lines)), dma((2 * local, lines)), dma((2 * local, lines)),
            dma((local, lines)), dma((local, lines)),
            dma((images, 4)), dma((6,)), dma((3,)), dma(()), dma((2,)),
            dma((2, 2)), dma((2, 2)), dma((2, 2)), dma((2, 2)),
            dma((2,)), dma((2, last)), dma((2,)), dma((2, last)),
            regular((2,)), regular((2,)),
            dma((3,)), dma((3,)), dma((3,)), dma((3,)),
            dma((4, 2)), dma((4, 2)), dma((4, 2)), dma((4, last)), dma((4, lines)),
            dma((4, 3)), dma((4, 3)), dma((3, 2)), dma((last,)), dma((lines,)),
        ],
        compiler_params=pltpu.CompilerParams(
            collective_id=0, has_side_effects=True, vmem_limit_bytes=VMEM_LIMIT
        ),
    )(route, comb, attn, vec, *vec_state, tok, cot, expw, *attn_state)
    vec_new, grads, mixed, grad_tok, attn_new = outs[:3], outs[15], outs[16], outs[17], outs[18:]
    return mixed, grad_tok, grads, attn_new, vec_new


def by_image(rows):
    images = rows.shape[0] // SEQ
    return jnp.pad(rows.reshape((images, SEQ) + rows.shape[1:]), ((0, 0), (0, PAD - SEQ), (0, 0)))


def as_lanes(table, fill):
    images = table.shape[0] // SEQ
    wide = table.T.reshape(TOP, images, SEQ)
    wide = jnp.pad(wide, ((0, 8 - TOP), (0, 0), (0, PAD - SEQ)), constant_values=fill)
    return wide.reshape(8, images * PAD)


def to_tokens(rows, count):
    return rows[:, :SEQ].reshape(count, D)


def chip_body(shards, group):
    def run(
        tokens, cotangent, routes, combine, attn_master, attn_first, attn_second,
        vector_master, vector_first, vector_second, expert_master, expert_first, expert_second,
    ):
        count = tokens.shape[0]
        experts = expert_master.shape[2] * group
        capacity = max(2, 4 * count // experts)
        width = vector_master.shape[1]
        vec = jnp.pad(vector_master, ((0, 8 - vector_master.shape[0]), (0, 128 - width)))
        shard = jnp.transpose(expert_master.astype(BF16), (2, 1, 0, 3))
        mixed, grad_tokens, grads, attn_new, vec_new = block(
            shards, capacity, as_lanes(routes, -1), as_lanes(combine, 0.0), attn_master.astype(BF16), vec,
            by_image(tokens), by_image(cotangent), shard,
            [attn_master, attn_first, attn_second], [vector_master, vector_first, vector_second], group,
        )
        expert_new = adam_update(
            expert_master, expert_first, expert_second, jnp.transpose(grads, (2, 1, 0, 3)), 0.02, 0.1
        )
        return (to_tokens(mixed, count), to_tokens(grad_tokens, count), *attn_new, *vec_new, *expert_new)

    return run


def gelu_slope(preact):
    return (
        0.5 * (1.0 + lax.erf(preact * 0.7071067811865476))
        + preact * jnp.exp(-0.5 * preact * preact) * 0.3989422804014327
    )


def slot_places(routes, experts):
    flat_routes = routes.reshape(-1)
    onehot = (flat_routes[:, None] == jnp.arange(experts, dtype=jnp.int32)[None, :]).astype(
        jnp.int32
    )
    before = jnp.cumsum(onehot, axis=0) - onehot
    return jnp.sum(before * onehot, axis=1)


def general_body(
    tokens,
    cotangent,
    routes,
    combine,
    attn_master,
    attn_first,
    attn_second,
    vector_master,
    vector_first,
    vector_second,
    expert_master,
    expert_first,
    expert_second,
):
    group_size = lax.axis_size("expert")
    local_experts = expert_master.shape[2]
    experts = local_experts * group_size
    token_count = tokens.shape[0]
    capacity = max(2, 4 * token_count // experts)
    images = token_count // SEQ
    score_scale = HEAD_DIM ** (-0.5)
    attn_weight, vector_weight, expert_weight = (
        lax.all_gather(attn_master.astype(jnp.bfloat16), "dp", axis=0, tiled=True),
        lax.all_gather(vector_master.astype(jnp.bfloat16), "dp", axis=1, tiled=True),
        lax.all_gather(expert_master.astype(jnp.bfloat16), "dp", axis=0, tiled=True),
    )
    vectors = vector_weight.astype(jnp.float32)
    w_packed = attn_weight[:, : 3 * D]
    w_project = attn_weight[:, 3 * D :]
    inputs = tokens.astype(jnp.float32)
    normed_one, inverse_one = normalize(inputs)
    lowered_one = (normed_one * vectors[0] + vectors[1]).astype(jnp.bfloat16)
    packed = jnp.dot(lowered_one, w_packed, preferred_element_type=jnp.float32).astype(jnp.bfloat16)
    packed = packed.reshape(images, SEQ, 3, HEADS, HEAD_DIM)
    queries = packed[:, :, 0]
    keys_all = packed[:, :, 1]
    values_all = packed[:, :, 2]
    scores = (
        jnp.einsum("bqhc,bkhc->bhqk", queries, keys_all, preferred_element_type=jnp.float32)
        * score_scale
    )
    softmax_out = jax.nn.softmax(scores, axis=-1)
    softmax_low = softmax_out.astype(jnp.bfloat16)
    attended = jnp.einsum(
        "bhqk,bkhc->bqhc", softmax_low, values_all, preferred_element_type=jnp.float32
    )
    attended = attended.reshape(token_count, D).astype(jnp.bfloat16)
    middle = inputs + jnp.dot(attended, w_project, preferred_element_type=jnp.float32) + vectors[4]
    normed_two, inverse_two = normalize(middle)
    mixed_in = (normed_two * vectors[2] + vectors[3]).astype(jnp.bfloat16)
    slot_index = routes.reshape(-1) * capacity + slot_places(routes, experts)

    def dispatch(slot_rows):
        filled = jnp.zeros((experts * capacity, D), jnp.bfloat16).at[slot_index].set(slot_rows)
        return filled.reshape(group_size, local_experts, capacity, D)

    def collect(returned):
        picked = returned.reshape(experts * capacity, D)[slot_index]
        return picked.reshape(token_count, TOP, D).astype(jnp.float32)

    received = lax.all_to_all(
        dispatch(jnp.repeat(mixed_in, TOP, axis=0)),
        "expert",
        split_axis=0,
        concat_axis=0,
        tiled=True,
    )
    produced = []
    for expert_item in range(local_experts):
        arrived = received[:, expert_item].reshape(group_size * capacity, D)
        preact = jnp.dot(
            arrived, expert_weight[:, 0, expert_item], preferred_element_type=jnp.float32
        )
        hidden = jax.nn.gelu(preact, approximate=False).astype(jnp.bfloat16)
        output_rows = contract_last(hidden, expert_weight[:, 1, expert_item]).astype(jnp.bfloat16)
        produced.append(output_rows.reshape(group_size, capacity, D))
    returned = lax.all_to_all(
        jnp.stack(produced, 1), "expert", split_axis=0, concat_axis=0, tiled=True
    )
    mixed = middle + jnp.sum(combine[:, :, None] * collect(returned), axis=1)
    grad_out = cotangent.astype(jnp.float32)
    slot_grads = (
        (combine[:, :, None] * grad_out[:, None, :])
        .reshape(token_count * TOP, D)
        .astype(jnp.bfloat16)
    )
    grads_in = lax.all_to_all(
        dispatch(slot_grads), "expert", split_axis=0, concat_axis=0, tiled=True
    )
    sent_back = []
    shards = []
    for expert_item in range(local_experts):
        arrived = received[:, expert_item].reshape(group_size * capacity, D)
        arrived_grad = grads_in[:, expert_item].reshape(group_size * capacity, D)
        w_in = expert_weight[:, 0, expert_item]
        w_out = expert_weight[:, 1, expert_item]
        preact = jnp.dot(arrived, w_in, preferred_element_type=jnp.float32)
        hidden = jax.nn.gelu(preact, approximate=False).astype(jnp.bfloat16)
        grad_hidden = jnp.dot(arrived_grad, w_out, preferred_element_type=jnp.float32)
        grad_pre = (grad_hidden * gelu_slope(preact)).astype(jnp.bfloat16)
        sent_back.append(
            contract_last(grad_pre, w_in).astype(jnp.bfloat16).reshape(group_size, capacity, D)
        )
        full_grad = jnp.stack(
            [contract_rows(arrived, grad_pre), contract_rows(arrived_grad, hidden)], 1
        )
        shards.append(lax.psum_scatter(full_grad, "dp", scatter_dimension=0, tiled=True))
    expert_grad = jnp.stack(shards, 2)
    returned_grads = lax.all_to_all(
        jnp.stack(sent_back, 1), "expert", split_axis=0, concat_axis=0, tiled=True
    )
    grad_mixed = jnp.sum(collect(returned_grads), axis=1)
    grad_gain_two = jnp.sum(grad_mixed * normed_two, axis=0)
    grad_shift_two = jnp.sum(grad_mixed, axis=0)
    grad_middle = grad_out + norm_back(grad_mixed * vectors[2], normed_two, inverse_two)
    middle_low = grad_middle.astype(jnp.bfloat16)
    grad_project = contract_rows(attended, middle_low)
    grad_attended = (
        contract_last(middle_low, w_project)
        .astype(jnp.bfloat16)
        .reshape(images, SEQ, HEADS, HEAD_DIM)
    )
    grad_soft = jnp.einsum(
        "bqhc,bkhc->bhqk", grad_attended, values_all, preferred_element_type=jnp.float32
    )
    grad_scores = (
        softmax_out * (grad_soft - jnp.sum(softmax_out * grad_soft, axis=-1, keepdims=True))
    ).astype(jnp.bfloat16)
    grad_queries = (
        jnp.einsum("bhqk,bkhc->bqhc", grad_scores, keys_all, preferred_element_type=jnp.float32)
        * score_scale
    )
    grad_keys = (
        jnp.einsum("bhqk,bqhc->bkhc", grad_scores, queries, preferred_element_type=jnp.float32)
        * score_scale
    )
    grad_values = jnp.einsum(
        "bhqk,bqhc->bkhc", softmax_low, grad_attended, preferred_element_type=jnp.float32
    )
    grad_packed = (
        jnp.stack([grad_queries, grad_keys, grad_values], 2)
        .reshape(token_count, 3 * D)
        .astype(jnp.bfloat16)
    )
    grad_weight_packed = contract_rows(lowered_one, grad_packed)
    grad_lowered = contract_last(grad_packed, w_packed)
    grad_gain_one = jnp.sum(grad_lowered * normed_one, axis=0)
    grad_shift_one = jnp.sum(grad_lowered, axis=0)
    grad_tokens = grad_middle + norm_back(grad_lowered * vectors[0], normed_one, inverse_one)
    attn_grad = jnp.concatenate([grad_weight_packed, grad_project], axis=1)
    vector_grad = jnp.stack(
        [
            grad_gain_one,
            grad_shift_one,
            grad_gain_two,
            grad_shift_two,
            jnp.sum(grad_middle, axis=0),
        ],
        0,
    )
    attn_whole, vector_whole = lax.psum((attn_grad, vector_grad), "expert")
    attn_part, vector_part = (
        lax.psum_scatter(attn_whole, "dp", scatter_dimension=0, tiled=True),
        lax.psum_scatter(vector_whole, "dp", scatter_dimension=1, tiled=True),
    )
    attn_new = adam_update(attn_master, attn_first, attn_second, attn_part, 0.03, 0.1)
    vector_new = adam_update(vector_master, vector_first, vector_second, vector_part, 0.2, 0.0)
    expert_new = adam_update(expert_master, expert_first, expert_second, expert_grad, 0.02, 0.1)
    return (
        mixed.astype(jnp.bfloat16),
        grad_tokens.astype(jnp.bfloat16),
        attn_new[0],
        attn_new[1],
        attn_new[2],
        vector_new[0],
        vector_new[1],
        vector_new[2],
        expert_new[0],
        expert_new[1],
        expert_new[2],
    )


def solution(mesh):
    shards, group = mesh.shape["dp"], mesh.shape["expert"]
    chips = shards == 4 * COLUMNS and group == 2 * CORES
    body = chip_body(shards, group) if chips else general_body
    return jax.shard_map(
        body,
        mesh=mesh,
        in_specs=(
            P(("dp", "expert"), None),
            P(("dp", "expert"), None),
            P(("dp", "expert"), None),
            P(("dp", "expert"), None),
            P("dp", None),
            P("dp", None),
            P("dp", None),
            P(None, "dp"),
            P(None, "dp"),
            P(None, "dp"),
            P("dp", None, "expert", None),
            P("dp", None, "expert", None),
            P("dp", None, "expert", None),
        ),
        out_specs=(
            P(("dp", "expert"), None),
            P(("dp", "expert"), None),
            P("dp", None),
            P("dp", None),
            P("dp", None),
            P(None, "dp"),
            P(None, "dp"),
            P(None, "dp"),
            P("dp", None, "expert", None),
            P("dp", None, "expert", None),
            P("dp", None, "expert", None),
        ),
        check_vma=False,
    )
```

```python
import functools

import jax
import jax.numpy as jnp
from jax import lax
from jax.experimental import pallas as pl
from jax.experimental.layout import Layout, with_layout_constraint
from jax.experimental.pallas import tpu as pltpu
from jax.sharding import PartitionSpec as P

D = 512
HEADS = 8
HEAD_DIM = 64
SEQ = 197
TOP = 2
STEP = 10
PAD = 256
SENT = 208
CORES = 2
COLUMNS = 2

LN_EPS = 1e-06
BETA_ONE = 0.9
BETA_TWO = 0.999
ADAM_EPS = 1e-08
MESH = pl.DeviceIdType.MESH
F32 = jnp.float32
BF16 = jnp.bfloat16
VMEM_LIMIT = 63 * 1024 * 1024


def dot(left, right):
    return jnp.dot(left, right, preferred_element_type=F32)


def contract_rows(left, right):
    return lax.dot_general(
        left, right, (((0,), (0,)), ((), ())), preferred_element_type=F32
    )


def contract_last(left, right):
    return lax.dot_general(
        left, right, (((1,), (1,)), ((), ())), preferred_element_type=F32
    )


def normalize(values):
    centered = values - jnp.mean(values, axis=-1, keepdims=True)
    inverse = lax.rsqrt(jnp.mean(centered * centered, axis=-1, keepdims=True) + LN_EPS)
    return (centered * inverse, inverse)


def norm_back(grad_normed, normed, inverse):
    first_mean = jnp.mean(grad_normed, axis=-1, keepdims=True)
    second_mean = jnp.mean(grad_normed * normed, axis=-1, keepdims=True)
    return inverse * (grad_normed - first_mean - normed * second_mean)


def remote(source, target, send_sem, recv_sem, device):
    return pltpu.make_async_remote_copy(
        src_ref=source,
        dst_ref=target,
        send_sem=send_sem,
        recv_sem=recv_sem,
        device_id=device,
        device_id_type=MESH,
    )


def greet(devices):
    barrier = pltpu.get_barrier_semaphore()
    for device in devices:
        pl.semaphore_signal(barrier, inc=1, device_id=device, device_id_type=MESH)
    pl.semaphore_wait(barrier, len(devices))


def softmax_rows(query, key_rows, half, lane):
    own = jnp.where(lane // HEAD_DIM == half, query, jnp.zeros_like(query))
    scores = contract_last(own, key_rows) * HEAD_DIM ** (-0.5)
    column = lax.broadcasted_iota(jnp.int32, scores.shape, 1)
    scores = jnp.where(column < SEQ, scores, -1e30)
    powers = jnp.exp(scores - jnp.max(scores, axis=-1, keepdims=True))
    return powers * (1.0 / jnp.sum(powers, axis=-1, keepdims=True))


def gelu_parts(preact):
    size = jnp.abs(preact)
    below = 1.0 + 0.23164189 * size
    inner = pl.reciprocal(below, approx=True)
    inner = inner * (2.0 - below * inner)
    series = inner * (
        0.127414796
        + inner * (-0.142248368 + inner * (0.7107068705 + inner * (-0.7265760135 + inner * 0.5307027145)))
    )
    bell = jnp.exp(-0.5 * preact * preact)
    tail = series * bell
    area = jnp.where(preact >= 0.0, 1.0 - tail, tail)
    return preact * area, area + preact * bell * 0.3989422804014327


def adam_update(master, first, second, gradient, step_rate, decay_rate):
    first = BETA_ONE * first + (1.0 - BETA_ONE) * gradient
    second = BETA_TWO * second + (1.0 - BETA_TWO) * gradient * gradient
    first_hat = first / (1.0 - BETA_ONE**STEP)
    second_hat = second / (1.0 - BETA_TWO**STEP)
    master = master - step_rate * (
        first_hat / (jnp.sqrt(second_hat) + ADAM_EPS) + decay_rate * master
    )
    return (master, first, second)


ROUTE_FIRST = ()
SUM_FIRST = (0, 1)
CHAINS = (0, 1, 2, 3)


def block_kernel(
    shards, lines, slots,
    route, comb, attn_f, vec_old, vec_first_old, vec_second_old,
    tok, cot, expw, attn_old, first_old, second_old,
    vec_new, vec_first_new, vec_second_new,
    u_all, g_all, wfull, middle, qkv, att_t, low_t, own_out, d_mate, d_corner, d_over, y_stage, y_got,
    grads, mixed, grad_tok, attn_new, first_new, second_new,
    attn, vec, attnw, route_all, comb_all, vslots, chosen, place, shares,
    gst, xr, xo, xst, zr, zs, fin,
    part_a, part_b, part_c, part_d, whole, v_sum, v_stage, v_got, v_lines,
    attn_send, attn_recv, vec_send, vec_recv, pass_sem, table_send, table_recv,
    g_sem, u_send, u_recv, own_sem, up_send, up_recv, down_send, down_recv, x_send, x_recv,
    out_sem, in_sem, load_sem, w_sem, fin_sem,
    rx_send, rx_recv, ro_send, ro_recv, ru_send, ru_recv, rd_send, rd_recv, credit_up, credit_down,
    back_send, back_recv, y_send, y_recv,
    a_sem, b_sem, c_sem, d_send, d_recv, e_send, e_recv, v_sem, vd_send, vd_recv,
):
    dp, me = lax.axis_index("dp"), lax.axis_index("expert")
    z, x = dp // COLUMNS, dp % COLUMNS
    y, core = me // CORES, me % CORES
    group, images = u_all.shape[:2]
    local, _, rows, ff = expw.shape
    last = lines - 1
    half, quarter = rows // 2, rows // 4
    tile = 512
    tiles = ff // tile
    mate_s, over_s, corner_s = y * CORES + 1 - core, (1 - y) * CORES + core, (1 - y) * CORES + 1 - core
    mate, over, corner = (dp, mate_s), (dp, over_s), (dp, corner_s)
    above = (lax.rem(z + 1, lines) * COLUMNS + x, me)
    below = (lax.rem(z + last, lines) * COLUMNS + x, me)
    beside = (z * COLUMNS + 1 - x, me)
    along = [(lax.rem(z + k, lines) * COLUMNS + x, me) for k in range(1, lines)]
    peers = [(lax.rem(dp + k, shards), me) for k in range(1, shards)]
    sources = [lax.rem(dp + shards - k, shards) for k in range(1, shards)]
    partners = (mate, over, corner)
    greet(peers + list(partners))
    mine = pl.ds(pl.multiple_of(core * half, half), half)
    theirs = pl.ds(pl.multiple_of((1 - core) * half, half), half)
    sent_images = pl.ds(0, SENT)

    attn[...] = attn_f[...].astype(BF16)
    vec[...] = jnp.zeros_like(vec)
    vec[: vec_old.shape[0], : vec_old.shape[1]] = vec_old[...]
    for k, peer in enumerate(peers):
        remote(attn.at[mine], attnw.at[dp, mine], attn_send.at[k], attn_recv.at[dp], peer).start()
        remote(vec, vslots.at[dp], vec_send.at[k], vec_recv.at[dp], peer).start()
    for k, partner in enumerate(partners):
        remote(route, route_all.at[me], table_send.at[k, 0], table_recv.at[me, 0], partner).start()
        remote(comb, comb_all.at[me], table_send.at[k, 1], table_recv.at[me, 1], partner).start()

    def held(e, chain, at):
        column = x if chain == 0 else 1 - x
        return wfull.at[e, :, at * COLUMNS + column]

    def up(e, chain, hop, ref):
        return remote(ref, ref, up_send.at[e * 2 + chain, hop], up_recv.at[e * 2 + chain, hop], above)

    def down(e, chain, hop, ref):
        return remote(ref, ref, down_send.at[e * 2 + chain, hop], down_recv.at[e * 2 + chain, hop], below)

    def across(e, at, ref):
        return remote(ref, ref, x_send.at[e, at], x_recv.at[e, at], beside)

    def start_own(e):
        target = held(e, 0, z)
        remote(expw.at[e], target, x_send.at[e, z], x_recv.at[e, z], beside).start()

        @pl.when(z < last)
        def _():
            remote(expw.at[e], target, up_send.at[e * 2, 0], up_recv.at[e * 2, 0], above).start()

        @pl.when(z > 0)
        def _():
            remote(expw.at[e], target, down_send.at[e * 2, 0], down_recv.at[e * 2, 0], below).start()

    def start_other(e):
        ref = held(e, 1, z)
        across(e, z, ref).wait_recv()

        @pl.when(z < last)
        def _():
            up(e, 1, 0, ref).start()

        @pl.when(z > 0)
        def _():
            down(e, 1, 0, ref).start()

    def hand_on(e, chain, hop):
        cross = e not in ROUTE_FIRST
        from_below = jnp.maximum(z - 1 - hop, 0)
        from_above = jnp.minimum(z + 1 + hop, last)

        @pl.when(z - 1 - hop >= 0)
        def _():
            ref = held(e, chain, from_below)
            up(e, chain, hop, ref).wait_recv()

            @pl.when(z < last)
            def _():
                up(e, chain, hop + 1, ref).start()

            if cross:
                across(e, from_below, ref).start()

        @pl.when(z + 1 + hop <= last)
        def _():
            ref = held(e, chain, from_above)
            down(e, chain, hop, ref).wait_recv()

            @pl.when(z > 0)
            def _():
                down(e, chain, hop + 1, ref).start()

            if cross:
                across(e, from_above, ref).start()

    def weights_here(e):
        if e not in ROUTE_FIRST:
            for at in range(lines):
                across(e, at, held(e, 1, at)).wait_recv()

    def settle_weights(e):
        ref = held(e, 0, z)
        for chain in range(2 if e in ROUTE_FIRST else 1):
            for hop in range(last):
                @pl.when(jnp.logical_and(z - hop >= 0, z < last))
                def _():
                    up(e, chain, hop, ref).wait_send()

                @pl.when(jnp.logical_and(z + hop <= last, z > 0))
                def _():
                    down(e, chain, hop, ref).wait_send()

        if e in ROUTE_FIRST:
            across(e, z, ref).wait_send()
        else:
            for at in range(lines):
                across(e, at, ref).wait_send()

    start_own(0)
    start_own(1)
    g_own = cot.at[:, sent_images]
    g_mine = g_all.at[me]
    remote(g_own, g_mine, g_sem.at[0], g_sem.at[1], mate).start()
    remote(g_own, g_mine, g_sem.at[2], g_sem.at[3], over).start()

    attnw[dp, mine] = attn[mine]
    vslots[dp] = vec[...]
    route_all[me] = route[...]
    comb_all[me] = comb[...]

    for k, partner in enumerate(partners):
        source = partner[1]
        remote(route, route_all.at[source], table_send.at[k, 0], table_recv.at[source, 0], partner).wait()
        remote(comb, comb_all.at[source], table_send.at[k, 1], table_recv.at[source, 1], partner).wait()
    for s in range(group):
        for el in range(local):
            named = me * local + el
            row = s * local + el
            hits = [route_all[s, t : t + 1, :] == named for t in range(TOP)]
            chosen[row : row + 1, :] = sum(jnp.where(h, 1.0, 0.0) for h in hits)
            shares[row : row + 1, :] = sum(
                jnp.where(h, comb_all[s, t : t + 1, :], 0.0) for t, h in enumerate(hits)
            )
    earlier = lax.broadcasted_iota(jnp.int32, (PAD, PAD), 0) < lax.broadcasted_iota(
        jnp.int32, (PAD, PAD), 1
    )
    earlier = jnp.where(earlier, 1.0, 0.0).astype(BF16)
    count = jnp.zeros((group * local, 1), F32)
    for i in range(images):
        block = chosen[:, i * PAD : (i + 1) * PAD]
        position = count + dot(block.astype(BF16), earlier)
        place[:, i * PAD : (i + 1) * PAD] = jnp.where(block > 0.0, position, -1.0).astype(jnp.int32)
        count = count + jnp.sum(block, axis=1, keepdims=True)

    for k, (peer, source) in enumerate(zip(peers, sources)):
        remote(attn.at[mine], attnw.at[source, mine], attn_send.at[k], attn_recv.at[source], peer).wait()
        remote(vec, vslots.at[source], vec_send.at[k], vec_recv.at[source], peer).wait()
    to_mate = remote(attnw.at[:, mine], attnw.at[:, mine], pass_sem.at[0], pass_sem.at[1], mate)
    to_mate.start()
    lane = lax.broadcasted_iota(jnp.int32, (128, D), 1)
    entry = lax.broadcasted_iota(jnp.int32, (128, D), 0)
    width = D // shards
    vectors = jnp.zeros((8, D), F32)
    for d in range(shards):
        spread = jnp.where(jnp.logical_and(entry < width, lane == entry + d * width), 1.0, 0.0)
        vectors = vectors + dot(vslots[d].astype(BF16), spread.astype(BF16))
    gain_one, shift_one = vectors[0:1], vectors[1:2]
    gain_two, shift_two, shift_out = vectors[2:3], vectors[3:4], vectors[4:5]
    remote(attnw.at[:, theirs], attnw.at[:, theirs], pass_sem.at[0], pass_sem.at[1], mate).wait_recv()
    pair_lane = lax.broadcasted_iota(jnp.int32, (PAD, 2 * HEAD_DIM), 1)

    def u_part(s, i):
        return u_all.at[s, i]

    def u_to(k, s, i, partner):
        return remote(u_part(s, i), u_part(s, i), u_send.at[i, k], u_recv.at[i, k], partner)

    def forward(tok_v, qkv_v, att_v, mid_v, u_v, att_tv, low_tv):
        fetch = pltpu.make_async_copy(tok, tok_v, in_sem.at[0])
        fetch.start()
        fetch.wait()

        def outs(i):
            return (
                pltpu.make_async_copy(u_v.at[i, sent_images], u_all.at[me, i], out_sem.at[i, 0]),
                pltpu.make_async_copy(qkv_v.at[i], qkv.at[i], out_sem.at[i, 1]),
                pltpu.make_async_copy(mid_v.at[i], middle.at[i], out_sem.at[i, 2]),
                pltpu.make_async_copy(att_tv.at[i], att_t.at[i], out_sem.at[i, 3]),
                pltpu.make_async_copy(low_tv.at[i], low_t.at[i], out_sem.at[i, 4]),
            )

        def send_image(i):
            outs(i)[0].wait()
            u_to(0, me, i, over).start()
            u_to(1, me, i, mate).start()

        def one_image(i, carry):
            inputs = tok_v[i].astype(F32)
            normed, _ = normalize(inputs)
            lowered = (normed * gain_one + shift_one).astype(BF16)
            for part in range(3):
                columns = pl.ds(part * D, D)
                qkv_v[i, :, columns] = dot(lowered, attnw[:, :, columns].reshape(D, D)).astype(BF16)
            for pair in range(HEADS // 2):
                offset = pair * 2 * HEAD_DIM
                query = qkv_v[i, :, offset : offset + 128]
                key_rows = qkv_v[i, :, D + offset : D + offset + 128]
                value = qkv_v[i, :, 2 * D + offset : 2 * D + offset + 128]
                results = []
                for which in range(2):
                    probs = softmax_rows(query, key_rows, which, pair_lane)
                    results.append(dot(probs.astype(BF16), value))
                joined = jnp.where(pair_lane < HEAD_DIM, results[0], results[1])
                att_v[i, :, offset : offset + 128] = joined.astype(BF16)
            mid = inputs + dot(att_v[i], attnw[:, :, 3 * D :].reshape(D, D)) + shift_out
            mid_v[i] = mid
            normed_two, _ = normalize(mid)
            u_v[i] = (normed_two * gain_two + shift_two).astype(BF16)
            att_tv[i] = att_v[i].T
            low_tv[i] = lowered.T
            for copy in outs(i):
                copy.start()

            @pl.when(i > 0)
            def _():
                send_image(i - 1)

            for turn, actions in enumerate((
                (lambda: start_own(2),),
                (lambda: hand_on(0, 0, 1),),
                (lambda: hand_on(1, 0, 0),),
                (lambda: hand_on(0, 0, 2),),
                (lambda: hand_on(1, 0, 1), lambda: start_own(3)),
            )):
                @pl.when(i == turn)
                def _():
                    for action in actions:
                        action()

            return carry

        hand_on(0, 0, 0)
        lax.fori_loop(0, images, one_image, 0)
        send_image(images - 1)
        for i in range(images):
            for copy in outs(i)[1:]:
                copy.wait()

    pl.run_scoped(
        forward,
        pltpu.VMEM((images, PAD, D), BF16),
        pltpu.VMEM((images, PAD, 3 * D), BF16),
        pltpu.VMEM((images, PAD, D), BF16),
        pltpu.VMEM((images, PAD, D), F32),
        pltpu.VMEM((images, PAD, D), BF16),
        pltpu.VMEM((images, D, PAD), BF16),
        pltpu.VMEM((images, D, PAD), BF16),
    )
    g_over = g_all.at[over_s]
    remote(g_over, g_over, g_sem.at[2], g_sem.at[3], over).wait()
    remote(g_over, g_over, g_sem.at[4], g_sem.at[5], mate).start()
    g_mate = g_all.at[mate_s]
    remote(g_mate, g_mate, g_sem.at[0], g_sem.at[1], mate).wait()
    g_corner = g_all.at[corner_s]
    remote(g_corner, g_corner, g_sem.at[4], g_sem.at[5], mate).wait()

    def slot_of(e):
        return e % 2 if e < local - 1 else 2

    def cross_sum(e, k):
        return remote(
            gst.at[slot_of(e), k, pl.ds(lines, lines)], xr.at[e % 2, k],
            rx_send.at[e % 2, k], rx_recv.at[e % 2, k], beside,
        )

    def swap(e, k):
        return remote(xst.at[k], xo.at[e % 2, k], ro_send.at[e % 2, k], ro_recv.at[e % 2, k], beside)

    def partial(e, k, owner, which):
        value = gst[slot_of(e), k, which * lines + owner].astype(F32)
        if e not in SUM_FIRST:
            value = value + xr[e % 2, k, owner].astype(F32)
        return value

    def z_send(e, k, way, hop):
        sent, landed = zs.at[k, way], zr.at[k, way, hop]
        if e not in SUM_FIRST:
            sent, landed = sent.at[0], landed.at[0]
        if way == 0:
            return remote(sent, landed, ru_send.at[k], ru_recv.at[k, hop], above)
        return remote(sent, landed, rd_send.at[k], rd_recv.at[k, hop], below)

    def one_hop(e, k, hop, way):
        ahead = z if way == 0 else last - z
        owner = jnp.minimum(z + last - hop, last) if way == 0 else jnp.maximum(z - last + hop, 0)
        credit = (credit_up, credit_down)[way]
        both = range(2 if e in SUM_FIRST else 1)

        @pl.when(jnp.logical_and(ahead <= hop, ahead < last))
        def _():
            if hop > 0:
                @pl.when(ahead <= hop - 1)
                def _():
                    z_send(e, k, way, hop - 1).wait_send()

            if CHAINS.index(e) > 0:
                @pl.when(ahead == hop)
                def _():
                    pl.semaphore_wait(credit.at[k], 1)

            if hop > 0:
                @pl.when(ahead >= 1)
                def _():
                    z_send(e, k, way, hop - 1).wait_recv()
                    for which in both:
                        total = partial(e, k, owner, which) + zr[k, way, hop - 1, which].astype(F32)
                        zs[k, way, which] = total.astype(BF16)

                @pl.when(ahead < 1)
                def _():
                    for which in both:
                        zs[k, way, which] = partial(e, k, owner, which).astype(BF16)
            else:
                for which in both:
                    zs[k, way, which] = partial(e, k, owner, which).astype(BF16)
            z_send(e, k, way, hop).start()

    def hop_step(e, k, hop):
        if hop == 0 and e not in SUM_FIRST:
            cross_sum(e, k).wait_recv()
        one_hop(e, k, hop, 0)
        one_hop(e, k, hop, 1)

    def to_result(e, k):
        return pltpu.make_async_copy(fin.at[k], grads.at[e, k], fin_sem.at[k])

    def finish(e, k):
        turn = CHAINS.index(e)
        if turn > 0:
            to_result(e, k).wait()
        fin[k] = partial(e, k, z, 0)

        @pl.when(z > 0)
        def _():
            z_send(e, k, 0, last - 1).wait_recv()
            fin[k] += zr[k, 0, last - 1, 0].astype(F32)
            z_send(e, k, 1, last - 1).wait_send()

        @pl.when(z < last)
        def _():
            z_send(e, k, 1, last - 1).wait_recv()
            fin[k] += zr[k, 1, last - 1, 0].astype(F32)
            z_send(e, k, 0, last - 1).wait_send()

        if e in SUM_FIRST:
            own = partial(e, k, z, 1)

            @pl.when(z == 0)
            def _():
                xst[k] = (own + zr[k, 1, last - 1, 1].astype(F32)).astype(BF16)

            @pl.when(z == last)
            def _():
                xst[k] = (own + zr[k, 0, last - 1, 1].astype(F32)).astype(BF16)

            @pl.when(jnp.logical_and(z > 0, z < last))
            def _():
                arrived = zr[k, 0, last - 1, 1].astype(F32) + zr[k, 1, last - 1, 1].astype(F32)
                xst[k] = (own + arrived).astype(BF16)

            swap(e, k).start()
        else:
            to_result(e, k).start()
        if turn + 1 < local:
            @pl.when(z > 0)
            def _():
                pl.semaphore_signal(credit_up.at[k], inc=1, device_id=below, device_id_type=MESH)

            @pl.when(z < last)
            def _():
                pl.semaphore_signal(credit_down.at[k], inc=1, device_id=above, device_id_type=MESH)

    def collect(e, k):
        swap(e, k).wait()
        fin[k] += xo[e % 2, k].astype(F32)
        to_result(e, k).start()

    def source_of(e, t):
        r = t if e == local - 1 else group - 1 - t
        across_y = (1 - y) + (r // CORES) * (2 * y - 1)
        return across_y * CORES + (1 - core) + (r % CORES) * (2 * core - 1)

    def experts(ubuf, gbuf, work, x_t, m_t, dacc, made_all, d_stage):
        def load_u(s):
            return pltpu.make_async_copy(u_all.at[s], ubuf.at[:, sent_images], load_sem.at[0])

        def load_g(ref):
            return pltpu.make_async_copy(ref, gbuf.at[:, sent_images], load_sem.at[1])

        def start_load(s):
            load_u(s).start()

            @pl.when(s == me)
            def _():
                load_g(g_own).start()

            @pl.when(s != me)
            def _():
                load_g(g_all.at[s]).start()

        def load_weights(e):
            copies = [pltpu.make_async_copy(expw.at[e], gst.at[2, :, dp], w_sem.at[0])]
            for k, d in enumerate(sources):
                copies.append(pltpu.make_async_copy(wfull.at[e, :, d], gst.at[2, :, d], w_sem.at[k + 1]))
            return copies

        def weight_grad(e, k):
            left = x_t if k == 0 else m_t

            def one_tile(j, carry):
                right = work[tiles * (1 - k) + j]
                block = dot(left[...], right).astype(BF16)
                columns = pl.ds(pl.multiple_of(j * tile, tile), tile)
                for d in range(shards):
                    which = lax.rem(x + d % COLUMNS, COLUMNS)
                    index = which * lines + d // COLUMNS
                    gst[slot_of(e), k, index, :, columns] = block[d * rows : (d + 1) * rows]
                return carry

            lax.fori_loop(0, tiles, one_tile, 0)
            if e not in SUM_FIRST:
                cross_sum(e, k).start()

        def pick_of(s, e, i):
            slot_row = lax.broadcasted_iota(jnp.int32, (slots, PAD), 0)
            return slot_row == place[pl.ds(s * local + e, 1), i * PAD : (i + 1) * PAD]

        def one_source(e, t, after_gather):
            s = source_of(e, t)
            load_u(s).wait()
            load_g(g_own).wait()
            arrived = jnp.zeros((slots, D), F32)
            grad = jnp.zeros((slots, D), F32)
            share = jnp.zeros((slots, 1), F32)
            for i in range(images):
                hit = pick_of(s, e, i)
                pick = jnp.where(hit, 1.0, 0.0).astype(BF16)
                weight = shares[pl.ds(s * local + e, 1), i * PAD : (i + 1) * PAD]
                share += jnp.sum(jnp.where(hit, weight, 0.0), axis=1, keepdims=True)
                arrived += dot(pick, ubuf[i])
                grad += dot(pick, gbuf[i])
            arrived = arrived.astype(BF16)
            grad = (share * grad).astype(BF16)
            here = pl.ds(pl.multiple_of(t * slots, slots), slots)
            x_t[:, here] = arrived.T
            m_t[:, here] = grad.T
            after_gather()

            def one_tile(j, carry):
                columns = pl.ds(pl.multiple_of(j * tile, tile), tile)
                preact = dot(arrived, gst[2, 0, :, :, columns].reshape(D, tile))
                hidden, slope = gelu_parts(preact)
                work[j, here, :] = hidden.astype(BF16)
                grad_hidden = dot(grad, gst[2, 1, :, :, columns].reshape(D, tile))
                work[tiles + j, here, :] = (grad_hidden * slope).astype(BF16)
                return carry

            lax.fori_loop(0, tiles, one_tile, 0)
            made = jnp.zeros((slots, D), F32)
            back = jnp.zeros((slots, D), F32)
            for j in range(tiles):
                columns = pl.ds(j * tile, tile)
                made += contract_last(work[j, here, :], gst[2, 1, :, :, columns].reshape(D, tile))
                back += contract_last(work[tiles + j, here, :], gst[2, 0, :, :, columns].reshape(D, tile))
            made_all[s, e * slots : (e + 1) * slots] = (share * made.astype(BF16).astype(F32)).astype(BF16)
            back = back.astype(BF16)
            for i in range(images):
                pick = jnp.where(pick_of(s, e, i), 1.0, 0.0).astype(BF16)
                placed = contract_rows(pick, back)[:SENT]
                if e == 0:
                    dacc[s, i * SENT : (i + 1) * SENT] = placed
                else:
                    dacc[s, i * SENT : (i + 1) * SENT] += placed

        def next_load(e, t):
            @pl.when(t + 1 < group)
            def _():
                if e == 0:
                    @pl.when(t == 0)
                    def _():
                        for i in range(images):
                            u_to(1, mate_s, i, mate).wait()

                    @pl.when(t == 1)
                    def _():
                        for i in range(images):
                            u_to(0, over_s, i, over).wait()
                            u_to(2, over_s, i, mate).start()

                    @pl.when(t == 2)
                    def _():
                        for i in range(images):
                            u_to(2, corner_s, i, mate).wait()

                start_load(source_of(e, t + 1))

            if e + 1 < local:
                @pl.when(t + 1 == group)
                def _():
                    start_load(source_of(e + 1, 0))

        def to_corner():
            return remote(d_stage.at[0], d_corner, back_send.at[0], back_recv.at[0], mate)

        def to_mate_sum():
            return remote(d_stage.at[1], d_mate, back_send.at[1], back_recv.at[1], mate)

        def to_over():
            return remote(d_stage.at[2], d_over, back_send.at[2], back_recv.at[2], over)

        def sums_corner():
            d_stage[0] = dacc[corner_s].astype(BF16)
            to_corner().start()

        def sums_mate():
            d_stage[1] = dacc[mate_s].astype(BF16)
            to_mate_sum().start()
            to_corner().wait_recv()
            landed = pltpu.make_async_copy(d_corner, d_stage.at[2], load_sem.at[2])
            landed.start()
            landed.wait()
            d_stage[2] = (dacc[over_s] + d_stage[2].astype(F32)).astype(BF16)
            to_over().start()

        plan = {
            (0, 0): (lambda: hand_on(1, 0, 2),),
            (0, 1): (lambda: hand_on(2, 0, 0),),
            (0, 3): (lambda: hand_on(2, 0, 1),),
            (1, 0): (lambda: hand_on(2, 0, 2), lambda: hand_on(3, 0, 0)),
            (1, 1): (lambda: hop_step(0, 0, 1),),
            (1, 2): (lambda: hand_on(3, 0, 1),),
            (1, 3): (lambda: hop_step(0, 1, 1), lambda: hand_on(3, 0, 2)),
            (2, 0): (lambda: hop_step(0, 1, 2),),
            (2, 1): (lambda: finish(0, 0),),
            (2, 2): (lambda: finish(0, 1), lambda: hop_step(1, 0, 0)),
            (2, 3): (lambda: hop_step(1, 1, 0),),
            (3, 0): (sums_corner, lambda: collect(0, 0), lambda: collect(0, 1)),
            (3, 1): (lambda: hop_step(1, 0, 1),),
            (3, 2): (sums_mate, lambda: hop_step(1, 1, 1)),
            (3, 3): (lambda: hop_step(1, 0, 2),),
        }
        after_grad = {
            (0, 0): (lambda: hop_step(0, 0, 0),),
            (0, 1): (lambda: hop_step(0, 1, 0),),
            (1, 1): (lambda: hop_step(0, 0, 2),),
            (3, 1): (lambda: hop_step(1, 1, 2),),
        }

        empty = jnp.zeros((images, PAD - SENT, D), BF16)
        ubuf[:, SENT:, :] = empty
        gbuf[:, SENT:, :] = empty
        start_load(source_of(0, 0))
        for e in range(local):
            weights_here(e)
            copies = load_weights(e)
            for copy in copies:
                copy.start()
            for copy in copies:
                copy.wait()

            def step(t, carry, e=e):
                one_source(e, t, lambda: next_load(e, t))
                for turn in range(group):
                    actions = plan.get((e, turn), ())
                    if actions:
                        @pl.when(t == turn)
                        def _():
                            for action in actions:
                                action()

                return carry

            lax.fori_loop(0, group, step, 0)
            for k in range(2):
                weight_grad(e, k)
                for action in after_grad.get((e, k), ()):
                    action()

        own_sum = pltpu.make_async_copy(dacc.at[me], own_out, own_sem.at[2])
        own_sum.start()

        def one_sum(s, i):
            total = jnp.zeros((PAD, D), F32)
            for e in range(local):
                pick = jnp.where(pick_of(s, e, i), 1.0, 0.0).astype(BF16)
                total += contract_rows(pick, made_all[s, e * slots : (e + 1) * slots])
            return total[:SENT]

        def stage(k):
            return pltpu.make_async_copy(d_stage.at[k], y_stage.at[k], own_sem.at[3])

        for k, (s, partner) in enumerate(zip((mate_s, over_s, corner_s), partners)):
            (to_corner, to_mate_sum, to_over)[k]().wait_send()
            for i in range(images):
                d_stage[k, i * SENT : (i + 1) * SENT] = one_sum(s, i).astype(BF16)
            stage(k).start()
            stage(k).wait()
            remote(y_stage.at[k], y_got.at[k], y_send.at[k], y_recv.at[k], partner).start()
        for i in range(images):
            d_stage[0, i * SENT : (i + 1) * SENT] = one_sum(me, i).astype(BF16)
        last_stage = pltpu.make_async_copy(d_stage.at[0], y_stage.at[3], own_sem.at[3])
        last_stage.start()
        last_stage.wait()
        own_sum.wait()

    count_rows = images * SENT
    pl.run_scoped(
        experts,
        pltpu.VMEM((images, PAD, D), BF16),
        pltpu.VMEM((images, PAD, D), BF16),
        pltpu.VMEM((2 * tiles, group * slots, tile), BF16),
        pltpu.VMEM((D, group * slots), BF16),
        pltpu.VMEM((D, group * slots), BF16),
        pltpu.VMEM((group, count_rows, D), F32),
        pltpu.VMEM((group, local * slots, D), BF16),
        pltpu.VMEM((3, count_rows, D), BF16),
    )
    remote(d_mate, d_mate, back_send.at[1], back_recv.at[1], mate).wait_recv()
    remote(d_over, d_over, back_send.at[2], back_recv.at[2], over).wait_recv()

    def rows_of(start, size):
        return pl.ds(pl.multiple_of(start, quarter), size)

    kept_y, given_y = rows_of(y * quarter, quarter), rows_of((1 - y) * quarter, quarter)
    final_rows = rows_of(core * half + y * quarter, quarter)

    def backward(g_low, g_mid, d_att):
        v_sum[...] = jnp.zeros_like(v_sum)

        def before_attention(cot_v, mid_v, own_v, mate_v, over_v):
            fetches = [
                pltpu.make_async_copy(source, target, in_sem.at[n])
                for n, (source, target) in enumerate((
                    (cot, cot_v), (middle, mid_v), (own_out, own_v), (d_mate, mate_v), (d_over, over_v),
                ))
            ]
            for fetch in fetches:
                fetch.start()
            for fetch in fetches:
                fetch.wait()

            def one_image(i, carry):
                here = pl.ds(pl.multiple_of(i * SENT, SENT), SENT)
                normed, inverse = normalize(mid_v[i])
                grad = own_v[here] + mate_v[here].astype(F32) + over_v[here].astype(F32)
                grad = jnp.concatenate([grad, jnp.zeros((PAD - SENT, D), F32)], axis=0)
                v_sum[2:3] += jnp.sum(grad * normed, axis=0, keepdims=True)
                v_sum[3:4] += jnp.sum(grad, axis=0, keepdims=True)
                total = cot_v[i].astype(F32) + norm_back(grad * gain_two, normed, inverse)
                v_sum[4:5] += jnp.sum(total, axis=0, keepdims=True)
                g_mid[i] = total
                low = total.astype(BF16)
                g_low[i] = low
                d_att[i] = contract_last(low, attnw[:, :, 3 * D :].reshape(D, D)).astype(BF16)
                return carry

            lax.fori_loop(0, images, one_image, 0)

        pl.run_scoped(
            before_attention,
            pltpu.VMEM((images, PAD, D), BF16),
            pltpu.VMEM((images, PAD, D), F32),
            pltpu.VMEM((count_rows, D), F32),
            pltpu.VMEM((count_rows, D), BF16),
            pltpu.VMEM((count_rows, D), BF16),
        )

        def through_attention(
            tok_v, qkv_v, att_tv, low_tv, dqkv, part_own, sum_a, sum_b, sum_c, sum_d, gt_v, old_v, got_v,
        ):
            def move_a(p):
                return remote(part_own.at[p, :, theirs], part_a.at[p], a_sem.at[p, 0], a_sem.at[p, 1], mate)

            def move_b(p):
                return remote(sum_a.at[p, :, given_y], part_b.at[p], b_sem.at[p, 0], b_sem.at[p, 1], over)

            def move_c(p):
                return remote(sum_b.at[p, :, 1 - x], part_c.at[p], c_sem.at[p, 0], c_sem.at[p, 1], beside)

            def move_d(p, k):
                target = lax.rem(z + k, lines)
                return remote(
                    sum_c.at[p, target], part_d.at[p, z], d_send.at[p, k - 1], d_recv.at[p, z], along[k - 1]
                )

            def arrived_d(p, k):
                source = lax.rem(z + lines - k, lines)
                return remote(
                    sum_c.at[p, source], part_d.at[p, source], d_send.at[p, k - 1], d_recv.at[p, source],
                    along[k - 1],
                )

            def move_e(p, k):
                own = whole.at[final_rows, pl.ds(p * D, D)]
                return remote(own, own, e_send.at[p, k], e_recv.at[p, k], partners[k])

            def stage_b(p):
                move_a(p).wait()
                sum_a[p] = (part_own[p, :, mine].astype(F32) + part_a[p].astype(F32)).astype(BF16)
                move_b(p).start()

            def stage_c(p):
                move_b(p).wait()
                total = sum_a[p, :, kept_y].astype(F32) + part_b[p].astype(F32)
                sum_b[p] = total.astype(BF16).reshape(lines, COLUMNS, quarter, D)
                move_c(p).start()

            def stage_d(p):
                move_c(p).wait()
                total = sum_b[p, :, x].astype(F32) + part_c[p].astype(F32)
                sum_c[p] = total.astype(BF16)
                sum_d[p] = total
                for k in range(1, lines):
                    move_d(p, k).start()

            def stage_e(p):
                total = sum_d[p, z]
                for k in range(1, lines):
                    arrived_d(p, k).wait_recv()
                    total = total + part_d[p, lax.rem(z + lines - k, lines)].astype(F32)
                whole[final_rows, pl.ds(p * D, D)] = total
                for k in range(3):
                    move_e(p, k).start()

            def settle(p):
                for k in range(1, lines):
                    move_d(p, k).wait_send()
                for k in range(3):
                    move_e(p, k).wait()

            def scatter_part(p, left_t, right):
                block = jnp.zeros((D, D), F32)
                for i in range(images):
                    block += dot(left_t[i], right(i))
                part_own[p] = block.astype(BF16).reshape(shards, rows, D)
                move_a(p).start()

            def block_output():
                for k, partner in enumerate(partners):
                    remote(y_stage.at[k], y_got.at[k], y_send.at[k], y_recv.at[k], partner).wait()
                fetch_output.wait()
                for k in range(4):
                    source = y_stage.at[3] if k == 3 else y_got.at[k]
                    landed = pltpu.make_async_copy(source, got_v, in_sem.at[3])
                    landed.start()
                    landed.wait()
                    for i in range(images):
                        part = got_v[i * SENT : (i + 1) * SENT].astype(F32)
                        if k < 3:
                            g_mid[i, :SENT] += part
                        else:
                            g_low[i, :SENT] = (g_mid[i, :SENT] + part).astype(BF16)
                pltpu.make_async_copy(g_low, mixed, in_sem.at[5]).start()

            fetches = [
                pltpu.make_async_copy(source, target, in_sem.at[n])
                for n, (source, target) in enumerate((
                    (tok, tok_v), (qkv, qkv_v), (att_t, att_tv), (low_t, low_tv),
                    (attn_old, old_v.at[0]), (first_old, old_v.at[1]), (second_old, old_v.at[2]),
                ))
            ]
            for fetch in fetches:
                fetch.start()
            for fetch in fetches:
                fetch.wait()
            finish(1, 0)
            finish(1, 1)
            hop_step(2, 0, 0)
            hop_step(2, 1, 0)
            scatter_part(3, att_tv, lambda i: g_low[i])

            key_index = lax.broadcasted_iota(jnp.int32, (PAD, PAD), 0)

            def result(i):
                return pltpu.make_async_copy(gt_v.at[i], grad_tok.at[i], out_sem.at[i, 0])

            def one_image(i, carry):
                for pair in range(HEADS // 2):
                    offset = pair * 2 * HEAD_DIM
                    query = qkv_v[i, :, offset : offset + 128]
                    key_rows = qkv_v[i, :, D + offset : D + offset + 128]
                    value = qkv_v[i, :, 2 * D + offset : 2 * D + offset + 128]
                    grad = d_att[i, :, offset : offset + 128]
                    results = []
                    for which in range(2):
                        own_half = pair_lane // HEAD_DIM == which
                        scores = contract_last(
                            jnp.where(own_half, key_rows, jnp.zeros_like(key_rows)), query
                        ) * HEAD_DIM ** (-0.5)
                        scores = jnp.where(key_index < SEQ, scores, -1e30)
                        powers = jnp.exp(scores - jnp.max(scores, axis=0, keepdims=True))
                        probs = powers * (1.0 / jnp.sum(powers, axis=0, keepdims=True))
                        grad_probs = contract_last(
                            jnp.where(own_half, value, jnp.zeros_like(value)), grad
                        )
                        inner = jnp.sum(probs * grad_probs, axis=0, keepdims=True)
                        grad_scores = (probs * (grad_probs - inner)).astype(BF16)
                        results.append((
                            contract_rows(grad_scores, key_rows) * HEAD_DIM ** (-0.5),
                            dot(grad_scores, query) * HEAD_DIM ** (-0.5),
                            dot(probs.astype(BF16), grad),
                        ))
                    for part in range(3):
                        joined = jnp.where(pair_lane < HEAD_DIM, results[0][part], results[1][part])
                        dqkv[i, :, part * D + offset : part * D + offset + 128] = joined.astype(BF16)
                grad = jnp.zeros((PAD, D), F32)
                for part in range(3):
                    columns = pl.ds(part * D, D)
                    grad += contract_last(dqkv[i, :, columns], attnw[:, :, columns].reshape(D, D))
                normed, inverse = normalize(tok_v[i].astype(F32))
                v_sum[0:1] += jnp.sum(grad * normed, axis=0, keepdims=True)
                v_sum[1:2] += jnp.sum(grad, axis=0, keepdims=True)
                gt_v[i] = (g_mid[i] + norm_back(grad * gain_one, normed, inverse)).astype(BF16)
                result(i).start()
                for turn, actions in enumerate((
                    (lambda: stage_b(3), lambda: hop_step(2, 0, 1), lambda: hop_step(2, 1, 1)),
                    (lambda: stage_c(3), lambda: collect(1, 0), lambda: collect(1, 1),
                     lambda: hop_step(2, 0, 2), lambda: hop_step(2, 1, 2)),
                    (lambda: stage_d(3), lambda: finish(2, 0), lambda: finish(2, 1), lambda: hop_step(3, 0, 0)),
                    (lambda: stage_e(3), lambda: hop_step(3, 1, 0), lambda: hop_step(3, 0, 1)),
                    (lambda: hop_step(3, 1, 1), lambda: hop_step(3, 0, 2)),
                )):
                    @pl.when(i == turn)
                    def _():
                        for action in actions:
                            action()

                return carry

            lax.fori_loop(0, images, one_image, 0)

            def v_move(n, partner):
                return remote(v_stage.at[n], v_got.at[n], v_sem.at[n, 0], v_sem.at[n, 1], partner)

            fetch_output = pltpu.make_async_copy(middle, g_mid, in_sem.at[6])
            fetch_output.start()
            v_stage[0] = v_sum[...]
            v_move(0, mate).start()
            for p in range(3):
                scatter_part(p, low_tv, lambda i: dqkv[i, :, p * D : (p + 1) * D])
            tail = {
                0: (lambda: hop_step(3, 1, 2), block_output),
                1: (lambda: finish(3, 0),),
                2: (lambda: finish(3, 1),),
            }
            for n, stage in enumerate((stage_b, stage_c, stage_d)):
                for p in range(3):
                    stage(p)
                v_move(n, (mate, over, beside)[n]).wait()
                total = v_stage[n] + v_got[n]
                if n < 2:
                    v_stage[n + 1] = total
                    v_move(n + 1, (over, beside)[n]).start()
                else:
                    v_lines[z] = total
                    for k in range(1, lines):
                        remote(
                            v_lines.at[z], v_lines.at[z], vd_send.at[k - 1], vd_recv.at[z], along[k - 1]
                        ).start()
                for action in tail[n]:
                    action()
            for p in range(3):
                stage_e(p)
            for k in range(1, lines):
                source = lax.rem(z + lines - k, lines)
                remote(
                    v_lines.at[source], v_lines.at[source], vd_send.at[k - 1], vd_recv.at[source], along[k - 1]
                ).wait()
            total = v_lines[0]
            for n in range(1, lines):
                total = total + v_lines[n]
            for d in range(shards):
                @pl.when(dp == d)
                def _():
                    gradient = total[: vec_old.shape[0], d * width : (d + 1) * width]
                    new = adam_update(
                        vec_old[...], vec_first_old[...], vec_second_old[...], gradient, 0.2, 0.0
                    )
                    vec_new[...], vec_first_new[...], vec_second_new[...] = new

            for p in (3, 0, 1, 2):
                settle(p)
            for p in range(4):
                columns = pl.ds(p * D, D)
                new = adam_update(
                    old_v[0, :, columns], old_v[1, :, columns], old_v[2, :, columns], whole[:, columns],
                    0.03, 0.1,
                )
                for n in range(3):
                    old_v[n, :, columns] = new[n]
            results = [
                pltpu.make_async_copy(old_v.at[n], target, in_sem.at[n])
                for n, target in enumerate((attn_new, first_new, second_new))
            ]
            for copy in results:
                copy.start()
            for copy in results:
                copy.wait()
            for i in range(images):
                result(i).wait()
            pltpu.make_async_copy(g_low, mixed, in_sem.at[5]).wait()

        pl.run_scoped(
            through_attention,
            pltpu.VMEM((images, PAD, D), BF16),
            pltpu.VMEM((images, PAD, 3 * D), BF16),
            pltpu.VMEM((images, D, PAD), BF16),
            pltpu.VMEM((images, D, PAD), BF16),
            pltpu.VMEM((images, PAD, 3 * D), BF16),
            pltpu.VMEM((4, shards, rows, D), BF16),
            pltpu.VMEM((4, shards, half, D), BF16),
            pltpu.VMEM((4, lines, COLUMNS, quarter, D), BF16),
            pltpu.VMEM((4, lines, quarter, D), BF16),
            pltpu.VMEM((4, lines, quarter, D), F32),
            pltpu.VMEM((images, PAD, D), BF16),
            pltpu.VMEM((3, rows, 4 * D), F32),
            pltpu.VMEM((count_rows, D), BF16),
        )

    pl.run_scoped(
        backward,
        pltpu.VMEM((images, PAD, D), BF16),
        pltpu.VMEM((images, PAD, D), F32),
        pltpu.VMEM((images, PAD, D), BF16),
    )

    to_mate.wait_send()
    for e in range(local):
        settle_weights(e)
        if e not in SUM_FIRST:
            for k in range(2):
                cross_sum(e, k).wait_send()
    for k in range(2):
        to_result(3, k).wait()


def block(shards, capacity, route, comb, attn, tok, cot, expw, attn_state, vec_state, group):
    lines = shards // COLUMNS
    images = tok.shape[0]
    local, _, rows, ff = expw.shape
    slots = -(-capacity // 128) * 128
    half, quarter = rows // 2, rows // 4
    wide = images * PAD
    count_rows = images * SENT
    dma = pltpu.SemaphoreType.DMA
    regular = pltpu.SemaphoreType.REGULAR
    vm = pl.BlockSpec(memory_space=pltpu.VMEM)
    hbm = pl.BlockSpec(memory_space=pl.ANY)
    shape = jax.ShapeDtypeStruct
    states = [shape(a.shape, F32) for a in vec_state]
    attn_states = [shape(a.shape, F32) for a in attn_state]
    last = lines - 1
    outs = pl.pallas_call(
        functools.partial(block_kernel, shards, lines, slots),
        out_shape=states + [
            shape((group, images, SENT, D), BF16),
            shape((group, images, SENT, D), BF16),
            shape((local, 2, shards, rows, ff), BF16),
            shape((images, PAD, D), F32),
            shape((images, PAD, 3 * D), BF16),
            shape((images, D, PAD), BF16),
            shape((images, D, PAD), BF16),
            shape((count_rows, D), F32),
            shape((count_rows, D), BF16),
            shape((count_rows, D), BF16),
            shape((count_rows, D), BF16),
            shape((4, count_rows, D), BF16),
            shape((3, count_rows, D), BF16),
            shape((local, 2, rows, ff), F32),
            shape((images, PAD, D), BF16),
            shape((images, PAD, D), BF16),
        ] + attn_states,
        in_specs=[vm] * 6 + [hbm] * 6,
        out_specs=[vm] * 3 + [hbm] * 19,
        scratch_shapes=[
            pltpu.VMEM(attn.shape, BF16),
            pltpu.VMEM((8, 128), F32),
            pltpu.VMEM((shards,) + attn.shape, BF16),
            pltpu.VMEM((group, 8, wide), jnp.int32),
            pltpu.VMEM((group, 8, wide), F32),
            pltpu.VMEM((shards, 8, 128), F32),
            pltpu.VMEM((group * local, wide), F32),
            pltpu.VMEM((group * local, wide), jnp.int32),
            pltpu.VMEM((group * local, wide), F32),
            pltpu.VMEM((3, 2, shards, rows, ff), BF16),
            pltpu.VMEM((2, 2, lines, rows, ff), BF16),
            pltpu.VMEM((2, 2, rows, ff), BF16),
            pltpu.VMEM((2, rows, ff), BF16),
            pltpu.VMEM((2, 2, last, 2, rows, ff), BF16),
            pltpu.VMEM((2, 2, 2, rows, ff), BF16),
            pltpu.VMEM((2, rows, ff), F32),
            pltpu.VMEM((4, shards, half, D), BF16),
            pltpu.VMEM((4, shards, quarter, D), BF16),
            pltpu.VMEM((4, lines, quarter, D), BF16),
            pltpu.VMEM((4, lines, quarter, D), BF16),
            pltpu.VMEM((rows, 4 * D), F32),
            pltpu.VMEM((8, D), F32),
            pltpu.VMEM((3, 8, D), F32),
            pltpu.VMEM((3, 8, D), F32),
            pltpu.VMEM((lines, 8, D), F32),
            dma((shards,)), dma((shards,)), dma((shards,)), dma((shards,)),
            dma((2,)), dma((3, 2)), dma((group, 2)),
            dma((6,)), dma((images, 3)), dma((images, 3)), dma((5,)),
            dma((2 * local, lines)), dma((2 * local, lines)), dma((2 * local, lines)), dma((2 * local, lines)),
            dma((local, lines)), dma((local, lines)),
            dma((images, 5)), dma((8,)), dma((3,)), dma((shards,)), dma((2,)),
            dma((2, 2)), dma((2, 2)), dma((2, 2)), dma((2, 2)),
            dma((2,)), dma((2, last)), dma((2,)), dma((2, last)),
            regular((2,)), regular((2,)),
            dma((3,)), dma((3,)), dma((3,)), dma((3,)),
            dma((4, 2)), dma((4, 2)), dma((4, 2)), dma((4, last)), dma((4, lines)),
            dma((4, 3)), dma((4, 3)), dma((3, 2)), dma((last,)), dma((lines,)),
        ],
        compiler_params=pltpu.CompilerParams(
            collective_id=0, has_side_effects=True, vmem_limit_bytes=VMEM_LIMIT
        ),
    )(route, comb, attn, *vec_state, tok, cot, expw, *attn_state)
    vec_new, grads, mixed, grad_tok, attn_new = outs[:3], outs[16], outs[17], outs[18], outs[19:]
    return mixed, grad_tok, grads, attn_new, vec_new


def by_image(rows):
    images = rows.shape[0] // SEQ
    return jnp.pad(rows.reshape((images, SEQ) + rows.shape[1:]), ((0, 0), (0, PAD - SEQ), (0, 0)))


def as_lanes(table, fill):
    images = table.shape[0] // SEQ
    wide = table.T.reshape(TOP, images, SEQ)
    wide = jnp.pad(wide, ((0, 8 - TOP), (0, 0), (0, PAD - SEQ)), constant_values=fill)
    return wide.reshape(8, images * PAD)


def to_tokens(rows, count):
    return rows[:, :SEQ].reshape(count, D)


def chip_body(shards, group):
    def run(
        tokens, cotangent, routes, combine, attn_master, attn_first, attn_second,
        vector_master, vector_first, vector_second, expert_master, expert_first, expert_second,
    ):
        count = tokens.shape[0]
        experts = expert_master.shape[2] * group
        capacity = max(2, 4 * count // experts)
        shard = jnp.transpose(expert_master.astype(BF16), (2, 1, 0, 3))
        mixed, grad_tokens, grads, attn_new, vec_new = block(
            shards, capacity, as_lanes(routes, -1), as_lanes(combine, 0.0), attn_master,
            by_image(tokens), by_image(cotangent), shard,
            [attn_master, attn_first, attn_second], [vector_master, vector_first, vector_second], group,
        )
        gradient = with_layout_constraint(jnp.transpose(grads, (2, 1, 0, 3)), Layout((0, 1, 2, 3)))
        expert_new = adam_update(expert_master, expert_first, expert_second, gradient, 0.02, 0.1)
        return (to_tokens(mixed, count), to_tokens(grad_tokens, count), *attn_new, *vec_new, *expert_new)

    return run


def gelu_slope(preact):
    return (
        0.5 * (1.0 + lax.erf(preact * 0.7071067811865476))
        + preact * jnp.exp(-0.5 * preact * preact) * 0.3989422804014327
    )


def slot_places(routes, experts):
    flat_routes = routes.reshape(-1)
    onehot = (flat_routes[:, None] == jnp.arange(experts, dtype=jnp.int32)[None, :]).astype(
        jnp.int32
    )
    before = jnp.cumsum(onehot, axis=0) - onehot
    return jnp.sum(before * onehot, axis=1)


def general_body(
    tokens,
    cotangent,
    routes,
    combine,
    attn_master,
    attn_first,
    attn_second,
    vector_master,
    vector_first,
    vector_second,
    expert_master,
    expert_first,
    expert_second,
):
    group_size = lax.axis_size("expert")
    local_experts = expert_master.shape[2]
    experts = local_experts * group_size
    token_count = tokens.shape[0]
    capacity = max(2, 4 * token_count // experts)
    images = token_count // SEQ
    score_scale = HEAD_DIM ** (-0.5)
    attn_weight, vector_weight, expert_weight = (
        lax.all_gather(attn_master.astype(jnp.bfloat16), "dp", axis=0, tiled=True),
        lax.all_gather(vector_master.astype(jnp.bfloat16), "dp", axis=1, tiled=True),
        lax.all_gather(expert_master.astype(jnp.bfloat16), "dp", axis=0, tiled=True),
    )
    vectors = vector_weight.astype(jnp.float32)
    w_packed = attn_weight[:, : 3 * D]
    w_project = attn_weight[:, 3 * D :]
    inputs = tokens.astype(jnp.float32)
    normed_one, inverse_one = normalize(inputs)
    lowered_one = (normed_one * vectors[0] + vectors[1]).astype(jnp.bfloat16)
    packed = jnp.dot(lowered_one, w_packed, preferred_element_type=jnp.float32).astype(jnp.bfloat16)
    packed = packed.reshape(images, SEQ, 3, HEADS, HEAD_DIM)
    queries = packed[:, :, 0]
    keys_all = packed[:, :, 1]
    values_all = packed[:, :, 2]
    scores = (
        jnp.einsum("bqhc,bkhc->bhqk", queries, keys_all, preferred_element_type=jnp.float32)
        * score_scale
    )
    softmax_out = jax.nn.softmax(scores, axis=-1)
    softmax_low = softmax_out.astype(jnp.bfloat16)
    attended = jnp.einsum(
        "bhqk,bkhc->bqhc", softmax_low, values_all, preferred_element_type=jnp.float32
    )
    attended = attended.reshape(token_count, D).astype(jnp.bfloat16)
    middle = inputs + jnp.dot(attended, w_project, preferred_element_type=jnp.float32) + vectors[4]
    normed_two, inverse_two = normalize(middle)
    mixed_in = (normed_two * vectors[2] + vectors[3]).astype(jnp.bfloat16)
    slot_index = routes.reshape(-1) * capacity + slot_places(routes, experts)

    def dispatch(slot_rows):
        filled = jnp.zeros((experts * capacity, D), jnp.bfloat16).at[slot_index].set(slot_rows)
        return filled.reshape(group_size, local_experts, capacity, D)

    def collect(returned):
        picked = returned.reshape(experts * capacity, D)[slot_index]
        return picked.reshape(token_count, TOP, D).astype(jnp.float32)

    received = lax.all_to_all(
        dispatch(jnp.repeat(mixed_in, TOP, axis=0)),
        "expert",
        split_axis=0,
        concat_axis=0,
        tiled=True,
    )
    produced = []
    for expert_item in range(local_experts):
        arrived = received[:, expert_item].reshape(group_size * capacity, D)
        preact = jnp.dot(
            arrived, expert_weight[:, 0, expert_item], preferred_element_type=jnp.float32
        )
        hidden = jax.nn.gelu(preact, approximate=False).astype(jnp.bfloat16)
        output_rows = contract_last(hidden, expert_weight[:, 1, expert_item]).astype(jnp.bfloat16)
        produced.append(output_rows.reshape(group_size, capacity, D))
    returned = lax.all_to_all(
        jnp.stack(produced, 1), "expert", split_axis=0, concat_axis=0, tiled=True
    )
    mixed = middle + jnp.sum(combine[:, :, None] * collect(returned), axis=1)
    grad_out = cotangent.astype(jnp.float32)
    slot_grads = (
        (combine[:, :, None] * grad_out[:, None, :])
        .reshape(token_count * TOP, D)
        .astype(jnp.bfloat16)
    )
    grads_in = lax.all_to_all(
        dispatch(slot_grads), "expert", split_axis=0, concat_axis=0, tiled=True
    )
    sent_back = []
    shards = []
    for expert_item in range(local_experts):
        arrived = received[:, expert_item].reshape(group_size * capacity, D)
        arrived_grad = grads_in[:, expert_item].reshape(group_size * capacity, D)
        w_in = expert_weight[:, 0, expert_item]
        w_out = expert_weight[:, 1, expert_item]
        preact = jnp.dot(arrived, w_in, preferred_element_type=jnp.float32)
        hidden = jax.nn.gelu(preact, approximate=False).astype(jnp.bfloat16)
        grad_hidden = jnp.dot(arrived_grad, w_out, preferred_element_type=jnp.float32)
        grad_pre = (grad_hidden * gelu_slope(preact)).astype(jnp.bfloat16)
        sent_back.append(
            contract_last(grad_pre, w_in).astype(jnp.bfloat16).reshape(group_size, capacity, D)
        )
        full_grad = jnp.stack(
            [contract_rows(arrived, grad_pre), contract_rows(arrived_grad, hidden)], 1
        )
        shards.append(lax.psum_scatter(full_grad, "dp", scatter_dimension=0, tiled=True))
    expert_grad = jnp.stack(shards, 2)
    returned_grads = lax.all_to_all(
        jnp.stack(sent_back, 1), "expert", split_axis=0, concat_axis=0, tiled=True
    )
    grad_mixed = jnp.sum(collect(returned_grads), axis=1)
    grad_gain_two = jnp.sum(grad_mixed * normed_two, axis=0)
    grad_shift_two = jnp.sum(grad_mixed, axis=0)
    grad_middle = grad_out + norm_back(grad_mixed * vectors[2], normed_two, inverse_two)
    middle_low = grad_middle.astype(jnp.bfloat16)
    grad_project = contract_rows(attended, middle_low)
    grad_attended = (
        contract_last(middle_low, w_project)
        .astype(jnp.bfloat16)
        .reshape(images, SEQ, HEADS, HEAD_DIM)
    )
    grad_soft = jnp.einsum(
        "bqhc,bkhc->bhqk", grad_attended, values_all, preferred_element_type=jnp.float32
    )
    grad_scores = (
        softmax_out * (grad_soft - jnp.sum(softmax_out * grad_soft, axis=-1, keepdims=True))
    ).astype(jnp.bfloat16)
    grad_queries = (
        jnp.einsum("bhqk,bkhc->bqhc", grad_scores, keys_all, preferred_element_type=jnp.float32)
        * score_scale
    )
    grad_keys = (
        jnp.einsum("bhqk,bqhc->bkhc", grad_scores, queries, preferred_element_type=jnp.float32)
        * score_scale
    )
    grad_values = jnp.einsum(
        "bhqk,bqhc->bkhc", softmax_low, grad_attended, preferred_element_type=jnp.float32
    )
    grad_packed = (
        jnp.stack([grad_queries, grad_keys, grad_values], 2)
        .reshape(token_count, 3 * D)
        .astype(jnp.bfloat16)
    )
    grad_weight_packed = contract_rows(lowered_one, grad_packed)
    grad_lowered = contract_last(grad_packed, w_packed)
    grad_gain_one = jnp.sum(grad_lowered * normed_one, axis=0)
    grad_shift_one = jnp.sum(grad_lowered, axis=0)
    grad_tokens = grad_middle + norm_back(grad_lowered * vectors[0], normed_one, inverse_one)
    attn_grad = jnp.concatenate([grad_weight_packed, grad_project], axis=1)
    vector_grad = jnp.stack(
        [
            grad_gain_one,
            grad_shift_one,
            grad_gain_two,
            grad_shift_two,
            jnp.sum(grad_middle, axis=0),
        ],
        0,
    )
    attn_whole, vector_whole = lax.psum((attn_grad, vector_grad), "expert")
    attn_part, vector_part = (
        lax.psum_scatter(attn_whole, "dp", scatter_dimension=0, tiled=True),
        lax.psum_scatter(vector_whole, "dp", scatter_dimension=1, tiled=True),
    )
    attn_new = adam_update(attn_master, attn_first, attn_second, attn_part, 0.03, 0.1)
    vector_new = adam_update(vector_master, vector_first, vector_second, vector_part, 0.2, 0.0)
    expert_new = adam_update(expert_master, expert_first, expert_second, expert_grad, 0.02, 0.1)
    return (
        mixed.astype(jnp.bfloat16),
        grad_tokens.astype(jnp.bfloat16),
        attn_new[0],
        attn_new[1],
        attn_new[2],
        vector_new[0],
        vector_new[1],
        vector_new[2],
        expert_new[0],
        expert_new[1],
        expert_new[2],
    )


def solution(mesh):
    shards, group = mesh.shape["dp"], mesh.shape["expert"]
    chips = shards == 4 * COLUMNS and group == 2 * CORES
    body = chip_body(shards, group) if chips else general_body
    return jax.shard_map(
        body,
        mesh=mesh,
        in_specs=(
            P(("dp", "expert"), None),
            P(("dp", "expert"), None),
            P(("dp", "expert"), None),
            P(("dp", "expert"), None),
            P("dp", None),
            P("dp", None),
            P("dp", None),
            P(None, "dp"),
            P(None, "dp"),
            P(None, "dp"),
            P("dp", None, "expert", None),
            P("dp", None, "expert", None),
            P("dp", None, "expert", None),
        ),
        out_specs=(
            P(("dp", "expert"), None),
            P(("dp", "expert"), None),
            P("dp", None),
            P("dp", None),
            P("dp", None),
            P(None, "dp"),
            P(None, "dp"),
            P(None, "dp"),
            P("dp", None, "expert", None),
            P("dp", None, "expert", None),
            P("dp", None, "expert", None),
        ),
        check_vma=False,
    )
```

```python
import functools

import jax
import jax.numpy as jnp
from jax import lax
from jax.experimental import pallas as pl
from jax.experimental.pallas import tpu as pltpu
from jax.sharding import PartitionSpec as P

D = 512
HEADS = 8
HEAD_DIM = 64
SEQ = 197
TOP = 2
STEP = 10
PAD = 256
SENT = 208
CORES = 2
COLUMNS = 2

LN_EPS = 1e-06
BETA_ONE = 0.9
BETA_TWO = 0.999
ADAM_EPS = 1e-08
MESH = pl.DeviceIdType.MESH
F32 = jnp.float32
BF16 = jnp.bfloat16
VMEM_LIMIT = 63 * 1024 * 1024


def dot(left, right):
    return jnp.dot(left, right, preferred_element_type=F32)


def contract_rows(left, right):
    return lax.dot_general(
        left, right, (((0,), (0,)), ((), ())), preferred_element_type=F32
    )


def contract_last(left, right):
    return lax.dot_general(
        left, right, (((1,), (1,)), ((), ())), preferred_element_type=F32
    )


def normalize(values):
    centered = values - jnp.mean(values, axis=-1, keepdims=True)
    inverse = lax.rsqrt(jnp.mean(centered * centered, axis=-1, keepdims=True) + LN_EPS)
    return (centered * inverse, inverse)


def norm_back(grad_normed, normed, inverse):
    first_mean = jnp.mean(grad_normed, axis=-1, keepdims=True)
    second_mean = jnp.mean(grad_normed * normed, axis=-1, keepdims=True)
    return inverse * (grad_normed - first_mean - normed * second_mean)


def remote(source, target, send_sem, recv_sem, device):
    return pltpu.make_async_remote_copy(
        src_ref=source,
        dst_ref=target,
        send_sem=send_sem,
        recv_sem=recv_sem,
        device_id=device,
        device_id_type=MESH,
    )


def greet(devices):
    barrier = pltpu.get_barrier_semaphore()
    for device in devices:
        pl.semaphore_signal(barrier, inc=1, device_id=device, device_id_type=MESH)
    pl.semaphore_wait(barrier, len(devices))


def softmax_rows(query, key_rows, half, lane):
    own = jnp.where(lane // HEAD_DIM == half, query, jnp.zeros_like(query))
    scores = contract_last(own, key_rows) * HEAD_DIM ** (-0.5)
    column = lax.broadcasted_iota(jnp.int32, scores.shape, 1)
    scores = jnp.where(column < SEQ, scores, -1e30)
    powers = jnp.exp(scores - jnp.max(scores, axis=-1, keepdims=True))
    return powers * (1.0 / jnp.sum(powers, axis=-1, keepdims=True))


def gelu_parts(preact):
    size = jnp.abs(preact)
    below = 1.0 + 0.23164189 * size
    inner = pl.reciprocal(below, approx=True)
    inner = inner * (2.0 - below * inner)
    series = inner * (
        0.127414796
        + inner * (-0.142248368 + inner * (0.7107068705 + inner * (-0.7265760135 + inner * 0.5307027145)))
    )
    bell = jnp.exp(-0.5 * preact * preact)
    tail = series * bell
    area = jnp.where(preact >= 0.0, 1.0 - tail, tail)
    return preact * area, area + preact * bell * 0.3989422804014327


def adam_update(master, first, second, gradient, step_rate, decay_rate):
    first = BETA_ONE * first + (1.0 - BETA_ONE) * gradient
    second = BETA_TWO * second + (1.0 - BETA_TWO) * gradient * gradient
    first_hat = first / (1.0 - BETA_ONE**STEP)
    second_hat = second / (1.0 - BETA_TWO**STEP)
    master = master - step_rate * (
        first_hat / (jnp.sqrt(second_hat) + ADAM_EPS) + decay_rate * master
    )
    return (master, first, second)


ROUTE_FIRST = ()
SUM_FIRST = (0, 1)
CHAINS = (0, 1, 2, 3)


def block_kernel(
    shards, lines, slots,
    route, comb, vec_old, vec_first_old, vec_second_old,
    tok, cot, expw, attn_old,
    vec_new, vec_first_new, vec_second_new,
    u_all, g_all, wfull, middle, qkv, att_t, low_t, attn_full, own_out, d_mate, d_corner, d_over, y_stage, y_got,
    grads, mixed, grad_tok, attn_grad,
    attn, vec, route_all, comb_all, vslots, chosen, place, shares,
    gst, xr, xo, xst, zr, zs, fin,
    part_a, part_b, part_c, part_d, whole, v_sum, v_stage, v_got, v_lines,
    attn_send, attn_recv, vec_send, vec_recv, pass_sem, table_send, table_recv,
    g_sem, u_send, u_recv, own_sem, up_send, up_recv, down_send, down_recv, x_send, x_recv,
    out_sem, in_sem, load_sem, w_sem, fin_sem,
    rx_send, rx_recv, ro_send, ro_recv, ru_send, ru_recv, rd_send, rd_recv, credit_up, credit_down,
    back_send, back_recv, y_send, y_recv,
    a_sem, b_sem, c_sem, d_send, d_recv, e_send, e_recv, v_sem, vd_send, vd_recv,
):
    dp, me = lax.axis_index("dp"), lax.axis_index("expert")
    z, x = dp // COLUMNS, dp % COLUMNS
    y, core = me // CORES, me % CORES
    group, images = u_all.shape[:2]
    local, _, rows, ff = expw.shape
    last = lines - 1
    half, quarter = rows // 2, rows // 4
    tile = 512
    tiles = ff // tile
    mate_s, over_s, corner_s = y * CORES + 1 - core, (1 - y) * CORES + core, (1 - y) * CORES + 1 - core
    mate, over, corner = (dp, mate_s), (dp, over_s), (dp, corner_s)
    above = (lax.rem(z + 1, lines) * COLUMNS + x, me)
    below = (lax.rem(z + last, lines) * COLUMNS + x, me)
    beside = (z * COLUMNS + 1 - x, me)
    along = [(lax.rem(z + k, lines) * COLUMNS + x, me) for k in range(1, lines)]
    peers = [(lax.rem(dp + k, shards), me) for k in range(1, shards)]
    sources = [lax.rem(dp + shards - k, shards) for k in range(1, shards)]
    partners = (mate, over, corner)
    early = pltpu.make_async_copy(attn_old, whole, in_sem.at[0])
    early.start()
    greet(peers + list(partners))
    early.wait()
    mine = pl.ds(pl.multiple_of(core * half, half), half)
    theirs = pl.ds(pl.multiple_of((1 - core) * half, half), half)
    sent_images = pl.ds(0, SENT)

    attn[...] = whole[...].astype(BF16)
    vec[...] = jnp.zeros_like(vec)
    vec[: vec_old.shape[0], : vec_old.shape[1]] = vec_old[...]
    for k, peer in enumerate(peers):
        remote(attn.at[mine], gst.at[1, 0, dp, mine], attn_send.at[k], attn_recv.at[dp], peer).start()
        remote(vec, vslots.at[dp], vec_send.at[k], vec_recv.at[dp], peer).start()
    for k, partner in enumerate(partners):
        remote(route, route_all.at[me], table_send.at[k, 0], table_recv.at[me, 0], partner).start()
        remote(comb, comb_all.at[me], table_send.at[k, 1], table_recv.at[me, 1], partner).start()

    def held(e, chain, at):
        column = x if chain == 0 else 1 - x
        return wfull.at[e, :, at * COLUMNS + column]

    def up(e, chain, hop, ref):
        return remote(ref, ref, up_send.at[e * 2 + chain, hop], up_recv.at[e * 2 + chain, hop], above)

    def down(e, chain, hop, ref):
        return remote(ref, ref, down_send.at[e * 2 + chain, hop], down_recv.at[e * 2 + chain, hop], below)

    def across(e, at, ref):
        return remote(ref, ref, x_send.at[e, at], x_recv.at[e, at], beside)

    def start_own(e):
        target = held(e, 0, z)
        remote(expw.at[e], target, x_send.at[e, z], x_recv.at[e, z], beside).start()

        @pl.when(z < last)
        def _():
            remote(expw.at[e], target, up_send.at[e * 2, 0], up_recv.at[e * 2, 0], above).start()

        @pl.when(z > 0)
        def _():
            remote(expw.at[e], target, down_send.at[e * 2, 0], down_recv.at[e * 2, 0], below).start()

    def start_other(e):
        ref = held(e, 1, z)
        across(e, z, ref).wait_recv()

        @pl.when(z < last)
        def _():
            up(e, 1, 0, ref).start()

        @pl.when(z > 0)
        def _():
            down(e, 1, 0, ref).start()

    def hand_on(e, chain, hop):
        cross = e not in ROUTE_FIRST
        from_below = jnp.maximum(z - 1 - hop, 0)
        from_above = jnp.minimum(z + 1 + hop, last)

        @pl.when(z - 1 - hop >= 0)
        def _():
            ref = held(e, chain, from_below)
            up(e, chain, hop, ref).wait_recv()

            @pl.when(z < last)
            def _():
                up(e, chain, hop + 1, ref).start()

            if cross:
                across(e, from_below, ref).start()

        @pl.when(z + 1 + hop <= last)
        def _():
            ref = held(e, chain, from_above)
            down(e, chain, hop, ref).wait_recv()

            @pl.when(z > 0)
            def _():
                down(e, chain, hop + 1, ref).start()

            if cross:
                across(e, from_above, ref).start()

    def weights_here(e):
        if e not in ROUTE_FIRST:
            for at in range(lines):
                across(e, at, held(e, 1, at)).wait_recv()

    def settle_weights(e):
        ref = held(e, 0, z)
        for chain in range(2 if e in ROUTE_FIRST else 1):
            for hop in range(last):
                @pl.when(jnp.logical_and(z - hop >= 0, z < last))
                def _():
                    up(e, chain, hop, ref).wait_send()

                @pl.when(jnp.logical_and(z + hop <= last, z > 0))
                def _():
                    down(e, chain, hop, ref).wait_send()

        if e in ROUTE_FIRST:
            across(e, z, ref).wait_send()
        else:
            for at in range(lines):
                across(e, at, ref).wait_send()

    start_own(0)
    start_own(1)
    g_own = cot.at[:, sent_images]
    g_mine = g_all.at[me]
    remote(g_own, g_mine, g_sem.at[0], g_sem.at[1], mate).start()
    remote(g_own, g_mine, g_sem.at[2], g_sem.at[3], over).start()

    gst[1, 0, dp, mine] = attn[mine]
    vslots[dp] = vec[...]
    route_all[me] = route[...]
    comb_all[me] = comb[...]

    for k, partner in enumerate(partners):
        source = partner[1]
        remote(route, route_all.at[source], table_send.at[k, 0], table_recv.at[source, 0], partner).wait()
        remote(comb, comb_all.at[source], table_send.at[k, 1], table_recv.at[source, 1], partner).wait()
    for s in range(group):
        for el in range(local):
            named = me * local + el
            row = s * local + el
            hits = [route_all[s, t : t + 1, :] == named for t in range(TOP)]
            chosen[row : row + 1, :] = sum(jnp.where(h, 1.0, 0.0) for h in hits)
            shares[row : row + 1, :] = sum(
                jnp.where(h, comb_all[s, t : t + 1, :], 0.0) for t, h in enumerate(hits)
            )
    earlier = lax.broadcasted_iota(jnp.int32, (PAD, PAD), 0) < lax.broadcasted_iota(
        jnp.int32, (PAD, PAD), 1
    )
    earlier = jnp.where(earlier, 1.0, 0.0).astype(BF16)
    count = jnp.zeros((group * local, 1), F32)
    for i in range(images):
        block = chosen[:, i * PAD : (i + 1) * PAD]
        position = count + dot(block.astype(BF16), earlier)
        place[:, i * PAD : (i + 1) * PAD] = jnp.where(block > 0.0, position, -1.0).astype(jnp.int32)
        count = count + jnp.sum(block, axis=1, keepdims=True)

    for k, (peer, source) in enumerate(zip(peers, sources)):
        remote(attn.at[mine], gst.at[1, 0, source, mine], attn_send.at[k], attn_recv.at[source], peer).wait()
        remote(vec, vslots.at[source], vec_send.at[k], vec_recv.at[source], peer).wait()
    to_mate = remote(gst.at[1, 0, :, mine], gst.at[1, 0, :, mine], pass_sem.at[0], pass_sem.at[1], mate)
    to_mate.start()
    lane = lax.broadcasted_iota(jnp.int32, (128, D), 1)
    entry = lax.broadcasted_iota(jnp.int32, (128, D), 0)
    width = D // shards
    vectors = jnp.zeros((8, D), F32)
    for d in range(shards):
        spread = jnp.where(jnp.logical_and(entry < width, lane == entry + d * width), 1.0, 0.0)
        vectors = vectors + dot(vslots[d].astype(BF16), spread.astype(BF16))
    gain_one, shift_one = vectors[0:1], vectors[1:2]
    gain_two, shift_two, shift_out = vectors[2:3], vectors[3:4], vectors[4:5]
    remote(gst.at[1, 0, :, theirs], gst.at[1, 0, :, theirs], pass_sem.at[0], pass_sem.at[1], mate).wait_recv()
    pair_lane = lax.broadcasted_iota(jnp.int32, (PAD, 2 * HEAD_DIM), 1)

    def u_part(s, i):
        return u_all.at[s, i]

    def u_to(k, s, i, partner):
        return remote(u_part(s, i), u_part(s, i), u_send.at[i, k], u_recv.at[i, k], partner)

    def forward(tok_v, qkv_v, att_v, mid_v, u_v, att_tv, low_tv):
        fetch = pltpu.make_async_copy(tok, tok_v, in_sem.at[0])
        fetch.start()
        fetch.wait()

        def outs(i):
            return (
                pltpu.make_async_copy(u_v.at[i, sent_images], u_all.at[me, i], out_sem.at[i, 0]),
                pltpu.make_async_copy(qkv_v.at[i], qkv.at[i], out_sem.at[i, 1]),
                pltpu.make_async_copy(mid_v.at[i], middle.at[i], out_sem.at[i, 2]),
                pltpu.make_async_copy(att_tv.at[i], att_t.at[i], out_sem.at[i, 3]),
                pltpu.make_async_copy(low_tv.at[i], low_t.at[i], out_sem.at[i, 4]),
            )

        def send_image(i):
            outs(i)[0].wait()
            u_to(0, me, i, over).start()
            u_to(1, me, i, mate).start()

        def one_image(i, carry):
            inputs = tok_v[i].astype(F32)
            normed, _ = normalize(inputs)
            lowered = (normed * gain_one + shift_one).astype(BF16)
            for part in range(3):
                columns = pl.ds(part * D, D)
                qkv_v[i, :, columns] = dot(lowered, gst[1, 0, :, :, columns].reshape(D, D)).astype(BF16)
            for pair in range(HEADS // 2):
                offset = pair * 2 * HEAD_DIM
                query = qkv_v[i, :, offset : offset + 128]
                key_rows = qkv_v[i, :, D + offset : D + offset + 128]
                value = qkv_v[i, :, 2 * D + offset : 2 * D + offset + 128]
                results = []
                for which in range(2):
                    probs = softmax_rows(query, key_rows, which, pair_lane)
                    results.append(dot(probs.astype(BF16), value))
                joined = jnp.where(pair_lane < HEAD_DIM, results[0], results[1])
                att_v[i, :, offset : offset + 128] = joined.astype(BF16)
            mid = inputs + dot(att_v[i], gst[1, 0, :, :, 3 * D :].reshape(D, D)) + shift_out
            mid_v[i] = mid
            normed_two, _ = normalize(mid)
            u_v[i] = (normed_two * gain_two + shift_two).astype(BF16)
            att_tv[i] = att_v[i].T
            low_tv[i] = lowered.T
            for copy in outs(i):
                copy.start()

            @pl.when(i > 0)
            def _():
                send_image(i - 1)

            for turn, actions in enumerate((
                (lambda: start_own(2),),
                (lambda: hand_on(0, 0, 1),),
                (lambda: hand_on(1, 0, 0),),
                (lambda: hand_on(0, 0, 2),),
                (lambda: hand_on(1, 0, 1), lambda: start_own(3)),
            )):
                @pl.when(i == turn)
                def _():
                    for action in actions:
                        action()

            return carry

        hand_on(0, 0, 0)
        lax.fori_loop(0, images, one_image, 0)
        send_image(images - 1)
        for i in range(images):
            for copy in outs(i)[1:]:
                copy.wait()

    pl.run_scoped(
        forward,
        pltpu.VMEM((images, PAD, D), BF16),
        pltpu.VMEM((images, PAD, 3 * D), BF16),
        pltpu.VMEM((images, PAD, D), BF16),
        pltpu.VMEM((images, PAD, D), F32),
        pltpu.VMEM((images, PAD, D), BF16),
        pltpu.VMEM((images, D, PAD), BF16),
        pltpu.VMEM((images, D, PAD), BF16),
    )
    keep_attn = pltpu.make_async_copy(gst.at[1, 0], attn_full, own_sem.at[0])
    keep_attn.start()
    g_over = g_all.at[over_s]
    remote(g_over, g_over, g_sem.at[2], g_sem.at[3], over).wait()
    remote(g_over, g_over, g_sem.at[4], g_sem.at[5], mate).start()
    g_mate = g_all.at[mate_s]
    remote(g_mate, g_mate, g_sem.at[0], g_sem.at[1], mate).wait()
    g_corner = g_all.at[corner_s]
    remote(g_corner, g_corner, g_sem.at[4], g_sem.at[5], mate).wait()

    to_mate.wait_send()
    keep_attn.wait()

    def slot_of(e):
        return e % 2 if e < local - 1 else 2

    def cross_sum(e, k):
        return remote(
            gst.at[slot_of(e), k, pl.ds(lines, lines)], xr.at[e % 2, k],
            rx_send.at[e % 2, k], rx_recv.at[e % 2, k], beside,
        )

    def swap(e, k):
        return remote(xst.at[k], xo.at[e % 2, k], ro_send.at[e % 2, k], ro_recv.at[e % 2, k], beside)

    def partial(e, k, owner, which):
        value = gst[slot_of(e), k, which * lines + owner].astype(F32)
        if e not in SUM_FIRST:
            value = value + xr[e % 2, k, owner].astype(F32)
        return value

    def z_send(e, k, way, hop):
        sent, landed = zs.at[k, way], zr.at[k, way, hop]
        if e not in SUM_FIRST:
            sent, landed = sent.at[0], landed.at[0]
        if way == 0:
            return remote(sent, landed, ru_send.at[k], ru_recv.at[k, hop], above)
        return remote(sent, landed, rd_send.at[k], rd_recv.at[k, hop], below)

    def one_hop(e, k, hop, way):
        ahead = z if way == 0 else last - z
        owner = jnp.minimum(z + last - hop, last) if way == 0 else jnp.maximum(z - last + hop, 0)
        credit = (credit_up, credit_down)[way]
        both = range(2 if e in SUM_FIRST else 1)

        @pl.when(jnp.logical_and(ahead <= hop, ahead < last))
        def _():
            if hop > 0:
                @pl.when(ahead <= hop - 1)
                def _():
                    z_send(e, k, way, hop - 1).wait_send()

            if CHAINS.index(e) > 0:
                @pl.when(ahead == hop)
                def _():
                    pl.semaphore_wait(credit.at[k], 1)

            if hop > 0:
                @pl.when(ahead >= 1)
                def _():
                    z_send(e, k, way, hop - 1).wait_recv()
                    for which in both:
                        total = partial(e, k, owner, which) + zr[k, way, hop - 1, which].astype(F32)
                        zs[k, way, which] = total.astype(BF16)

                @pl.when(ahead < 1)
                def _():
                    for which in both:
                        zs[k, way, which] = partial(e, k, owner, which).astype(BF16)
            else:
                for which in both:
                    zs[k, way, which] = partial(e, k, owner, which).astype(BF16)
            z_send(e, k, way, hop).start()

    def hop_step(e, k, hop):
        if hop == 0 and e not in SUM_FIRST:
            cross_sum(e, k).wait_recv()
        one_hop(e, k, hop, 0)
        one_hop(e, k, hop, 1)

    def to_result(e, k):
        return pltpu.make_async_copy(fin.at[k], grads.at[:, k, e], fin_sem.at[k])

    def finish(e, k):
        turn = CHAINS.index(e)
        if turn > 0:
            to_result(e, k).wait()
        fin[k] = partial(e, k, z, 0)

        @pl.when(z > 0)
        def _():
            z_send(e, k, 0, last - 1).wait_recv()
            fin[k] += zr[k, 0, last - 1, 0].astype(F32)
            z_send(e, k, 1, last - 1).wait_send()

        @pl.when(z < last)
        def _():
            z_send(e, k, 1, last - 1).wait_recv()
            fin[k] += zr[k, 1, last - 1, 0].astype(F32)
            z_send(e, k, 0, last - 1).wait_send()

        if e in SUM_FIRST:
            own = partial(e, k, z, 1)

            @pl.when(z == 0)
            def _():
                xst[k] = (own + zr[k, 1, last - 1, 1].astype(F32)).astype(BF16)

            @pl.when(z == last)
            def _():
                xst[k] = (own + zr[k, 0, last - 1, 1].astype(F32)).astype(BF16)

            @pl.when(jnp.logical_and(z > 0, z < last))
            def _():
                arrived = zr[k, 0, last - 1, 1].astype(F32) + zr[k, 1, last - 1, 1].astype(F32)
                xst[k] = (own + arrived).astype(BF16)

            swap(e, k).start()
        else:
            to_result(e, k).start()
        if turn + 1 < local:
            @pl.when(z > 0)
            def _():
                pl.semaphore_signal(credit_up.at[k], inc=1, device_id=below, device_id_type=MESH)

            @pl.when(z < last)
            def _():
                pl.semaphore_signal(credit_down.at[k], inc=1, device_id=above, device_id_type=MESH)

    def collect(e, k):
        swap(e, k).wait()
        fin[k] += xo[e % 2, k].astype(F32)
        to_result(e, k).start()

    def source_of(e, t):
        r = t if e == local - 1 else group - 1 - t
        across_y = (1 - y) + (r // CORES) * (2 * y - 1)
        return across_y * CORES + (1 - core) + (r % CORES) * (2 * core - 1)

    def experts(ubuf, gbuf, work, x_t, m_t, dacc, made_all, d_stage):
        def load_u(s):
            return pltpu.make_async_copy(u_all.at[s], ubuf.at[:, sent_images], load_sem.at[0])

        def load_g(ref):
            return pltpu.make_async_copy(ref, gbuf.at[:, sent_images], load_sem.at[1])

        def start_load(s):
            load_u(s).start()

            @pl.when(s == me)
            def _():
                load_g(g_own).start()

            @pl.when(s != me)
            def _():
                load_g(g_all.at[s]).start()

        def load_weights(e):
            copies = [pltpu.make_async_copy(expw.at[e], gst.at[2, :, dp], w_sem.at[0])]
            for k, d in enumerate(sources):
                copies.append(pltpu.make_async_copy(wfull.at[e, :, d], gst.at[2, :, d], w_sem.at[k + 1]))
            return copies

        def weight_grad(e, k):
            left = x_t if k == 0 else m_t

            def one_tile(j, carry):
                right = work[tiles * (1 - k) + j]
                block = dot(left[...], right).astype(BF16)
                columns = pl.ds(pl.multiple_of(j * tile, tile), tile)
                for d in range(shards):
                    which = lax.rem(x + d % COLUMNS, COLUMNS)
                    index = which * lines + d // COLUMNS
                    gst[slot_of(e), k, index, :, columns] = block[d * rows : (d + 1) * rows]
                return carry

            lax.fori_loop(0, tiles, one_tile, 0)
            if e not in SUM_FIRST:
                cross_sum(e, k).start()

        def pick_of(s, e, i):
            slot_row = lax.broadcasted_iota(jnp.int32, (slots, PAD), 0)
            return slot_row == place[pl.ds(s * local + e, 1), i * PAD : (i + 1) * PAD]

        def one_source(e, t, after_gather):
            s = source_of(e, t)
            load_u(s).wait()
            load_g(g_own).wait()
            arrived = jnp.zeros((slots, D), F32)
            grad = jnp.zeros((slots, D), F32)
            share = jnp.zeros((slots, 1), F32)
            for i in range(images):
                hit = pick_of(s, e, i)
                pick = jnp.where(hit, 1.0, 0.0).astype(BF16)
                weight = shares[pl.ds(s * local + e, 1), i * PAD : (i + 1) * PAD]
                share += jnp.sum(jnp.where(hit, weight, 0.0), axis=1, keepdims=True)
                arrived += dot(pick, ubuf[i])
                grad += dot(pick, gbuf[i])
            arrived = arrived.astype(BF16)
            grad = (share * grad).astype(BF16)
            here = pl.ds(pl.multiple_of(t * slots, slots), slots)
            x_t[:, here] = arrived.T
            m_t[:, here] = grad.T
            after_gather()

            def one_tile(j, carry):
                columns = pl.ds(pl.multiple_of(j * tile, tile), tile)
                preact = dot(arrived, gst[2, 0, :, :, columns].reshape(D, tile))
                hidden, slope = gelu_parts(preact)
                work[j, here, :] = hidden.astype(BF16)
                grad_hidden = dot(grad, gst[2, 1, :, :, columns].reshape(D, tile))
                work[tiles + j, here, :] = (grad_hidden * slope).astype(BF16)
                return carry

            lax.fori_loop(0, tiles, one_tile, 0)
            made = jnp.zeros((slots, D), F32)
            back = jnp.zeros((slots, D), F32)
            for j in range(tiles):
                columns = pl.ds(j * tile, tile)
                made += contract_last(work[j, here, :], gst[2, 1, :, :, columns].reshape(D, tile))
                back += contract_last(work[tiles + j, here, :], gst[2, 0, :, :, columns].reshape(D, tile))
            made_all[s, e * slots : (e + 1) * slots] = (share * made.astype(BF16).astype(F32)).astype(BF16)
            back = back.astype(BF16)
            for i in range(images):
                pick = jnp.where(pick_of(s, e, i), 1.0, 0.0).astype(BF16)
                placed = contract_rows(pick, back)[:SENT]
                if e == 0:
                    dacc[s, i * SENT : (i + 1) * SENT] = placed
                else:
                    dacc[s, i * SENT : (i + 1) * SENT] += placed

        def next_load(e, t):
            @pl.when(t + 1 < group)
            def _():
                if e == 0:
                    @pl.when(t == 0)
                    def _():
                        for i in range(images):
                            u_to(1, mate_s, i, mate).wait()

                    @pl.when(t == 1)
                    def _():
                        for i in range(images):
                            u_to(0, over_s, i, over).wait()
                            u_to(2, over_s, i, mate).start()

                    @pl.when(t == 2)
                    def _():
                        for i in range(images):
                            u_to(2, corner_s, i, mate).wait()

                start_load(source_of(e, t + 1))

            if e + 1 < local:
                @pl.when(t + 1 == group)
                def _():
                    start_load(source_of(e + 1, 0))

        def to_corner():
            return remote(d_stage.at[0], d_corner, back_send.at[0], back_recv.at[0], mate)

        def to_mate_sum():
            return remote(d_stage.at[1], d_mate, back_send.at[1], back_recv.at[1], mate)

        def to_over():
            return remote(d_stage.at[0], d_over, back_send.at[2], back_recv.at[2], over)

        def sums_corner():
            d_stage[0] = dacc[corner_s].astype(BF16)
            to_corner().start()

        def sums_mate():
            d_stage[1] = dacc[mate_s].astype(BF16)
            to_mate_sum().start()
            to_corner().wait()
            landed = pltpu.make_async_copy(d_corner, d_stage.at[0], load_sem.at[2])
            landed.start()
            landed.wait()
            d_stage[0] = (dacc[over_s] + d_stage[0].astype(F32)).astype(BF16)
            to_over().start()

        plan = {
            (0, 0): (lambda: hand_on(1, 0, 2),),
            (0, 1): (lambda: hand_on(2, 0, 0),),
            (0, 3): (lambda: hand_on(2, 0, 1),),
            (1, 0): (lambda: hand_on(2, 0, 2), lambda: hand_on(3, 0, 0)),
            (1, 1): (lambda: hop_step(0, 0, 1),),
            (1, 2): (lambda: hop_step(0, 1, 1), lambda: hand_on(3, 0, 1)),
            (1, 3): (lambda: hand_on(3, 0, 2),),
            (2, 1): (lambda: finish(0, 0), lambda: hop_step(1, 0, 0)),
            (2, 2): (lambda: finish(0, 1), lambda: hop_step(1, 1, 0)),
            (3, 0): (sums_corner, lambda: collect(0, 0), lambda: collect(0, 1)),
            (3, 2): (sums_mate, lambda: hop_step(1, 0, 2)),
            (3, 3): (lambda: hop_step(1, 1, 2),),
        }
        after_grad = {
            (0, 0): (lambda: hop_step(0, 0, 0),),
            (0, 1): (lambda: hop_step(0, 1, 0),),
            (1, 1): (lambda: hop_step(0, 0, 2), lambda: hop_step(0, 1, 2)),
            (2, 1): (lambda: hop_step(1, 0, 1), lambda: hop_step(1, 1, 1)),
        }

        empty = jnp.zeros((images, PAD - SENT, D), BF16)
        ubuf[:, SENT:, :] = empty
        gbuf[:, SENT:, :] = empty
        start_load(source_of(0, 0))
        for e in range(local):
            weights_here(e)
            copies = load_weights(e)
            for copy in copies:
                copy.start()
            for copy in copies:
                copy.wait()

            def step(t, carry, e=e):
                one_source(e, t, lambda: next_load(e, t))
                for turn in range(group):
                    actions = plan.get((e, turn), ())
                    if actions:
                        @pl.when(t == turn)
                        def _():
                            for action in actions:
                                action()

                return carry

            lax.fori_loop(0, group, step, 0)
            for k in range(2):
                weight_grad(e, k)
                for action in after_grad.get((e, k), ()):
                    action()

        own_sum = pltpu.make_async_copy(dacc.at[me], own_out, own_sem.at[2])
        own_sum.start()

        def one_sum(s, i):
            total = jnp.zeros((PAD, D), F32)
            for e in range(local):
                pick = jnp.where(pick_of(s, e, i), 1.0, 0.0).astype(BF16)
                total += contract_rows(pick, made_all[s, e * slots : (e + 1) * slots])
            return total[:SENT]

        def stage(k):
            return pltpu.make_async_copy(d_stage.at[1], y_stage.at[k], own_sem.at[3])

        to_mate_sum().wait_send()

        for k, (s, partner) in enumerate(zip((mate_s, over_s, corner_s), partners)):
            for i in range(images):
                d_stage[1, i * SENT : (i + 1) * SENT] = one_sum(s, i).astype(BF16)
            stage(k).start()
            stage(k).wait()
            remote(y_stage.at[k], y_got.at[k], y_send.at[k], y_recv.at[k], partner).start()
        for i in range(images):
            d_stage[1, i * SENT : (i + 1) * SENT] = one_sum(me, i).astype(BF16)
        stage(3).start()
        stage(3).wait()
        own_sum.wait()
        to_over().wait_send()

    count_rows = images * SENT
    pl.run_scoped(
        experts,
        pltpu.VMEM((images, PAD, D), BF16),
        pltpu.VMEM((images, PAD, D), BF16),
        pltpu.VMEM((2 * tiles, group * slots, tile), BF16),
        pltpu.VMEM((D, group * slots), BF16),
        pltpu.VMEM((D, group * slots), BF16),
        pltpu.VMEM((group, count_rows, D), F32),
        pltpu.VMEM((group, local * slots, D), BF16),
        pltpu.VMEM((2, count_rows, D), BF16),
    )

    def rows_of(start, size):
        return pl.ds(pl.multiple_of(start, quarter), size)

    kept_y, given_y = rows_of(y * quarter, quarter), rows_of((1 - y) * quarter, quarter)
    final_rows = rows_of(core * half + y * quarter, quarter)

    def backward(g_low, g_mid, d_att, attnw):
        fetch_attn = pltpu.make_async_copy(attn_full, attnw, own_sem.at[0])
        fetch_attn.start()
        for k in range(2):
            finish(1, k)
            hop_step(2, k, 0)
        fetch_attn.wait()
        remote(d_mate, d_mate, back_send.at[1], back_recv.at[1], mate).wait_recv()
        remote(d_over, d_over, back_send.at[2], back_recv.at[2], over).wait_recv()
        v_sum[...] = jnp.zeros_like(v_sum)

        def before_attention(cot_v, mid_v, own_v, mate_v, over_v):
            fetches = [
                pltpu.make_async_copy(source, target, in_sem.at[n])
                for n, (source, target) in enumerate((
                    (cot, cot_v), (middle, mid_v), (own_out, own_v), (d_mate, mate_v), (d_over, over_v),
                ))
            ]
            for fetch in fetches:
                fetch.start()
            for fetch in fetches:
                fetch.wait()

            def one_image(i, carry):
                here = pl.ds(pl.multiple_of(i * SENT, SENT), SENT)
                normed, inverse = normalize(mid_v[i])
                grad = own_v[here] + mate_v[here].astype(F32) + over_v[here].astype(F32)
                grad = jnp.concatenate([grad, jnp.zeros((PAD - SENT, D), F32)], axis=0)
                v_sum[2:3] += jnp.sum(grad * normed, axis=0, keepdims=True)
                v_sum[3:4] += jnp.sum(grad, axis=0, keepdims=True)
                total = cot_v[i].astype(F32) + norm_back(grad * gain_two, normed, inverse)
                v_sum[4:5] += jnp.sum(total, axis=0, keepdims=True)
                g_mid[i] = total
                low = total.astype(BF16)
                g_low[i] = low
                d_att[i] = contract_last(low, attnw[:, :, 3 * D :].reshape(D, D)).astype(BF16)
                return carry

            lax.fori_loop(0, images, one_image, 0)

        pl.run_scoped(
            before_attention,
            pltpu.VMEM((images, PAD, D), BF16),
            pltpu.VMEM((images, PAD, D), F32),
            pltpu.VMEM((count_rows, D), F32),
            pltpu.VMEM((count_rows, D), BF16),
            pltpu.VMEM((count_rows, D), BF16),
        )

        def through_attention(
            tok_v, qkv_v, att_tv, low_tv, part_own, sum_a, sum_b, sum_c, sum_d, got_v,
        ):
            def move_a(p):
                return remote(part_own.at[p, :, theirs], part_a.at[p], a_sem.at[p, 0], a_sem.at[p, 1], mate)

            def move_b(p):
                return remote(sum_a.at[p, :, given_y], part_b.at[p], b_sem.at[p, 0], b_sem.at[p, 1], over)

            def move_c(p):
                return remote(sum_b.at[p, :, 1 - x], part_c.at[p], c_sem.at[p, 0], c_sem.at[p, 1], beside)

            def move_d(p, k):
                target = lax.rem(z + k, lines)
                return remote(
                    sum_c.at[p, target], part_d.at[p, z], d_send.at[p, k - 1], d_recv.at[p, z], along[k - 1]
                )

            def arrived_d(p, k):
                source = lax.rem(z + lines - k, lines)
                return remote(
                    sum_c.at[p, source], part_d.at[p, source], d_send.at[p, k - 1], d_recv.at[p, source],
                    along[k - 1],
                )

            def move_e(p, k):
                own = whole.at[final_rows, pl.ds(p * D, D)]
                return remote(own, own, e_send.at[p, k], e_recv.at[p, k], partners[k])

            def stage_b(p):
                move_a(p).wait()
                sum_a[p] = (part_own[p, :, mine].astype(F32) + part_a[p].astype(F32)).astype(BF16)
                move_b(p).start()

            def stage_c(p):
                move_b(p).wait()
                total = sum_a[p, :, kept_y].astype(F32) + part_b[p].astype(F32)
                sum_b[p] = total.astype(BF16).reshape(lines, COLUMNS, quarter, D)
                move_c(p).start()

            def stage_d(p):
                move_c(p).wait()
                total = sum_b[p, :, x].astype(F32) + part_c[p].astype(F32)
                sum_c[p] = total.astype(BF16)
                sum_d[p] = total
                for k in range(1, lines):
                    move_d(p, k).start()

            def stage_e(p):
                total = sum_d[p, z]
                for k in range(1, lines):
                    arrived_d(p, k).wait_recv()
                    total = total + part_d[p, lax.rem(z + lines - k, lines)].astype(F32)
                whole[final_rows, pl.ds(p * D, D)] = total
                for k in range(3):
                    move_e(p, k).start()

            def settle(p):
                for k in range(1, lines):
                    move_d(p, k).wait_send()
                for k in range(3):
                    move_e(p, k).wait()

            def scatter_part(p, left_t, right):
                block = jnp.zeros((D, D), F32)
                for i in range(images):
                    block += dot(left_t[i], right(i))
                part_own[p] = block.astype(BF16).reshape(shards, rows, D)
                move_a(p).start()

            def block_output():
                for k, partner in enumerate(partners):
                    remote(y_stage.at[k], y_got.at[k], y_send.at[k], y_recv.at[k], partner).wait()
                fetch_output.wait()
                for k in range(4):
                    source = y_stage.at[3] if k == 3 else y_got.at[k]
                    landed = pltpu.make_async_copy(source, got_v, in_sem.at[3])
                    landed.start()
                    landed.wait()
                    for i in range(images):
                        part = got_v[i * SENT : (i + 1) * SENT].astype(F32)
                        if k < 3:
                            g_mid[i, :SENT] += part
                        else:
                            g_low[i, :SENT] = (g_mid[i, :SENT] + part).astype(BF16)
                pltpu.make_async_copy(g_low, mixed, in_sem.at[5]).start()

            fetches = [
                pltpu.make_async_copy(source, target, in_sem.at[n])
                for n, (source, target) in enumerate((
                    (tok, tok_v), (qkv, qkv_v), (att_t, att_tv), (low_t, low_tv),
                ))
            ]
            for fetch in fetches:
                fetch.start()
            for fetch in fetches:
                fetch.wait()
            hop_step(2, 0, 1)
            hop_step(2, 1, 1)
            scatter_part(3, att_tv, lambda i: g_low[i])

            key_index = lax.broadcasted_iota(jnp.int32, (PAD, PAD), 0)

            def result(i):
                return pltpu.make_async_copy(tok_v.at[i], grad_tok.at[i], out_sem.at[i, 0])

            def one_image(i, carry):
                for pair in range(HEADS // 2):
                    offset = pair * 2 * HEAD_DIM
                    query = qkv_v[i, :, offset : offset + 128]
                    key_rows = qkv_v[i, :, D + offset : D + offset + 128]
                    value = qkv_v[i, :, 2 * D + offset : 2 * D + offset + 128]
                    grad = d_att[i, :, offset : offset + 128]
                    results = []
                    for which in range(2):
                        own_half = pair_lane // HEAD_DIM == which
                        scores = contract_last(
                            jnp.where(own_half, key_rows, jnp.zeros_like(key_rows)), query
                        ) * HEAD_DIM ** (-0.5)
                        scores = jnp.where(key_index < SEQ, scores, -1e30)
                        powers = jnp.exp(scores - jnp.max(scores, axis=0, keepdims=True))
                        probs = powers * (1.0 / jnp.sum(powers, axis=0, keepdims=True))
                        grad_probs = contract_last(
                            jnp.where(own_half, value, jnp.zeros_like(value)), grad
                        )
                        inner = jnp.sum(probs * grad_probs, axis=0, keepdims=True)
                        grad_scores = (probs * (grad_probs - inner)).astype(BF16)
                        results.append((
                            contract_rows(grad_scores, key_rows) * HEAD_DIM ** (-0.5),
                            dot(grad_scores, query) * HEAD_DIM ** (-0.5),
                            dot(probs.astype(BF16), grad),
                        ))
                    for part in range(3):
                        joined = jnp.where(pair_lane < HEAD_DIM, results[0][part], results[1][part])
                        qkv_v[i, :, part * D + offset : part * D + offset + 128] = joined.astype(BF16)
                grad = jnp.zeros((PAD, D), F32)
                for part in range(3):
                    columns = pl.ds(part * D, D)
                    grad += contract_last(qkv_v[i, :, columns], attnw[:, :, columns].reshape(D, D))
                normed, inverse = normalize(tok_v[i].astype(F32))
                v_sum[0:1] += jnp.sum(grad * normed, axis=0, keepdims=True)
                v_sum[1:2] += jnp.sum(grad, axis=0, keepdims=True)
                tok_v[i] = (g_mid[i] + norm_back(grad * gain_one, normed, inverse)).astype(BF16)
                result(i).start()
                for turn, actions in enumerate((
                    (lambda: stage_b(3), lambda: collect(1, 0), lambda: collect(1, 1)),
                    (lambda: stage_c(3), lambda: hop_step(2, 0, 2), lambda: hop_step(2, 1, 2)),
                    (lambda: stage_d(3),),
                    (lambda: stage_e(3), lambda: finish(2, 0), lambda: finish(2, 1),
                     lambda: hop_step(3, 0, 0), lambda: hop_step(3, 1, 0)),
                )):
                    @pl.when(i == turn)
                    def _():
                        for action in actions:
                            action()

                return carry

            lax.fori_loop(0, images, one_image, 0)

            def v_move(n, partner):
                return remote(v_stage.at[n], v_got.at[n], v_sem.at[n, 0], v_sem.at[n, 1], partner)

            fetch_output = pltpu.make_async_copy(middle, g_mid, in_sem.at[6])
            fetch_output.start()
            v_stage[0] = v_sum[...]
            v_move(0, mate).start()
            for p in range(3):
                scatter_part(p, low_tv, lambda i: qkv_v[i, :, p * D : (p + 1) * D])
            tail = {
                0: (lambda: hop_step(3, 0, 2), lambda: hop_step(3, 1, 2)),
                1: (block_output,),
                2: (lambda: finish(3, 0), lambda: finish(3, 1)),
            }
            hop_step(3, 0, 1)
            hop_step(3, 1, 1)
            for n, stage in enumerate((stage_b, stage_c, stage_d)):
                for p in range(3):
                    stage(p)
                v_move(n, (mate, over, beside)[n]).wait()
                total = v_stage[n] + v_got[n]
                if n < 2:
                    v_stage[n + 1] = total
                    v_move(n + 1, (over, beside)[n]).start()
                else:
                    v_lines[z] = total
                    for k in range(1, lines):
                        remote(
                            v_lines.at[z], v_lines.at[z], vd_send.at[k - 1], vd_recv.at[z], along[k - 1]
                        ).start()
                for action in tail[n]:
                    action()
            for p in range(3):
                stage_e(p)
            for k in range(1, lines):
                source = lax.rem(z + lines - k, lines)
                remote(
                    v_lines.at[source], v_lines.at[source], vd_send.at[k - 1], vd_recv.at[source], along[k - 1]
                ).wait()
            total = v_lines[0]
            for n in range(1, lines):
                total = total + v_lines[n]
            for d in range(shards):
                @pl.when(dp == d)
                def _():
                    gradient = total[: vec_old.shape[0], d * width : (d + 1) * width]
                    new = adam_update(
                        vec_old[...], vec_first_old[...], vec_second_old[...], gradient, 0.2, 0.0
                    )
                    vec_new[...], vec_first_new[...], vec_second_new[...] = new

            for p in (3, 0, 1, 2):
                settle(p)
            copy = pltpu.make_async_copy(whole, attn_grad, in_sem.at[0])
            copy.start()
            copy.wait()
            for i in range(images):
                result(i).wait()
            pltpu.make_async_copy(g_low, mixed, in_sem.at[5]).wait()
            for k in range(2):
                to_result(local - 1, k).wait()

        pl.run_scoped(
            through_attention,
            pltpu.VMEM((images, PAD, D), BF16),
            pltpu.VMEM((images, PAD, 3 * D), BF16),
            pltpu.VMEM((images, D, PAD), BF16),
            pltpu.VMEM((images, D, PAD), BF16),
            pltpu.VMEM((4, shards, rows, D), BF16),
            pltpu.VMEM((4, shards, half, D), BF16),
            pltpu.VMEM((4, lines, COLUMNS, quarter, D), BF16),
            pltpu.VMEM((4, lines, quarter, D), BF16),
            pltpu.VMEM((4, lines, quarter, D), F32),
            pltpu.VMEM((count_rows, D), BF16),
        )

    pl.run_scoped(
        backward,
        pltpu.VMEM((images, PAD, D), BF16),
        pltpu.VMEM((images, PAD, D), F32),
        pltpu.VMEM((images, PAD, D), BF16),
        pltpu.VMEM((shards, rows, 4 * D), BF16),
    )

    for e in range(local):
        settle_weights(e)
        if e not in SUM_FIRST:
            for k in range(2):
                cross_sum(e, k).wait_send()


def block(shards, capacity, route, comb, attn, tok, cot, expw, vec_state, group):
    lines = shards // COLUMNS
    images = tok.shape[0]
    local, _, rows, ff = expw.shape
    slots = -(-capacity // 128) * 128
    half, quarter = rows // 2, rows // 4
    wide = images * PAD
    count_rows = images * SENT
    dma = pltpu.SemaphoreType.DMA
    regular = pltpu.SemaphoreType.REGULAR
    vm = pl.BlockSpec(memory_space=pltpu.VMEM)
    hbm = pl.BlockSpec(memory_space=pl.ANY)
    shape = jax.ShapeDtypeStruct
    states = [shape(a.shape, F32) for a in vec_state]
    last = lines - 1
    outs = pl.pallas_call(
        functools.partial(block_kernel, shards, lines, slots),
        out_shape=states + [
            shape((group, images, SENT, D), BF16),
            shape((group, images, SENT, D), BF16),
            shape((local, 2, shards, rows, ff), BF16),
            shape((images, PAD, D), F32),
            shape((images, PAD, 3 * D), BF16),
            shape((images, D, PAD), BF16),
            shape((images, D, PAD), BF16),
            shape((shards,) + attn.shape, BF16),
            shape((count_rows, D), F32),
            shape((count_rows, D), BF16),
            shape((count_rows, D), BF16),
            shape((count_rows, D), BF16),
            shape((4, count_rows, D), BF16),
            shape((3, count_rows, D), BF16),
            shape((rows, 2, local, ff), F32),
            shape((images, PAD, D), BF16),
            shape((images, PAD, D), BF16),
            shape(attn.shape, F32),
        ],
        in_specs=[vm] * 5 + [hbm] * 4,
        out_specs=[vm] * 3 + [hbm] * 18,
        scratch_shapes=[
            pltpu.VMEM(attn.shape, BF16),
            pltpu.VMEM((8, 128), F32),
            pltpu.VMEM((group, 8, wide), jnp.int32),
            pltpu.VMEM((group, 8, wide), F32),
            pltpu.VMEM((shards, 8, 128), F32),
            pltpu.VMEM((group * local, wide), F32),
            pltpu.VMEM((group * local, wide), jnp.int32),
            pltpu.VMEM((group * local, wide), F32),
            pltpu.VMEM((3, 2, shards, rows, ff), BF16),
            pltpu.VMEM((2, 2, lines, rows, ff), BF16),
            pltpu.VMEM((2, 2, rows, ff), BF16),
            pltpu.VMEM((2, rows, ff), BF16),
            pltpu.VMEM((2, 2, last, 2, rows, ff), BF16),
            pltpu.VMEM((2, 2, 2, rows, ff), BF16),
            pltpu.VMEM((2, rows, ff), F32),
            pltpu.VMEM((4, shards, half, D), BF16),
            pltpu.VMEM((4, shards, quarter, D), BF16),
            pltpu.VMEM((4, lines, quarter, D), BF16),
            pltpu.VMEM((4, lines, quarter, D), BF16),
            pltpu.VMEM((rows, 4 * D), F32),
            pltpu.VMEM((8, D), F32),
            pltpu.VMEM((3, 8, D), F32),
            pltpu.VMEM((3, 8, D), F32),
            pltpu.VMEM((lines, 8, D), F32),
            dma((shards,)), dma((shards,)), dma((shards,)), dma((shards,)),
            dma((2,)), dma((3, 2)), dma((group, 2)),
            dma((6,)), dma((images, 3)), dma((images, 3)), dma((5,)),
            dma((2 * local, lines)), dma((2 * local, lines)), dma((2 * local, lines)), dma((2 * local, lines)),
            dma((local, lines)), dma((local, lines)),
            dma((images, 5)), dma((8,)), dma((3,)), dma((shards,)), dma((2,)),
            dma((2, 2)), dma((2, 2)), dma((2, 2)), dma((2, 2)),
            dma((2,)), dma((2, last)), dma((2,)), dma((2, last)),
            regular((2,)), regular((2,)),
            dma((3,)), dma((3,)), dma((3,)), dma((3,)),
            dma((4, 2)), dma((4, 2)), dma((4, 2)), dma((4, last)), dma((4, lines)),
            dma((4, 3)), dma((4, 3)), dma((3, 2)), dma((last,)), dma((lines,)),
        ],
        compiler_params=pltpu.CompilerParams(
            collective_id=0, has_side_effects=True, vmem_limit_bytes=VMEM_LIMIT
        ),
    )(route, comb, *vec_state, tok, cot, expw, attn)
    grads, mixed, grad_tok, attn_grad = outs[17:]
    return mixed, grad_tok, grads, attn_grad, outs[:3]


def by_image(rows):
    images = rows.shape[0] // SEQ
    return jnp.pad(rows.reshape((images, SEQ) + rows.shape[1:]), ((0, 0), (0, PAD - SEQ), (0, 0)))


def as_lanes(table, fill):
    images = table.shape[0] // SEQ
    wide = table.T.reshape(TOP, images, SEQ)
    wide = jnp.pad(wide, ((0, 8 - TOP), (0, 0), (0, PAD - SEQ)), constant_values=fill)
    return wide.reshape(8, images * PAD)


def to_tokens(rows, count):
    return rows[:, :SEQ].reshape(count, D)


def chip_body(shards, group):
    def run(
        tokens, cotangent, routes, combine, attn_master, attn_first, attn_second,
        vector_master, vector_first, vector_second, expert_master, expert_first, expert_second,
    ):
        count = tokens.shape[0]
        experts = expert_master.shape[2] * group
        capacity = max(2, 4 * count // experts)
        shard = jnp.transpose(expert_master.astype(BF16), (2, 1, 0, 3))
        mixed, grad_tokens, grads, attn_grad, vec_new = block(
            shards, capacity, as_lanes(routes, -1), as_lanes(combine, 0.0), attn_master,
            by_image(tokens), by_image(cotangent), shard,
            [vector_master, vector_first, vector_second], group,
        )
        attn_new = adam_update(attn_master, attn_first, attn_second, attn_grad, 0.03, 0.1)
        expert_new = adam_update(expert_master, expert_first, expert_second, grads, 0.02, 0.1)
        return (to_tokens(mixed, count), to_tokens(grad_tokens, count), *attn_new, *vec_new, *expert_new)

    return run


def gelu_slope(preact):
    return (
        0.5 * (1.0 + lax.erf(preact * 0.7071067811865476))
        + preact * jnp.exp(-0.5 * preact * preact) * 0.3989422804014327
    )


def slot_places(routes, experts):
    flat_routes = routes.reshape(-1)
    onehot = (flat_routes[:, None] == jnp.arange(experts, dtype=jnp.int32)[None, :]).astype(
        jnp.int32
    )
    before = jnp.cumsum(onehot, axis=0) - onehot
    return jnp.sum(before * onehot, axis=1)


def general_body(
    tokens,
    cotangent,
    routes,
    combine,
    attn_master,
    attn_first,
    attn_second,
    vector_master,
    vector_first,
    vector_second,
    expert_master,
    expert_first,
    expert_second,
):
    group_size = lax.axis_size("expert")
    local_experts = expert_master.shape[2]
    experts = local_experts * group_size
    token_count = tokens.shape[0]
    capacity = max(2, 4 * token_count // experts)
    images = token_count // SEQ
    score_scale = HEAD_DIM ** (-0.5)
    attn_weight, vector_weight, expert_weight = (
        lax.all_gather(attn_master.astype(jnp.bfloat16), "dp", axis=0, tiled=True),
        lax.all_gather(vector_master.astype(jnp.bfloat16), "dp", axis=1, tiled=True),
        lax.all_gather(expert_master.astype(jnp.bfloat16), "dp", axis=0, tiled=True),
    )
    vectors = vector_weight.astype(jnp.float32)
    w_packed = attn_weight[:, : 3 * D]
    w_project = attn_weight[:, 3 * D :]
    inputs = tokens.astype(jnp.float32)
    normed_one, inverse_one = normalize(inputs)
    lowered_one = (normed_one * vectors[0] + vectors[1]).astype(jnp.bfloat16)
    packed = jnp.dot(lowered_one, w_packed, preferred_element_type=jnp.float32).astype(jnp.bfloat16)
    packed = packed.reshape(images, SEQ, 3, HEADS, HEAD_DIM)
    queries = packed[:, :, 0]
    keys_all = packed[:, :, 1]
    values_all = packed[:, :, 2]
    scores = (
        jnp.einsum("bqhc,bkhc->bhqk", queries, keys_all, preferred_element_type=jnp.float32)
        * score_scale
    )
    softmax_out = jax.nn.softmax(scores, axis=-1)
    softmax_low = softmax_out.astype(jnp.bfloat16)
    attended = jnp.einsum(
        "bhqk,bkhc->bqhc", softmax_low, values_all, preferred_element_type=jnp.float32
    )
    attended = attended.reshape(token_count, D).astype(jnp.bfloat16)
    middle = inputs + jnp.dot(attended, w_project, preferred_element_type=jnp.float32) + vectors[4]
    normed_two, inverse_two = normalize(middle)
    mixed_in = (normed_two * vectors[2] + vectors[3]).astype(jnp.bfloat16)
    slot_index = routes.reshape(-1) * capacity + slot_places(routes, experts)

    def dispatch(slot_rows):
        filled = jnp.zeros((experts * capacity, D), jnp.bfloat16).at[slot_index].set(slot_rows)
        return filled.reshape(group_size, local_experts, capacity, D)

    def collect(returned):
        picked = returned.reshape(experts * capacity, D)[slot_index]
        return picked.reshape(token_count, TOP, D).astype(jnp.float32)

    received = lax.all_to_all(
        dispatch(jnp.repeat(mixed_in, TOP, axis=0)),
        "expert",
        split_axis=0,
        concat_axis=0,
        tiled=True,
    )
    produced = []
    for expert_item in range(local_experts):
        arrived = received[:, expert_item].reshape(group_size * capacity, D)
        preact = jnp.dot(
            arrived, expert_weight[:, 0, expert_item], preferred_element_type=jnp.float32
        )
        hidden = jax.nn.gelu(preact, approximate=False).astype(jnp.bfloat16)
        output_rows = contract_last(hidden, expert_weight[:, 1, expert_item]).astype(jnp.bfloat16)
        produced.append(output_rows.reshape(group_size, capacity, D))
    returned = lax.all_to_all(
        jnp.stack(produced, 1), "expert", split_axis=0, concat_axis=0, tiled=True
    )
    mixed = middle + jnp.sum(combine[:, :, None] * collect(returned), axis=1)
    grad_out = cotangent.astype(jnp.float32)
    slot_grads = (
        (combine[:, :, None] * grad_out[:, None, :])
        .reshape(token_count * TOP, D)
        .astype(jnp.bfloat16)
    )
    grads_in = lax.all_to_all(
        dispatch(slot_grads), "expert", split_axis=0, concat_axis=0, tiled=True
    )
    sent_back = []
    shards = []
    for expert_item in range(local_experts):
        arrived = received[:, expert_item].reshape(group_size * capacity, D)
        arrived_grad = grads_in[:, expert_item].reshape(group_size * capacity, D)
        w_in = expert_weight[:, 0, expert_item]
        w_out = expert_weight[:, 1, expert_item]
        preact = jnp.dot(arrived, w_in, preferred_element_type=jnp.float32)
        hidden = jax.nn.gelu(preact, approximate=False).astype(jnp.bfloat16)
        grad_hidden = jnp.dot(arrived_grad, w_out, preferred_element_type=jnp.float32)
        grad_pre = (grad_hidden * gelu_slope(preact)).astype(jnp.bfloat16)
        sent_back.append(
            contract_last(grad_pre, w_in).astype(jnp.bfloat16).reshape(group_size, capacity, D)
        )
        full_grad = jnp.stack(
            [contract_rows(arrived, grad_pre), contract_rows(arrived_grad, hidden)], 1
        )
        shards.append(lax.psum_scatter(full_grad, "dp", scatter_dimension=0, tiled=True))
    expert_grad = jnp.stack(shards, 2)
    returned_grads = lax.all_to_all(
        jnp.stack(sent_back, 1), "expert", split_axis=0, concat_axis=0, tiled=True
    )
    grad_mixed = jnp.sum(collect(returned_grads), axis=1)
    grad_gain_two = jnp.sum(grad_mixed * normed_two, axis=0)
    grad_shift_two = jnp.sum(grad_mixed, axis=0)
    grad_middle = grad_out + norm_back(grad_mixed * vectors[2], normed_two, inverse_two)
    middle_low = grad_middle.astype(jnp.bfloat16)
    grad_project = contract_rows(attended, middle_low)
    grad_attended = (
        contract_last(middle_low, w_project)
        .astype(jnp.bfloat16)
        .reshape(images, SEQ, HEADS, HEAD_DIM)
    )
    grad_soft = jnp.einsum(
        "bqhc,bkhc->bhqk", grad_attended, values_all, preferred_element_type=jnp.float32
    )
    grad_scores = (
        softmax_out * (grad_soft - jnp.sum(softmax_out * grad_soft, axis=-1, keepdims=True))
    ).astype(jnp.bfloat16)
    grad_queries = (
        jnp.einsum("bhqk,bkhc->bqhc", grad_scores, keys_all, preferred_element_type=jnp.float32)
        * score_scale
    )
    grad_keys = (
        jnp.einsum("bhqk,bqhc->bkhc", grad_scores, queries, preferred_element_type=jnp.float32)
        * score_scale
    )
    grad_values = jnp.einsum(
        "bhqk,bqhc->bkhc", softmax_low, grad_attended, preferred_element_type=jnp.float32
    )
    grad_packed = (
        jnp.stack([grad_queries, grad_keys, grad_values], 2)
        .reshape(token_count, 3 * D)
        .astype(jnp.bfloat16)
    )
    grad_weight_packed = contract_rows(lowered_one, grad_packed)
    grad_lowered = contract_last(grad_packed, w_packed)
    grad_gain_one = jnp.sum(grad_lowered * normed_one, axis=0)
    grad_shift_one = jnp.sum(grad_lowered, axis=0)
    grad_tokens = grad_middle + norm_back(grad_lowered * vectors[0], normed_one, inverse_one)
    attn_grad = jnp.concatenate([grad_weight_packed, grad_project], axis=1)
    vector_grad = jnp.stack(
        [
            grad_gain_one,
            grad_shift_one,
            grad_gain_two,
            grad_shift_two,
            jnp.sum(grad_middle, axis=0),
        ],
        0,
    )
    attn_whole, vector_whole = lax.psum((attn_grad, vector_grad), "expert")
    attn_part, vector_part = (
        lax.psum_scatter(attn_whole, "dp", scatter_dimension=0, tiled=True),
        lax.psum_scatter(vector_whole, "dp", scatter_dimension=1, tiled=True),
    )
    attn_new = adam_update(attn_master, attn_first, attn_second, attn_part, 0.03, 0.1)
    vector_new = adam_update(vector_master, vector_first, vector_second, vector_part, 0.2, 0.0)
    expert_new = adam_update(expert_master, expert_first, expert_second, expert_grad, 0.02, 0.1)
    return (
        mixed.astype(jnp.bfloat16),
        grad_tokens.astype(jnp.bfloat16),
        attn_new[0],
        attn_new[1],
        attn_new[2],
        vector_new[0],
        vector_new[1],
        vector_new[2],
        expert_new[0],
        expert_new[1],
        expert_new[2],
    )


def solution(mesh):
    shards, group = mesh.shape["dp"], mesh.shape["expert"]
    chips = shards == 4 * COLUMNS and group == 2 * CORES
    body = chip_body(shards, group) if chips else general_body
    return jax.shard_map(
        body,
        mesh=mesh,
        in_specs=(
            P(("dp", "expert"), None),
            P(("dp", "expert"), None),
            P(("dp", "expert"), None),
            P(("dp", "expert"), None),
            P("dp", None),
            P("dp", None),
            P("dp", None),
            P(None, "dp"),
            P(None, "dp"),
            P(None, "dp"),
            P("dp", None, "expert", None),
            P("dp", None, "expert", None),
            P("dp", None, "expert", None),
        ),
        out_specs=(
            P(("dp", "expert"), None),
            P(("dp", "expert"), None),
            P("dp", None),
            P("dp", None),
            P("dp", None),
            P(None, "dp"),
            P(None, "dp"),
            P(None, "dp"),
            P("dp", None, "expert", None),
            P("dp", None, "expert", None),
            P("dp", None, "expert", None),
        ),
        check_vma=False,
    )
```
